512 devices in a mesh: dp: 8 (over y), row: 8 (over x, z_lo), col: 8 (over z_hi, core).
Axes of the slice: x: 4, y: 8, z: 8 (z_hi: 4, z_lo: 2; z = z_hi * 2 + z_lo), core: 2. Of those that a mesh axis runs over, the one named last changes fastest.
Arguments:
- timesteps: int32 [8], P('dp'), may hold values from 0 to 999
- features_win: bfloat16 [8, 64, 128, 320], P('dp', 'row', 'col'), may hold values from -25 to 25
- features_lose: bfloat16 [8, 64, 128, 320], P('dp', 'row', 'col'), may hold values from -25 to 25
- noise_win: bfloat16 [8, 64, 128, 320], P('dp', 'row', 'col'), may hold values from -6 to 6
- noise_lose: bfloat16 [8, 64, 128, 320], P('dp', 'row', 'col'), may hold values from -6 to 6
- conv_weight: bfloat16 [9, 320, 320], replicated, may hold values from -0.109375 to 0.109375
- ref_weight: bfloat16 [9, 320, 320], replicated, may hold values from -0.109375 to 0.109375
- norm_gain: float32 [320], replicated, may hold values from 0.5 to 1.5
- norm_shift: float32 [320], replicated, may hold values from -3 to 3
- ref_gain: float32 [320], replicated, may hold values from 0.5 to 1.5
- ref_shift: float32 [320], replicated, may hold values from -3 to 3
- time_weight: float32 [320, 320], replicated, may hold values from -0.3125 to 0.3125
Outputs:
- pair_loss: float32 [8], P('dp')
- grad_weight: float32 [320, 2880], P('dp', ('row', 'col'))
- grad_gain: float32 [320], replicated
- grad_shift: float32 [320], replicated
The draws below stay inside these ranges and needn't reach their ends.
All inputs are finite; a program needn't handle non-finite values.
Results may differ from the reference program's by a relative error of at most 0.00086.
Values may be sent and summed in bfloat16 or wider, within the bound.
No kernel may reach another device: no remote copies, remote signals or barrier semaphores. Data moves between devices by JAX's collectives and lax.ppermute only.
A program may use at most 64 MiB of HBM per device.

```python
import math
import jax
import jax.numpy as jnp
from jax import lax

C = 320
GROUPS = 32
TDIM = 320
PAIRS = 8
NH = 64
NW = 128


def shaped_field(base, key):
    row_pos = jnp.arange(NH, dtype=jnp.float32) / (NH - 1)
    col_pos = jnp.arange(NW, dtype=jnp.float32) / (NW - 1)
    tilt = jnp.exp(0.5 * math.log(3.0) * (row_pos[:, None] + col_pos[None, :]))
    channel_scale = jnp.exp(jax.random.uniform(jax.random.fold_in(key, 5), (C,), minval=-0.7, maxval=0.7))
    rough = jax.random.uniform(jax.random.fold_in(key, 6), (NH, NW, 1), minval=0.5, maxval=1.0)
    return base * (tilt[:, :, None] * rough)[None, :, :, :] * channel_scale[None, None, None, :]


def draw_features_win(key, part):
    key = jax.random.fold_in(key, 11)
    shape = (PAIRS, NH, NW, C)
    base = jnp.clip(jax.random.normal(key, shape), -4.0, 4.0)
    return shaped_field(base, key).astype(jnp.bfloat16)


def draw_features_lose(key, part):
    key = jax.random.fold_in(key, 23)
    shape = (PAIRS, NH, NW, C)
    base = jnp.clip(jax.random.normal(key, shape), -4.0, 4.0)
    return shaped_field(base, key).astype(jnp.bfloat16)


def set_ends(values, stream_key, low, high):
    longest = values.shape.index(max(values.shape))
    spots = []
    for shift in (0, 1):
        where = [jax.random.randint(jax.random.fold_in(stream_key, axis), (), 0, length) for axis, length in enumerate(values.shape)]
        where[longest] = (where[longest] + shift) % values.shape[longest]
        spots.append(tuple(where))
    return values.at[spots[0]].set(low).at[spots[1]].set(high)


def block_levels(rng, dims, split, low, high):
    def one(position, parts):
        draws = jax.random.uniform(jax.random.fold_in(jax.random.fold_in(rng, 6), position), (parts,), jnp.float32, low / len(split), high / len(split))
        return jnp.repeat(jnp.exp(draws), dims[position] // parts).reshape((-1,) + (1,) * (len(dims) - position - 1))

    level = one(*split[0])
    for cut in split[1:]:
        level = level * one(*cut)
    return level


def normal_values(own_key, shape, width, bound, cuts=(), held_as=jnp.bfloat16):
    level = block_levels(own_key, shape, cuts, -0.22, 0.18) if cuts else 1.0
    values = jax.random.normal(own_key, shape, jnp.float32) * width * level
    return jnp.minimum(jnp.maximum(values, -bound), bound).astype(held_as)


def setup_inputs(seed: int = 0) -> dict:
    key_of = jax.random.split(jax.random.key(seed), 13)
    timesteps = set_ends(jax.random.randint(key_of[0], (PAIRS,), 0, 1000), jax.random.fold_in(key_of[0], 1), 0, 999).astype(jnp.int32)
    features_win = draw_features_win(jax.random.fold_in(key_of[12], 71), 0)
    features_lose = draw_features_lose(jax.random.fold_in(key_of[12], 71), 0)
    noise_win = normal_values(key_of[3], (PAIRS, NH, NW, C), 1.0, 6.0, ((0, 8), (1, 8), (2, 8)))
    noise_lose = normal_values(key_of[4], (PAIRS, NH, NW, C), 1.0, 6.0, ((0, 8), (1, 8), (2, 8)))
    conv_weight = normal_values(key_of[5], (9, C, C), (9 * C) ** -0.5, 0.109375)
    ref_weight = normal_values(key_of[6], (9, C, C), (9 * C) ** -0.5, 0.109375)
    norm_gain = jnp.clip(1.0 + 0.1 * jax.random.normal(key_of[7], (C,), jnp.float32), 0.5, 1.5)
    norm_shift = normal_values(key_of[8], (C,), 0.5, 3.0, (), jnp.float32)
    ref_gain = jnp.clip(1.0 + 0.1 * jax.random.normal(key_of[9], (C,), jnp.float32), 0.5, 1.5)
    ref_shift = normal_values(key_of[10], (C,), 0.5, 3.0, (), jnp.float32)
    time_weight = normal_values(key_of[11], (TDIM, C), TDIM ** -0.5, 0.3125, (), jnp.float32)
    return {"timesteps": timesteps, "features_win": features_win, "features_lose": features_lose, "noise_win": noise_win, "noise_lose": noise_lose, "conv_weight": conv_weight, "ref_weight": ref_weight, "norm_gain": norm_gain, "norm_shift": norm_shift, "ref_gain": ref_gain, "ref_shift": ref_shift, "time_weight": time_weight}


beta_scale = 40.0

def time_embed(timesteps, time_weight):
    half_dim = time_weight.shape[0] // 2
    frequency = jnp.exp(-math.log(10000.0) * jnp.arange(half_dim, dtype=jnp.float32) / half_dim)
    angles = timesteps.astype(jnp.float32)[:, None] * frequency[None, :]
    sinusoid = jnp.concatenate([jnp.cos(angles), jnp.sin(angles)], axis=1)
    return jnp.dot(jax.nn.silu(sinusoid), time_weight, precision=lax.Precision.HIGHEST)

def normalize(feature, first, second, entries):
    channels = feature.shape[-1]
    values = feature.astype(jnp.float32).reshape(-1, GROUPS, channels // GROUPS)
    group_mean = first / entries
    group_var = second / entries - group_mean * group_mean
    normed = (values - group_mean[None, :, None]) * lax.rsqrt(group_var + 1e-05)[None, :, None]
    return normed.reshape(feature.shape)

def forward_columns(padded, height, width_cells):
    pieces = [padded[row_off:row_off + height, col_off:col_off + width_cells, :] for row_off in range(3) for col_off in range(3)]
    joined = jnp.concatenate(pieces, axis=-1)
    return joined.reshape(height * width_cells, joined.shape[-1])

def backward_columns(padded, height, width_cells):
    pieces = [padded[2 - row_off:2 - row_off + height, 2 - col_off:2 - col_off + width_cells, :] for row_off in range(3) for col_off in range(3)]
    joined = jnp.concatenate(pieces, axis=-1)
    return joined.reshape(height * width_cells, joined.shape[-1])

def silu_slope(pre):
    gate_sig = jax.nn.sigmoid(pre)
    return gate_sig * (1.0 + pre * (1.0 - gate_sig))

def reference(timesteps, features_win, features_lose, noise_win, noise_lose, conv_weight, ref_weight, norm_gain, norm_shift, ref_gain, ref_shift, time_weight):
    channels = C
    pixels = NH * NW
    time_bias = time_embed(timesteps, time_weight)
    entries = pixels * (channels // GROUPS)
    flat_kernels = (conv_weight.reshape(9 * channels, channels), ref_weight.reshape(9 * channels, channels))
    flipped = jnp.transpose(conv_weight, (0, 2, 1)).reshape(9 * channels, channels)
    gains = (norm_gain, ref_gain)
    shifts = (norm_shift, ref_shift)

    def one_pair(inputs):
        feat_w, feat_l, targ_w, targ_l, bias_row = inputs
        records = []
        for feature, target in ((feat_w, targ_w), (feat_l, targ_l)):
            values = feature.astype(jnp.float32).reshape(pixels, GROUPS, channels // GROUPS)
            normed = normalize(feature, lax.optimization_barrier(jnp.sum(values, axis=(0, 2))), lax.optimization_barrier(jnp.sum(values * values, axis=(0, 2))), entries)
            for model in range(2):
                pre = normed * gains[model] + shifts[model] + bias_row
                activated = jax.nn.silu(pre).astype(jnp.bfloat16)
                padded = jnp.pad(activated, ((1, 1), (1, 1), (0, 0)))
                columns = forward_columns(padded, NH, NW)
                conv_out = jnp.dot(columns, flat_kernels[model], preferred_element_type=jnp.float32)
                resid = feature.astype(jnp.float32).reshape(pixels, channels) + conv_out - target.astype(jnp.float32).reshape(pixels, channels)
                error = jnp.sum(resid * resid) / (pixels * channels)
                records.append((error, columns, resid, pre, normed))
        margin = records[0][0] - records[1][0] - (records[2][0] - records[3][0])
        loss_value = jax.nn.softplus(beta_scale * margin)
        scale = beta_scale * jax.nn.sigmoid(beta_scale * margin) * 2.0 / (PAIRS * channels)
        kernel_terms = []
        gain_terms = []
        shift_terms = []
        for index in (0, 2):
            error, columns, resid, pre, normed = records[index]
            cotangent = resid.astype(jnp.bfloat16)
            kernel_terms.append(jnp.dot(cotangent.T, columns, preferred_element_type=jnp.float32))
            padded_cot = jnp.pad(cotangent.reshape(NH, NW, channels), ((1, 1), (1, 1), (0, 0)))
            back = backward_columns(padded_cot, NH, NW)
            grad_act = jnp.dot(back, flipped, preferred_element_type=jnp.float32)
            grad_pre = grad_act * silu_slope(pre.reshape(pixels, channels))
            gain_terms.append(lax.optimization_barrier(jnp.sum(grad_pre * normed.reshape(pixels, channels), axis=0)))
            shift_terms.append(lax.optimization_barrier(jnp.sum(grad_pre, axis=0)))
        return (loss_value, scale * (kernel_terms[0] - kernel_terms[1]), scale * (gain_terms[0] - gain_terms[1]), scale * (shift_terms[0] - shift_terms[1]))
    losses, kernels, gain_parts, shift_parts = lax.map(one_pair, (features_win, features_lose, noise_win, noise_lose, time_bias))
    return (losses, lax.optimization_barrier(jnp.sum(kernels, axis=0)), lax.optimization_barrier(jnp.sum(gain_parts, axis=0)), lax.optimization_barrier(jnp.sum(shift_parts, axis=0)))
```

```python
import functools
import math

import jax
import jax.numpy as jnp
from jax import lax
from jax.experimental import pallas as pl
from jax.experimental.pallas import tpu as pltpu
from jax.sharding import Mesh
from jax.sharding import PartitionSpec as P

C = 320
GROUPS = 32
TAPS = 9
TH, TW = 8, 16
PIX = TH * TW
BLK = 45
PIXELS = 64 * 128
BETA = 40.0
F32 = jnp.float32
BF16 = jnp.bfloat16
I16 = jnp.int16
HIGHEST = lax.Precision.HIGHEST
VMEM_LIMIT = 50 * 1024 * 1024


def call(kernel, outs, scratch=(), flops=0, nbytes=0, smem=()):
    def run(*args):
        specs = [
            pl.BlockSpec(memory_space=pltpu.SMEM if i in smem else pltpu.VMEM)
            for i in range(len(args))
        ]
        return pl.pallas_call(
            kernel,
            out_shape=[jax.ShapeDtypeStruct(s, d) for s, d in outs],
            in_specs=specs,
            out_specs=[pl.BlockSpec(memory_space=pltpu.VMEM) for _ in outs],
            scratch_shapes=list(scratch),
            compiler_params=pltpu.CompilerParams(vmem_limit_bytes=VMEM_LIMIT),
            cost_estimate=pl.CostEstimate(flops=flops, bytes_accessed=nbytes, transcendentals=0),
        )(*args)

    return run


def pow2(n):
    size = jnp.abs(n)
    out = jnp.ones(n.shape, F32)
    for bit in range(7):
        step = jnp.where(n < 0, 0.5 ** (2**bit) if bit < 7 else 0.0, 2.0 ** (2**bit))
        out = out * jnp.where((size & (1 << bit)) != 0, step, 1.0)
    return out


def exponent(peak):
    level = jnp.log(jnp.maximum(peak, 1e-30)) * (1.0 / math.log(2.0))
    return jnp.clip(jnp.ceil(level + 0.01), -100.0, 100.0).astype(jnp.int32)


def rounded(values, exps):
    return jnp.clip(jnp.round(values * pow2(15 - exps)), -32767.0, 32767.0)


def split_small(small):
    exps = exponent(jnp.abs(small))
    scaled = small * pow2(15 - exps)
    high = jnp.round(scaled)
    low = jnp.round((scaled - high) * 32768.0)
    return jnp.clip(high, -32767.0, 32767.0), low, exps.astype(F32)


def write_extras(extra, small):
    high, low, exps = split_small(small)
    extra[...] = jnp.zeros_like(extra)
    for k in range(3):
        extra[k, 0:1, :] = high[k : k + 1]
        extra[k, 1:2, :] = low[k : k + 1]
    extra[3, 0:1, :] = exps[0:1]
    extra[3, 1:2, :] = exps[1:2]
    extra[4, 0:1, :] = exps[2:3]


def read_extras(blocks, base):
    tails = [blocks[base + k].astype(jnp.int32)[40:48] for k in range(5)]
    exps = [tails[3][6:7], tails[3][7:8], tails[4][6:7]]
    rows = []
    for k in range(3):
        high = tails[k][6:7].astype(F32)
        low = tails[k][7:8].astype(F32)
        rows.append((high + low * (1.0 / 32768.0)) * pow2(exps[k] - 15))
    return jnp.concatenate(rows + [jnp.zeros((5, C), F32)], axis=0)


def packed_block(block, extra):
    row = lax.broadcasted_iota(jnp.int32, block.shape, 0)
    exps = exponent(jnp.max(jnp.abs(block), axis=0, keepdims=True))
    q = rounded(block, exps)
    q = jnp.where(row == 45, exps.astype(F32), q)
    q = jnp.where(row == 46, extra[0:1], q)
    q = jnp.where(row == 47, extra[1:2], q)
    return q.astype(jnp.int32).astype(I16)


def unpacked_block(block):
    q = block.astype(jnp.int32)
    row = lax.broadcasted_iota(jnp.int32, q.shape, 0)
    return jnp.where(row < BLK, q.astype(F32) * pow2(q[45:46] - 15), 0.0)


def edge_rows(fw, fl, first, last):
    first[0] = fw[0]
    first[1] = fl[0]
    last[0] = fw[TH - 1]
    last[1] = fl[TH - 1]


def stats_and_time(step, fw, fl, time_weight, stats, bias):
    total = jnp.zeros((8, 128), F32)
    rows = lax.broadcasted_iota(jnp.int32, (C, 128), 0)
    lanes = lax.broadcasted_iota(jnp.int32, (C, 128), 1)
    size = C // GROUPS
    for k, ref in enumerate((fw, fl)):
        x = ref[...].astype(F32).reshape(PIX, C)
        sums = jnp.sum(x, axis=0, keepdims=True)
        squares = jnp.sum(x * x, axis=0, keepdims=True)
        for j, part in enumerate((sums, squares)):
            group = lanes - GROUPS * (2 * k + j)
            member = (group >= 0) & (group < GROUPS)
            member = member & (rows >= group * size) & (rows < group * size + size)
            total = total + jnp.dot(
                jnp.broadcast_to(part, (8, C)),
                member.astype(F32),
                precision=HIGHEST,
                preferred_element_type=F32,
            )
    stats[...] = jnp.broadcast_to(total[0:1], stats.shape)
    half = C // 2
    lane = lax.broadcasted_iota(jnp.int32, (8, C), 1)
    place = jnp.where(lane < half, lane, lane - half).astype(F32)
    frequency = jnp.exp(-math.log(10000.0) * place / half)
    angles = step[0].astype(F32) * frequency
    sinusoid = jnp.where(lane < half, jnp.cos(angles), jnp.sin(angles))
    gate = sinusoid * jax.nn.sigmoid(sinusoid)
    bias[...] = jnp.dot(gate, time_weight[...], precision=HIGHEST, preferred_element_type=F32)


def edge_columns(top, bottom, fw, fl, first, last):
    for s, ref in enumerate((fw, fl)):
        x = ref[...].astype(F32)
        above = top[s].astype(F32)
        below = bottom[s].astype(F32)
        for out, col in ((first, 0), (last, TW - 1)):
            side = jnp.concatenate(
                [above[col : col + 1]]
                + [x[r, col : col + 1] for r in range(TH)]
                + [below[col : col + 1], jnp.zeros((6, C), F32)],
                axis=0,
            )
            out[s] = side.astype(BF16)


def step_kernel(
    stats, bias, gain, shift, ref_gain, ref_shift, fw, fl, nw, nl, top, bottom, left, right,
    weight, ref_weight, own, send, small, field, act, cols, grad, parts, back, extra,
):
    x_at, zl_at = lax.axis_index("x"), lax.axis_index("zl")
    zh_at, core = lax.axis_index("zh"), lax.axis_index("core")
    row_at, col_at = 2 * x_at + zl_at, 2 * zh_at + core

    total = jnp.broadcast_to(jnp.sum(stats[...], axis=0, keepdims=True), (8, 128))
    groups = lax.broadcasted_iota(jnp.int32, (128, C), 0)
    chans = lax.broadcasted_iota(jnp.int32, (128, C), 1)
    size = C // GROUPS
    entries = float(PIXELS * size)

    def by_channel(k):
        group = groups - GROUPS * k
        member = (group >= 0) & (group < GROUPS)
        member = member & (chans >= group * size) & (chans < group * size + size)
        spread = jnp.dot(total, member.astype(F32), precision=HIGHEST, preferred_element_type=F32)
        return spread[0:1] / entries

    means, scales = [], []
    for s in range(2):
        mean, square = by_channel(2 * s), by_channel(2 * s + 1)
        means.append(mean)
        scales.append(lax.rsqrt(square - mean * mean + 1e-05))

    for s, ref in enumerate((fw, fl)):
        field[s] = jnp.zeros((TH + 2, 24, C), F32)
        field[s, 1 : TH + 1, 1 : TW + 1, :] = ref[...].astype(F32)
        field[s, 0, 1 : TW + 1, :] = top[s].astype(F32)
        field[s, TH + 1, 1 : TW + 1, :] = bottom[s].astype(F32)
        lhs = left[s].astype(F32)
        rhs = right[s].astype(F32)
        for r in range(TH + 2):
            field[s, r, 0:1, :] = lhs[r : r + 1]
            field[s, r, TW + 1 : TW + 2, :] = rhs[r : r + 1]

    column = lax.broadcasted_iota(jnp.int32, (24, C), 0)
    inside = (column < TW + 2) & ((column > 0) | (col_at > 0))
    inside = inside & ((column < TW + 1) | (col_at < 7))

    def valid(r):
        if r == 0:
            return inside & (row_at > 0)
        if r == TH + 1:
            return inside & (row_at < 7)
        return inside

    def pre_act(s, r, g, b):
        normed = (field[s, r] - means[s]) * scales[s]
        return normed, normed * g + b

    def columns_of(g, b):
        for s in range(2):
            for r in range(TH + 2):
                _, pre = pre_act(s, r, g, b)
                act[r] = jnp.where(valid(r), pre * jax.nn.sigmoid(pre), 0.0)
            for t in range(TAPS):
                a, c = t // 3, t % 3
                piece = act[a : a + TH, c : c + TW, :].reshape(PIX, C).astype(BF16)
                cols[s * PIX : (s + 1) * PIX, C * t : C * (t + 1)] = piece

    base = jnp.concatenate(
        [
            fw[...].astype(F32).reshape(PIX, C) - nw[...].astype(F32).reshape(PIX, C),
            fl[...].astype(F32).reshape(PIX, C) - nl[...].astype(F32).reshape(PIX, C),
        ],
        axis=0,
    )
    streams = lax.broadcasted_iota(jnp.int32, (2 * PIX, C), 0)
    sign = jnp.where(streams < PIX, 1.0, -1.0)

    def residual(kernel):
        conv = jnp.dot(cols[...], kernel[...].reshape(TAPS * C, C), preferred_element_type=F32)
        return base + conv

    time_row = bias[0:1]
    columns_of(ref_gain[...], ref_shift[...] + time_row)
    resid = residual(ref_weight)
    margin = -jnp.sum(resid * resid * sign, axis=0, keepdims=True)
    g, b = gain[...], shift[...] + time_row
    columns_of(g, b)
    resid = residual(weight)
    margin = margin + jnp.sum(resid * resid * sign, axis=0, keepdims=True)
    cot = (resid * sign).astype(BF16)

    grad[0 : TAPS * C, :] = lax.dot_general(
        cols[...], cot, (((0,), (0,)), ((), ())), preferred_element_type=F32
    )

    back[...] = jnp.zeros_like(back)
    for t in range(TAPS):
        a, c = t // 3, t % 3
        term = lax.dot_general(
            cot, weight[t], (((1,), (1,)), ((), ())), preferred_element_type=F32
        )
        for s in range(2):
            back[s, a : a + TH, c : c + TW, :] += term[s * PIX : (s + 1) * PIX].reshape(TH, TW, C)
    gains = jnp.zeros((24, C), F32)
    shifts = jnp.zeros((24, C), F32)
    for s in range(2):
        for r in range(TH + 2):
            normed, pre = pre_act(s, r, g, b)
            gate = jax.nn.sigmoid(pre)
            slope = gate * (1.0 + pre * (1.0 - gate))
            dpre = jnp.where(valid(r), back[s, r] * slope, 0.0)
            gains = gains + dpre * normed
            shifts = shifts + dpre
    totals = jnp.concatenate(
        [
            jnp.sum(gains, axis=0, keepdims=True),
            jnp.sum(shifts, axis=0, keepdims=True),
            jnp.broadcast_to(jnp.sum(margin, axis=1, keepdims=True), (1, C)),
            jnp.zeros((5, C), F32),
        ],
        axis=0,
    )
    small[...] = totals
    write_extras(extra, totals)

    row = lax.broadcasted_iota(jnp.int32, (48, C), 0)

    for k in range(64):
        parts[k] = jnp.where(row < BLK, grad[BLK * k : BLK * k + 48, :], 0.0)

    def split(q, carry):
        own[q] = parts[2 * q + core]
        send[q] = packed_block(parts[2 * q + 1 - core], extra[lax.rem(q, 8)])
        return carry

    lax.fori_loop(0, 32, split, 0)


def core_sum(own, small, other, out, extra):
    write_extras(extra, small[...] + read_extras(other, 0))

    def body(q, carry):
        out[q] = packed_block(own[q] + unpacked_block(other[q]), extra[lax.rem(q, 8)])
        return carry

    lax.fori_loop(0, 32, body, 0)


def chip_sum(blocks, out):
    small = read_extras(blocks, 0)
    for source in range(1, 4):
        small = small + read_extras(blocks, 8 * source)
    high, low, exps = split_small(small)
    lane = lax.broadcasted_iota(jnp.int32, (1, 128), 1)
    tail = jnp.zeros((1, 128), F32)
    vectors = []
    for k in range(2):
        e = exponent(jnp.max(jnp.abs(small[k : k + 1]), axis=1, keepdims=True))
        q = rounded(small[k : k + 1], e)
        q = jnp.concatenate([q, jnp.zeros((1, 64), F32)], axis=1)
        vectors += [q[:, 0:128], q[:, 128:256], q[:, 256:384]]
        tail = jnp.where(lane == k, e.astype(F32), tail)
    for k, part in enumerate((high, low, exps)):
        tail = jnp.where(lane == 2 + k, part[2:3, 0:128], tail)

    def body(z, carry):
        block = unpacked_block(blocks[z])
        for source in range(1, 4):
            block = block + unpacked_block(blocks[8 * source + z])
        e = exponent(jnp.max(jnp.abs(block), axis=0, keepdims=True))
        q = rounded(block, e)
        e = e.astype(F32)
        for y in range(8):
            part = q[:, 40 * y : 40 * y + 40]
            tile = jnp.concatenate(
                [part[0:16], part[16:32], part[32:48], jnp.zeros((16, 8), F32)], axis=1
            )
            ey = e[:, 40 * y : 40 * y + 40]
            ey = jnp.concatenate([ey, ey, ey, jnp.zeros((1, 8), F32)], axis=1)
            full = jnp.concatenate([tile] + vectors + [ey, tail], axis=0)
            out[y, z] = full.astype(jnp.int32).astype(I16)
        return carry

    lax.fori_loop(0, 8, body, 0)


def final_sum(blocks, loss, grad, gain, shift):
    y_at = lax.axis_index("y")
    weights = jnp.zeros((16, 128), F32)
    vectors = jnp.zeros((8, 128), F32)
    mine = jnp.zeros((1, 1), F32)
    row = lax.broadcasted_iota(jnp.int32, (8, 128), 0)
    for pair in range(8):
        part = jnp.zeros((16, 128), F32)
        vector = jnp.zeros((8, 128), F32)
        margin = jnp.zeros((1, 1), F32)
        for z in range(8):
            q = blocks[pair, z].astype(jnp.int32)
            v = q.astype(F32)
            tail = q[16:24]
            part = part + v[0:16] * pow2(tail[6:7] - 15)
            factor = pow2(tail[7:8] - 15)
            vector = vector + v[16:24] * jnp.where(row < 3, factor[:, 0:1], factor[:, 1:2])
            margin = margin + (v[23:24, 2:3] + v[23:24, 3:4] * (1.0 / 32768.0)) * factor[:, 4:5]
        margin = BETA * (margin / float(PIXELS * C))
        scale = BETA * jax.nn.sigmoid(margin) * (2.0 / (8 * C))
        weights = weights + scale * part
        vectors = vectors + scale * vector
        mine = jnp.where(y_at == pair, margin, mine)
    near = jnp.exp(-jnp.abs(mine))
    one = 1.0 + near
    log1p = jnp.where(one == 1.0, near, jnp.log(one) * near / jnp.where(one == 1.0, 1.0, one - 1.0))
    loss[...] = jnp.maximum(mine, 0.0) + log1p
    tall = jnp.concatenate([weights, jnp.roll(weights, -40, 1), jnp.roll(weights, -80, 1)], axis=0)
    tall = jnp.concatenate([tall, jnp.zeros((80, 128), F32)], axis=0)
    grad[...] = tall.T[0:40, 0:BLK]
    gain[...] = jnp.concatenate([vectors[0:1], vectors[1:2], vectors[2:3, 0:64]], axis=1)
    shift[...] = jnp.concatenate([vectors[3:4], vectors[4:5], vectors[5:6, 0:64]], axis=1)


def local(
    timesteps, features_win, features_lose, noise_win, noise_lose, conv_weight, ref_weight,
    norm_gain, norm_shift, ref_gain, ref_shift, time_weight,
):
    fw, fl = features_win[0], features_lose[0]
    strip = (2, TW, C)
    rows, columns = ("x", "zl"), ("zh", "core")
    up = [((i + 1) % 8, i) for i in range(8)]
    down = [(i, (i + 1) % 8) for i in range(8)]

    first, last = call(edge_rows, [(strip, BF16), (strip, BF16)])(fw, fl)
    top = lax.ppermute(last, rows, down)
    bottom = lax.ppermute(first, rows, up)
    stats, bias = call(
        stats_and_time, [((64, 128), F32), ((8, C), F32)], flops=10**7, nbytes=10**6, smem=(0,)
    )(timesteps, fw, fl, time_weight)
    first, last = call(edge_columns, [(strip, BF16), (strip, BF16)])(top, bottom, fw, fl)
    stats, first, last = lax.optimization_barrier((stats, first, last))
    left = lax.ppermute(last, columns, down)
    right = lax.ppermute(first, columns, up)
    stats = lax.all_to_all(stats, ("x", "zl", "zh", "core"), 0, 0, tiled=True)

    block = (32, 48, C)
    vectors = [v.reshape(1, C) for v in (norm_gain, norm_shift, ref_gain, ref_shift)]
    own, send, small = call(
        step_kernel,
        [(block, F32), (block, I16), ((8, C), F32)],
        [
            pltpu.VMEM((2, TH + 2, 24, C), F32),
            pltpu.VMEM((TH + 2, 24, C), F32),
            pltpu.VMEM((2 * PIX, TAPS * C), BF16),
            pltpu.VMEM((TAPS * C + 8, C), F32),
            pltpu.VMEM((64, 48, C), F32),
            pltpu.VMEM((2, TH + 2, 24, C), F32),
            pltpu.VMEM((8, 8, C), F32),
        ],
        flops=2 * 10**9,
        nbytes=10**7,
    )(
        stats, bias, *vectors, fw, fl, noise_win[0], noise_lose[0], top, bottom, left, right,
        conv_weight, ref_weight,
    )
    other = lax.ppermute(send, "core", [(0, 1), (1, 0)])
    (sums,) = call(core_sum, [(block, I16)], [pltpu.VMEM((8, 8, C), F32)])(own, small, other)
    sums = lax.all_to_all(sums, "x", 0, 0, tiled=True)
    (sums,) = call(chip_sum, [((8, 8, 24, 128), I16)])(sums)
    sums = lax.all_to_all(sums.reshape(64, 24, 128), ("y", "zl", "zh"), 0, 0, tiled=True)
    loss, grad, gain, shift = call(
        final_sum, [((1, 1), F32), ((40, BLK), F32), ((1, C), F32), ((1, C), F32)]
    )(sums.reshape(8, 8, 24, 128))
    return loss.reshape(1), grad, gain.reshape(C), shift.reshape(C)


def solution(mesh):
    fine = Mesh(mesh.devices.reshape(8, 4, 2, 4, 2), ("y", "x", "zl", "zh", "core"))
    image = P("y", ("x", "zl"), ("zh", "core"), None)
    return jax.shard_map(
        local,
        mesh=fine,
        in_specs=(P("y"), image, image, image, image) + (P(),) * 7,
        out_specs=(P("y"), P("y", ("x", "zl", "zh", "core")), P(), P()),
        check_vma=False,
    )
```

```python
import functools
import math

import jax
import jax.numpy as jnp
from jax import lax
from jax.experimental import pallas as pl
from jax.experimental.pallas import tpu as pltpu
from jax.sharding import Mesh
from jax.sharding import PartitionSpec as P

C = 320
GROUPS = 32
TAPS = 9
TH, TW = 8, 16
PIX = TH * TW
BLK = 45
PIXELS = 64 * 128
BETA = 40.0
F32 = jnp.float32
BF16 = jnp.bfloat16
I16 = jnp.int16
HIGHEST = lax.Precision.HIGHEST
VMEM_LIMIT = 28 * 1024 * 1024


def call(kernel, outs, scratch=(), flops=0, nbytes=0, far=()):
    def run(*args):
        specs = [
            pl.BlockSpec(memory_space=pl.ANY if i in far else pltpu.VMEM) for i in range(len(args))
        ]
        return pl.pallas_call(
            kernel,
            out_shape=[jax.ShapeDtypeStruct(s, d) for s, d in outs],
            in_specs=specs,
            out_specs=[pl.BlockSpec(memory_space=pltpu.VMEM) for _ in outs],
            scratch_shapes=list(scratch),
            compiler_params=pltpu.CompilerParams(vmem_limit_bytes=VMEM_LIMIT),
            cost_estimate=pl.CostEstimate(flops=flops, bytes_accessed=nbytes, transcendentals=0),
        )(*args)

    return run


def pow2(n):
    size = jnp.abs(n)
    out = jnp.ones(n.shape, F32)
    for bit in range(7):
        step = jnp.where(n < 0, 0.5 ** (2**bit) if bit < 7 else 0.0, 2.0 ** (2**bit))
        out = out * jnp.where((size & (1 << bit)) != 0, step, 1.0)
    return out


def exponent(peak):
    level = jnp.log(jnp.maximum(peak, 1e-30)) * (1.0 / math.log(2.0))
    return jnp.clip(jnp.ceil(level + 0.01), -100.0, 100.0).astype(jnp.int32)


def rounded(values, exps):
    return jnp.round(values * pow2(15 - exps))


def split_small(small):
    exps = exponent(jnp.abs(small))
    scaled = small * pow2(15 - exps)
    high = jnp.round(scaled)
    low = jnp.round((scaled - high) * 32768.0)
    return high, low, exps.astype(F32)


def write_extras(extra, small):
    high, low, exps = split_small(small)
    extra[...] = jnp.zeros_like(extra)
    for k in range(3):
        extra[k, 0:1, :] = high[k : k + 1]
        extra[k, 1:2, :] = low[k : k + 1]
    extra[3, 0:1, :] = exps[0:1]
    extra[3, 1:2, :] = exps[1:2]
    extra[4, 0:1, :] = exps[2:3]


def read_extras(blocks, base):
    tails = [blocks[base + k].astype(jnp.int32)[40:48] for k in range(5)]
    exps = [tails[3][6:7], tails[3][7:8], tails[4][6:7]]
    rows = []
    for k in range(3):
        high = tails[k][6:7].astype(F32)
        low = tails[k][7:8].astype(F32)
        rows.append((high + low * (1.0 / 32768.0)) * pow2(exps[k] - 15))
    return jnp.concatenate(rows + [jnp.zeros((5, C), F32)], axis=0)


def packed_block(block, extra):
    exps = exponent(jnp.max(jnp.abs(block), axis=0, keepdims=True))
    q = rounded(block, exps)
    row = lax.broadcasted_iota(jnp.int32, (8, C), 0)
    tail = jnp.where(row == 5, exps.astype(F32), q[40:48])
    tail = jnp.where(row == 6, extra[0:1], tail)
    tail = jnp.where(row == 7, extra[1:2], tail)
    q = jnp.concatenate([q[0:40], tail], axis=0)
    return q.astype(jnp.int32).astype(I16)


def unpacked_block(block):
    q = block.astype(jnp.int32)
    v = q.astype(F32) * pow2(q[45:46] - 15)
    row = lax.broadcasted_iota(jnp.int32, (8, C), 0)
    return jnp.concatenate([v[0:40], jnp.where(row < BLK - 40, v[40:48], 0.0)], axis=0)


def stats_and_time(
    step, fw, fl, time_weight, stats, bias, first, last, here, table, number, sems
):
    copies = [
        pltpu.make_async_copy(fw, here.at[0], sems.at[0]),
        pltpu.make_async_copy(fl, here.at[1], sems.at[1]),
        pltpu.make_async_copy(step, number, sems.at[2]),
        pltpu.make_async_copy(time_weight, table, sems.at[3]),
    ]
    for copy in copies:
        copy.start()
    copies[0].wait()
    copies[1].wait()
    total = jnp.zeros((8, 128), F32)
    rows = lax.broadcasted_iota(jnp.int32, (C, 128), 0)
    lanes = lax.broadcasted_iota(jnp.int32, (C, 128), 1)
    size = C // GROUPS
    for k in range(2):
        first[k] = here[k, 0]
        last[k] = here[k, TH - 1]
        x = here[k].astype(F32).reshape(PIX, C)
        sums = jnp.sum(x, axis=0, keepdims=True)
        squares = jnp.sum(x * x, axis=0, keepdims=True)
        for j, part in enumerate((sums, squares)):
            group = lanes - GROUPS * (2 * k + j)
            member = (group >= 0) & (group < GROUPS)
            member = member & (rows >= group * size) & (rows < group * size + size)
            total = total + jnp.dot(
                jnp.broadcast_to(part, (8, C)),
                member.astype(F32),
                precision=HIGHEST,
                preferred_element_type=F32,
            )
    stats[...] = jnp.broadcast_to(total[0:1], stats.shape)
    half = C // 2
    lane = lax.broadcasted_iota(jnp.int32, (8, C), 1)
    place = jnp.where(lane < half, lane, lane - half).astype(F32)
    frequency = jnp.exp(-math.log(10000.0) * place / half)
    copies[2].wait()
    angles = number[0].astype(F32) * frequency
    sinusoid = jnp.where(lane < half, jnp.cos(angles), jnp.sin(angles))
    gate = sinusoid * jax.nn.sigmoid(sinusoid)
    copies[3].wait()
    bias[...] = jnp.dot(gate, table[...], precision=HIGHEST, preferred_element_type=F32)


def edge_column(top, bottom, fw, fl, side):
    core = lax.axis_index("core")
    for s, ref in enumerate((fw, fl)):
        x = ref[...].astype(F32)
        above = top[s].astype(F32)
        below = bottom[s].astype(F32)
        column = [
            jnp.concatenate(
                [above[col : col + 1]]
                + [x[r, col : col + 1] for r in range(TH)]
                + [below[col : col + 1], jnp.zeros((6, C), F32)],
                axis=0,
            )
            for col in (0, TW - 1)
        ]
        side[s] = jnp.where(core == 0, column[0], column[1]).astype(BF16)


def tile_payload(top, bottom, side, fw, fl, nw, nl, out, sems):
    copies = [
        pltpu.make_async_copy(nw, out.at[0, pl.ds(11, TH)], sems.at[0]),
        pltpu.make_async_copy(nl, out.at[1, pl.ds(11, TH)], sems.at[1]),
    ]
    for copy in copies:
        copy.start()
    for s, ref in enumerate((fw, fl)):
        out[s, 0] = top[s]
        out[s, 1 : TH + 1] = ref[...]
        out[s, TH + 1] = bottom[s]
        out[s, TH + 2] = side[s]
    for copy in copies:
        copy.wait()


def forward(
    stats, bias, gain, shift, ref_gain, ref_shift, mine, theirs, weight_far, ref_far,
    cols, cot_out, small, field, act, back, weight, ref_weight, sems,
):
    copies = [
        pltpu.make_async_copy(ref_far, ref_weight, sems.at[0]),
        pltpu.make_async_copy(weight_far, weight, sems.at[1]),
    ]
    for copy in copies:
        copy.start()
    core = lax.axis_index("core")
    row_at = 2 * lax.axis_index("x") + lax.axis_index("zl")
    chip_at = 2 * lax.axis_index("zh")
    col_at = (chip_at + core, chip_at + 1 - core)

    total = jnp.broadcast_to(jnp.sum(stats[...], axis=0, keepdims=True), (8, 128))
    groups = lax.broadcasted_iota(jnp.int32, (128, C), 0)
    chans = lax.broadcasted_iota(jnp.int32, (128, C), 1)
    size = C // GROUPS
    entries = float(PIXELS * size)

    def by_channel(k):
        group = groups - GROUPS * k
        member = (group >= 0) & (group < GROUPS)
        member = member & (chans >= group * size) & (chans < group * size + size)
        spread = jnp.dot(total, member.astype(F32), precision=HIGHEST, preferred_element_type=F32)
        return spread[0:1] / entries

    means, scales = [], []
    for s in range(2):
        mean, square = by_channel(2 * s), by_channel(2 * s + 1)
        means.append(mean)
        scales.append(lax.rsqrt(square - mean * mean + 1e-05))

    tiles = (mine, theirs)
    for w in range(2):
        for s in range(2):
            here, beside = tiles[w], tiles[1 - w]
            f = 2 * w + s
            field[f, :, TW + 2 :, :] = jnp.zeros((TH + 2, 22 - TW, C), F32)
            field[f, :, 1 : TW + 1, :] = here[s, 0 : TH + 2].astype(F32)
            outer = here[s, TH + 2].astype(F32)
            is_left = core == w
            for r in range(TH + 2):
                near = beside[s, r].astype(F32)
                out = outer[r : r + 1]
                field[f, r, 0:1, :] = jnp.where(is_left, out, near[TW - 1 : TW])
                field[f, r, TW + 1 : TW + 2, :] = jnp.where(is_left, near[0:1], out)

    column = lax.broadcasted_iota(jnp.int32, (24, C), 0)
    inside = []
    for w in range(2):
        ok = (column < TW + 2) & ((column > 0) | (col_at[w] > 0))
        inside.append(ok & ((column < TW + 1) | (col_at[w] < 7)))

    def valid(w, r):
        if r == 0:
            return inside[w] & (row_at > 0)
        if r == TH + 1:
            return inside[w] & (row_at < 7)
        return inside[w]

    def pre_act(f, r, g, b):
        normed = (field[f, r] - means[f % 2]) * scales[f % 2]
        return normed, normed * g + b

    def columns_of(fields, g, b):
        for f in fields:
            for r in range(TH + 2):
                _, pre = pre_act(f, r, g, b)
                act[r] = jnp.where(valid(f // 2, r), pre * jax.nn.sigmoid(pre), 0.0)
            for t in range(TAPS):
                a, c = t // 3, t % 3
                piece = act[a : a + TH, c : c + TW, :].reshape(PIX, C).astype(BF16)
                cols[f * PIX : (f + 1) * PIX, C * t : C * (t + 1)] = piece

    def base(f):
        tile, s = tiles[f // 2], f % 2
        noise = tile[s, TH + 3 : 2 * TH + 3].astype(F32)
        return (tile[s, 1 : TH + 1].astype(F32) - noise).reshape(PIX, C)

    def residual(fields, kernel):
        conv = jnp.dot(
            cols[0 : PIX * len(fields)],
            kernel[...].reshape(TAPS * C, C),
            preferred_element_type=F32,
        )
        return [base(f) + conv[PIX * f : PIX * (f + 1)] for f in fields]

    def signed_squares(resid):
        return jnp.sum(resid[0] * resid[0] - resid[1] * resid[1], axis=0, keepdims=True)

    time_row = bias[0:1]
    columns_of((0, 1), ref_gain[...].reshape(1, C), ref_shift[...].reshape(1, C) + time_row)
    copies[0].wait()
    resid = residual((0, 1), ref_weight)
    margin = -signed_squares(resid)
    g, b = gain[...].reshape(1, C), shift[...].reshape(1, C) + time_row
    columns_of((0, 1, 2, 3), g, b)
    copies[1].wait()
    resid = residual((0, 1, 2, 3), weight)
    margin = margin + signed_squares(resid)
    for f in range(4):
        cot_out[PIX * f : PIX * (f + 1)] = (resid[f] if f % 2 == 0 else -resid[f]).astype(BF16)

    cot = cot_out[0 : 2 * PIX]
    back[...] = jnp.zeros_like(back)
    for t in range(TAPS):
        a, c = t // 3, t % 3
        term = lax.dot_general(
            cot, weight[t], (((1,), (1,)), ((), ())), preferred_element_type=F32
        )
        for s in range(2):
            back[s, a : a + TH, c : c + TW, :] += term[s * PIX : (s + 1) * PIX].reshape(TH, TW, C)
    gains = jnp.zeros((24, C), F32)
    shifts = jnp.zeros((24, C), F32)
    for s in range(2):
        for r in range(TH + 2):
            normed, pre = pre_act(s, r, g, b)
            gate = jax.nn.sigmoid(pre)
            slope = gate * (1.0 + pre * (1.0 - gate))
            dpre = jnp.where(valid(0, r), back[s, r] * slope, 0.0)
            gains = gains + dpre * normed
            shifts = shifts + dpre
    small[...] = jnp.concatenate(
        [
            jnp.sum(gains, axis=0, keepdims=True),
            jnp.sum(shifts, axis=0, keepdims=True),
            jnp.broadcast_to(jnp.sum(margin, axis=1, keepdims=True), (1, C)),
            jnp.zeros((5, C), F32),
        ],
        axis=0,
    )


def kernel_gradient(cols, cot, out, grad):
    grad[0 : TAPS * C, :] = lax.dot_general(
        cols[...], cot[...], (((0,), (0,)), ((), ())), preferred_element_type=F32
    )
    row = lax.broadcasted_iota(jnp.int32, (48, C), 0)
    for core in range(2):

        @pl.when(lax.axis_index("core") == core)
        def _():
            for q in range(32):
                start = BLK * (2 * q + core)
                out[q] = jnp.where(row < BLK, grad[start : start + 48, :], 0.0)


def pack_blocks(blocks, small, other, out, extra):
    write_extras(extra, small[...] + other[...])

    def body(i, carry):
        for k in range(4):
            q = 4 * i + k
            out[q] = packed_block(blocks[q], extra[lax.rem(q, 8)])
        return carry

    lax.fori_loop(0, 8, body, 0)


def chip_sum(blocks, out):
    small = read_extras(blocks, 0)
    for source in range(1, 4):
        small = small + read_extras(blocks, 8 * source)
    high, low, exps = split_small(small)
    lane = lax.broadcasted_iota(jnp.int32, (1, 128), 1)
    tail = jnp.zeros((1, 128), F32)
    vectors = []
    for k in range(2):
        e = exponent(jnp.max(jnp.abs(small[k : k + 1]), axis=1, keepdims=True))
        q = rounded(small[k : k + 1], e)
        q = jnp.concatenate([q, jnp.zeros((1, 64), F32)], axis=1)
        vectors += [q[:, 0:128], q[:, 128:256], q[:, 256:384]]
        tail = jnp.where(lane == k, e.astype(F32), tail)
    for k, part in enumerate((high, low, exps)):
        tail = jnp.where(lane == 2 + k, part[2:3, 0:128], tail)

    def body(z, carry):
        block = unpacked_block(blocks[z])
        for source in range(1, 4):
            block = block + unpacked_block(blocks[8 * source + z])
        e = exponent(jnp.max(jnp.abs(block), axis=0, keepdims=True))
        q = rounded(block, e)
        e = e.astype(F32)
        for y in range(8):
            part = q[:, 40 * y : 40 * y + 40]
            tile = jnp.concatenate(
                [part[0:16], part[16:32], part[32:48], jnp.zeros((16, 8), F32)], axis=1
            )
            ey = e[:, 40 * y : 40 * y + 40]
            ey = jnp.concatenate([ey, ey, ey, jnp.zeros((1, 8), F32)], axis=1)
            full = jnp.concatenate([tile] + vectors + [ey, tail], axis=0)
            out[y, z] = full.astype(jnp.int32).astype(I16)
        return carry

    lax.fori_loop(0, 8, body, 0)


def final_sum(blocks, loss, grad, gain, shift):
    y_at = lax.axis_index("y")
    weights = jnp.zeros((16, 128), F32)
    vectors = jnp.zeros((8, 128), F32)
    mine = jnp.zeros((1, 1), F32)
    row = lax.broadcasted_iota(jnp.int32, (8, 128), 0)
    for pair in range(8):
        part = jnp.zeros((16, 128), F32)
        vector = jnp.zeros((8, 128), F32)
        margin = jnp.zeros((1, 1), F32)
        for z in range(8):
            q = blocks[pair, z].astype(jnp.int32)
            v = q.astype(F32)
            tail = q[16:24]
            part = part + v[0:16] * pow2(tail[6:7] - 15)
            factor = pow2(tail[7:8] - 15)
            vector = vector + v[16:24] * jnp.where(row < 3, factor[:, 0:1], factor[:, 1:2])
            margin = margin + (v[23:24, 2:3] + v[23:24, 3:4] * (1.0 / 32768.0)) * factor[:, 4:5]
        margin = BETA * (margin / float(PIXELS * C))
        scale = BETA * jax.nn.sigmoid(margin) * (2.0 / (8 * C))
        weights = weights + scale * part
        vectors = vectors + scale * vector
        mine = jnp.where(y_at == pair, margin, mine)
    near = jnp.exp(-jnp.abs(mine))
    one = 1.0 + near
    log1p = jnp.where(one == 1.0, near, jnp.log(one) * near / jnp.where(one == 1.0, 1.0, one - 1.0))
    loss[...] = jnp.maximum(mine, 0.0) + log1p
    tall = jnp.concatenate([weights, jnp.roll(weights, -40, 1), jnp.roll(weights, -80, 1)], axis=0)
    tall = jnp.concatenate([tall, jnp.zeros((80, 128), F32)], axis=0)
    grad[...] = tall.T[0:40, 0:BLK]
    for out, k in ((gain, 0), (shift, 3)):
        pieces = [vectors[k : k + 1], vectors[k + 1 : k + 2], vectors[k + 2 : k + 3, 0:64]]
        out[...] = jnp.concatenate(pieces, axis=1).reshape(C)


def local(
    timesteps, features_win, features_lose, noise_win, noise_lose, conv_weight, ref_weight,
    norm_gain, norm_shift, ref_gain, ref_shift, time_weight,
):
    fw, fl = features_win[0], features_lose[0]
    strip = (2, TW, C)
    rows, columns = ("x", "zl"), ("zh", "core")
    up = [((i + 1) % 8, i) for i in range(8)]
    down = [(i, (i + 1) % 8) for i in range(8)]
    outward = [(i, (i + 1) % 8 if i % 2 else (i + 7) % 8) for i in range(8)]
    swap = [(0, 1), (1, 0)]

    stats, bias, first, last = call(
        stats_and_time,
        [((64, 128), F32), ((8, C), F32), (strip, BF16), (strip, BF16)],
        [
            pltpu.VMEM((2, TH, TW, C), BF16),
            pltpu.VMEM((C, C), F32),
            pltpu.SMEM((1,), jnp.int32),
            pltpu.SemaphoreType.DMA((4,)),
        ],
        flops=10**7,
        nbytes=10**6,
        far=(0, 1, 2, 3),
    )(timesteps, fw, fl, time_weight)
    stats = lax.all_to_all(stats, ("x", "zl", "zh", "core"), 0, 0, tiled=True)
    top = lax.ppermute(last, rows, down)
    bottom = lax.ppermute(first, rows, up)
    (side,) = call(edge_column, [(strip, BF16)])(top, bottom, fw, fl)
    side = lax.ppermute(side, columns, outward)
    payload = (2, 2 * TH + 3, TW, C)
    (mine,) = call(
        tile_payload, [(payload, BF16)], [pltpu.SemaphoreType.DMA((2,))], far=(5, 6)
    )(top, bottom, side, fw, fl, noise_win[0], noise_lose[0])
    theirs = lax.ppermute(mine, "core", swap)

    cols, cot, small = call(
        forward,
        [((4 * PIX, TAPS * C), BF16), ((4 * PIX, C), BF16), ((8, C), F32)],
        [
            pltpu.VMEM((4, TH + 2, 24, C), F32),
            pltpu.VMEM((TH + 2, 24, C), F32),
            pltpu.VMEM((2, TH + 2, 24, C), F32),
            pltpu.VMEM((TAPS, C, C), BF16),
            pltpu.VMEM((TAPS, C, C), BF16),
            pltpu.SemaphoreType.DMA((2,)),
        ],
        flops=2 * 10**9,
        nbytes=10**7,
        far=(8, 9),
    )(
        stats, bias, norm_gain, norm_shift, ref_gain, ref_shift, mine, theirs, conv_weight,
        ref_weight,
    )
    other = lax.ppermute(small, "core", swap)
    block = (32, 48, C)
    (blocks,) = call(
        kernel_gradient,
        [(block, F32)],
        [pltpu.VMEM((TAPS * C + 8, C), F32)],
        flops=10**9,
        nbytes=10**7,
    )(cols, cot)
    (blocks,) = call(pack_blocks, [(block, I16)], [pltpu.VMEM((8, 8, C), F32)])(
        blocks, small, other
    )
    blocks = lax.all_to_all(blocks, "x", 0, 0, tiled=True)
    (sums,) = call(chip_sum, [((8, 8, 24, 128), I16)])(blocks)
    sums = lax.all_to_all(sums.reshape(64, 24, 128), ("y", "zl", "zh"), 0, 0, tiled=True)
    loss, grad, gain, shift = call(
        final_sum, [((1, 1), F32), ((40, BLK), F32), ((C,), F32), ((C,), F32)]
    )(sums.reshape(8, 8, 24, 128))
    return loss.reshape(1), grad, gain, shift


def solution(mesh):
    fine = Mesh(mesh.devices.reshape(8, 4, 2, 4, 2), ("y", "x", "zl", "zh", "core"))
    image = P("y", ("x", "zl"), ("zh", "core"), None)
    return jax.shard_map(
        local,
        mesh=fine,
        in_specs=(P("y"), image, image, image, image) + (P(),) * 7,
        out_specs=(P("y"), P("y", ("x", "zl", "zh", "core")), P(), P()),
        check_vma=False,
    )
```

```python
import functools
import math

import jax
import jax.numpy as jnp
from jax import lax
from jax.experimental import pallas as pl
from jax.experimental.pallas import tpu as pltpu
from jax.sharding import Mesh
from jax.sharding import PartitionSpec as P

C = 320
GROUPS = 32
TAPS = 9
TH, TW = 8, 16
PIX = TH * TW
WIDE = 2 * C
BLK = 45
PIXELS = 64 * 128
BETA = 40.0
F32 = jnp.float32
BF16 = jnp.bfloat16
I16 = jnp.int16
HIGHEST = lax.Precision.HIGHEST


def call(kernel, outs, scratch=(), flops=0, nbytes=0, far=(), grant=28):
    def run(*args):
        specs = [
            pl.BlockSpec(memory_space=pltpu.HBM if i in far else pltpu.VMEM) for i in range(len(args))
        ]
        return pl.pallas_call(
            kernel,
            out_shape=[jax.ShapeDtypeStruct(s, d) for s, d in outs],
            in_specs=specs,
            out_specs=[pl.BlockSpec(memory_space=pltpu.VMEM) for _ in outs],
            scratch_shapes=list(scratch),
            compiler_params=pltpu.CompilerParams(vmem_limit_bytes=grant * 2**20),
            cost_estimate=pl.CostEstimate(flops=flops, bytes_accessed=nbytes, transcendentals=0),
        )(*args)

    return run


def pow2(n):
    size = jnp.abs(n)
    out = jnp.ones(n.shape, F32)
    for bit in range(7):
        step = jnp.where(n < 0, 0.5 ** (2**bit) if bit < 7 else 0.0, 2.0 ** (2**bit))
        out = out * jnp.where((size & (1 << bit)) != 0, step, 1.0)
    return out


def exponent(peak):
    level = jnp.log(jnp.maximum(peak, 1e-30)) * (1.0 / math.log(2.0))
    return jnp.clip(jnp.ceil(level + 0.01), -100.0, 100.0).astype(jnp.int32)


def rounded(values, exps):
    return jnp.round(values * pow2(15 - exps))


def split_small(small):
    exps = exponent(jnp.abs(small))
    scaled = small * pow2(15 - exps)
    high = jnp.round(scaled)
    low = jnp.round((scaled - high) * 32768.0)
    return high, low, exps.astype(F32)


def side_by_side(one, two):
    return jnp.concatenate([one[:, 0:256], two[:, 0:256], one[:, 256:C], two[:, 256:C]], axis=1)


def apart(both):
    one = jnp.concatenate([both[:, 0:256], both[:, 512:576]], axis=1)
    two = jnp.concatenate([both[:, 256:512], both[:, 576:640]], axis=1)
    return one, two


def write_extras(extra, small):
    high, low, exps = split_small(small)
    extra[...] = jnp.zeros_like(extra)
    extra[0, 0:1] = high[0:1]
    extra[0, 1:2] = low[0:1]
    extra[1, 0:1] = exps[0:1]
    extra[1, 1:2] = high[1:2]
    extra[2, 0:1] = low[1:2]
    extra[2, 1:2] = exps[1:2]


def read_extras(tails):
    rows = [tails[0][6:7], tails[0][7:8], tails[1][6:7], tails[1][7:8], tails[2][6:7], tails[2][7:8]]
    out = []
    for high, low, exps in (rows[0:3], rows[3:6]):
        value = high.astype(F32) + low.astype(F32) * (1.0 / 32768.0)
        out.append(value * pow2(exps - 15))
    return jnp.concatenate(out + [jnp.zeros((6, WIDE), F32)], axis=0)


def packed_pair(pair, extra):
    exps = exponent(jnp.max(jnp.abs(pair), axis=0, keepdims=True))
    q = rounded(pair, exps)
    row = lax.broadcasted_iota(jnp.int32, (8, WIDE), 0)
    tail = jnp.where(row == 5, exps.astype(F32), q[40:48])
    tail = jnp.where(row == 6, extra[0:1], tail)
    tail = jnp.where(row == 7, extra[1:2], tail)
    q = jnp.concatenate([q[0:40], tail], axis=0)
    return q.astype(jnp.int32).astype(I16)


def unpacked_pair(q):
    v = q.astype(F32) * pow2(q[45:46] - 15)
    row = lax.broadcasted_iota(jnp.int32, (8, WIDE), 0)
    return jnp.concatenate([v[0:40], jnp.where(row < BLK - 40, v[40:48], 0.0)], axis=0)


def tiles_of(pair):
    return [4 * pair, 4 * pair + 1, 4 * pair + 2, 4 * pair + 3, 16 + pair]


def stats_and_time(
    step, fw, fl, nw, nl, time_weight, stats, bias, first, last, here, table, number, sems
):
    copies = [
        pltpu.make_async_copy(fw, here.at[0, pl.ds(0, TH)], sems.at[0]),
        pltpu.make_async_copy(fl, here.at[1, pl.ds(0, TH)], sems.at[1]),
        pltpu.make_async_copy(step, number, sems.at[2]),
        pltpu.make_async_copy(time_weight, table, sems.at[3]),
        pltpu.make_async_copy(nw, here.at[0, pl.ds(TH, TH)], sems.at[4]),
        pltpu.make_async_copy(nl, here.at[1, pl.ds(TH, TH)], sems.at[5]),
    ]
    for copy in copies:
        copy.start()
    copies[0].wait()
    copies[1].wait()
    total = jnp.zeros((8, 128), F32)
    rows = lax.broadcasted_iota(jnp.int32, (C, 128), 0)
    lanes = lax.broadcasted_iota(jnp.int32, (C, 128), 1)
    size = C // GROUPS
    for k in range(2):
        first[k] = here[k, 0]
        last[k] = here[k, TH - 1]
        x = here[k, 0:TH].astype(F32).reshape(PIX, C)
        sums = jnp.sum(x, axis=0, keepdims=True)
        squares = jnp.sum(x * x, axis=0, keepdims=True)
        for j, part in enumerate((sums, squares)):
            group = lanes - GROUPS * (2 * k + j)
            member = (group >= 0) & (group < GROUPS)
            member = member & (rows >= group * size) & (rows < group * size + size)
            total = total + jnp.dot(
                jnp.broadcast_to(part, (8, C)),
                member.astype(F32),
                precision=HIGHEST,
                preferred_element_type=F32,
            )
    stats[...] = jnp.broadcast_to(total[0:1], stats.shape)
    half = C // 2
    lane = lax.broadcasted_iota(jnp.int32, (8, C), 1)
    place = jnp.where(lane < half, lane, lane - half).astype(F32)
    frequency = jnp.exp(-math.log(10000.0) * place / half)
    copies[2].wait()
    angles = number[0].astype(F32) * frequency
    sinusoid = jnp.where(lane < half, jnp.cos(angles), jnp.sin(angles))
    gate = sinusoid * jax.nn.sigmoid(sinusoid)
    copies[3].wait()
    bias[...] = jnp.dot(gate, table[...], precision=HIGHEST, preferred_element_type=F32)
    copies[4].wait()
    copies[5].wait()


def outer_column_and_tile(top, bottom, here, side, tile):
    core = lax.axis_index("core")
    for s in range(2):
        tile[s, 0] = top[s]
        tile[s, 1 : TH + 1] = here[s, 0:TH]
        tile[s, TH + 1] = bottom[s]
        tile[s, TH + 2 :] = here[s, TH:]
        x = [tile[s, r].astype(F32) for r in range(TH + 2)]
        column = [
            jnp.concatenate([v[col : col + 1] for v in x] + [jnp.zeros((6, C), F32)], axis=0)
            for col in (0, TW - 1)
        ]
        side[s] = jnp.where(core == 0, column[0], column[1]).astype(BF16)


def forward(
    stats, bias, mine, theirs, my_side, their_side, gain_far, shift_far, ref_gain_far, ref_shift_far,
    weight_far, ref_far, cols, cot_out, small, field, act, back, weight, ref_weight, gain, shift,
    ref_gain, ref_shift, sems,
):
    pairs = [
        (ref_gain_far, ref_gain), (ref_shift_far, ref_shift), (gain_far, gain), (shift_far, shift),
        (ref_far, ref_weight), (weight_far, weight),
    ]
    copies = [pltpu.make_async_copy(a, b, sems.at[i]) for i, (a, b) in enumerate(pairs)]
    for copy in copies:
        copy.start()
    core = lax.axis_index("core")
    row_at = 2 * lax.axis_index("x") + lax.axis_index("zl")
    chip_at = 2 * lax.axis_index("zh")
    col_at = (chip_at + core, chip_at + 1 - core)

    total = jnp.broadcast_to(jnp.sum(stats[...], axis=0, keepdims=True), (8, 128))
    groups = lax.broadcasted_iota(jnp.int32, (128, C), 0)
    chans = lax.broadcasted_iota(jnp.int32, (128, C), 1)
    size = C // GROUPS
    entries = float(PIXELS * size)

    def by_channel(k):
        group = groups - GROUPS * k
        member = (group >= 0) & (group < GROUPS)
        member = member & (chans >= group * size) & (chans < group * size + size)
        spread = jnp.dot(total, member.astype(F32), precision=HIGHEST, preferred_element_type=F32)
        return spread[0:1] / entries

    means, scales = [], []
    for s in range(2):
        mean, square = by_channel(2 * s), by_channel(2 * s + 1)
        means.append(mean)
        scales.append(lax.rsqrt(square - mean * mean + 1e-05))

    tiles = (mine, theirs)
    sides = (my_side, their_side)
    for w in range(2):
        for s in range(2):
            here, beside = tiles[w], tiles[1 - w]
            f = 2 * w + s
            field[f, :, TW + 2 :, :] = jnp.zeros((TH + 2, 22 - TW, C), F32)
            field[f, :, 1 : TW + 1, :] = here[s, 0 : TH + 2].astype(F32)
            outer = sides[w][s].astype(F32)
            is_left = core == w
            for r in range(TH + 2):
                near = beside[s, r].astype(F32)
                out = outer[r : r + 1]
                field[f, r, 0:1, :] = jnp.where(is_left, out, near[TW - 1 : TW])
                field[f, r, TW + 1 : TW + 2, :] = jnp.where(is_left, near[0:1], out)

    column = lax.broadcasted_iota(jnp.int32, (24, C), 0)
    inside = []
    for w in range(2):
        ok = (column < TW + 2) & ((column > 0) | (col_at[w] > 0))
        inside.append(ok & ((column < TW + 1) | (col_at[w] < 7)))

    def valid(w, r):
        if r == 0:
            return inside[w] & (row_at > 0)
        if r == TH + 1:
            return inside[w] & (row_at < 7)
        return inside[w]

    def pre_act(f, r, g, b):
        normed = (field[f, r] - means[f % 2]) * scales[f % 2]
        return normed, normed * g + b

    def columns_of(fields, g, b):
        for f in fields:
            for r in range(TH + 2):
                _, pre = pre_act(f, r, g, b)
                act[r] = jnp.where(valid(f // 2, r), pre * jax.nn.sigmoid(pre), 0.0)
            for t in range(TAPS):
                a, c = t // 3, t % 3
                piece = act[a : a + TH, c : c + TW, :].reshape(PIX, C).astype(BF16)
                cols[f * PIX : (f + 1) * PIX, C * t : C * (t + 1)] = piece

    def base(f):
        tile, s = tiles[f // 2], f % 2
        noise = tile[s, TH + 2 : 2 * TH + 2].astype(F32)
        return (tile[s, 1 : TH + 1].astype(F32) - noise).reshape(PIX, C)

    def residual(fields, kernel):
        conv = jnp.dot(
            cols[0 : PIX * len(fields)],
            kernel[...].reshape(TAPS * C, C),
            preferred_element_type=F32,
        )
        return [base(f) + conv[PIX * f : PIX * (f + 1)] for f in fields]

    def signed_squares(resid):
        return jnp.sum(resid[0] * resid[0] - resid[1] * resid[1], axis=0, keepdims=True)

    time_row = bias[0:1]
    for copy in copies[0:4]:
        copy.wait()
    columns_of((0, 1), ref_gain[...].reshape(1, C), ref_shift[...].reshape(1, C) + time_row)
    copies[4].wait()
    resid = residual((0, 1), ref_weight)
    margin = -signed_squares(resid)
    g, b = gain[...].reshape(1, C), shift[...].reshape(1, C) + time_row
    columns_of((0, 1, 2, 3), g, b)
    copies[5].wait()
    resid = residual((0, 1, 2, 3), weight)
    margin = margin + signed_squares(resid)
    for f in range(4):
        cot_out[PIX * f : PIX * (f + 1)] = (resid[f] if f % 2 == 0 else -resid[f]).astype(BF16)

    cot = cot_out[0 : 2 * PIX]
    back[...] = jnp.zeros_like(back)
    for t in range(TAPS):
        a, c = t // 3, t % 3
        term = lax.dot_general(
            cot, weight[t], (((1,), (1,)), ((), ())), preferred_element_type=F32
        )
        for s in range(2):
            back[s, a : a + TH, c : c + TW, :] += term[s * PIX : (s + 1) * PIX].reshape(TH, TW, C)
    gains = jnp.zeros((24, C), F32)
    shifts = jnp.zeros((24, C), F32)
    for s in range(2):
        for r in range(TH + 2):
            normed, pre = pre_act(s, r, g, b)
            gate = jax.nn.sigmoid(pre)
            slope = gate * (1.0 + pre * (1.0 - gate))
            dpre = jnp.where(valid(0, r), back[s, r] * slope, 0.0)
            gains = gains + dpre * normed
            shifts = shifts + dpre
    gains = jnp.sum(gains, axis=0, keepdims=True)
    shifts = jnp.sum(shifts, axis=0, keepdims=True)
    margin = jnp.broadcast_to(jnp.sum(margin, axis=1, keepdims=True), (1, WIDE))
    small[...] = jnp.concatenate(
        [side_by_side(gains, shifts), margin, jnp.zeros((6, WIDE), F32)], axis=0
    )


def kernel_gradient(cols, cot, out, grad):
    grad[0 : TAPS * C, :] = lax.dot_general(
        cols[...], cot[...], (((0,), (0,)), ((), ())), preferred_element_type=F32
    )
    row = lax.broadcasted_iota(jnp.int32, (48, C), 0)
    for core in range(2):

        @pl.when(lax.axis_index("core") == core)
        def _():
            for q in range(32):
                start = BLK * (2 * q + core)
                out[q] = jnp.where(row < BLK, grad[start : start + 48, :], 0.0)


def pack_blocks(blocks, small, other, out, extra):
    write_extras(extra, small[...] + other[...])

    def body(dest, carry):
        for pair in range(4):
            q = 8 * dest + 2 * pair
            packed = packed_pair(side_by_side(blocks[q], blocks[q + 1]), extra[pair])
            for k, tile in enumerate(tiles_of(pair)):
                out[dest, tile] = packed[:, 128 * k : 128 * k + 128]
        return carry

    lax.fori_loop(0, 4, body, 0)


def chip_sum(blocks, out):
    def pair_of(source, pair, rows):
        parts = [blocks[source, tile].astype(jnp.int32)[rows] for tile in tiles_of(pair)]
        return jnp.concatenate(parts, axis=1)

    tail_rows = slice(40, 48)
    small = jnp.zeros((8, WIDE), F32)
    for source in range(4):
        small = small + read_extras([pair_of(source, k, tail_rows) for k in range(3)])
    high, low, exps = split_small(small[:, 0:128])
    lane = lax.broadcasted_iota(jnp.int32, (1, 128), 1)
    tail = jnp.zeros((1, 128), F32)
    vectors = []
    for k, vector in enumerate(apart(small[0:1])):
        e = exponent(jnp.max(jnp.abs(vector), axis=1, keepdims=True))
        q = rounded(vector, e)
        q = jnp.concatenate([q, jnp.zeros((1, 64), F32)], axis=1)
        vectors += [q[:, 0:128], q[:, 128:256], q[:, 256:384]]
        tail = jnp.where(lane == k, e.astype(F32), tail)
    for k, part in enumerate((high, low, exps)):
        tail = jnp.where(lane == 2 + k, part[1:2], tail)

    def body(pair, carry):
        both = jnp.zeros((48, WIDE), F32)
        for source in range(4):
            both = both + unpacked_pair(pair_of(source, pair, slice(0, 48)))
        e = exponent(jnp.max(jnp.abs(both), axis=0, keepdims=True))
        values = apart(rounded(both, e))
        levels = apart(e.astype(F32))
        for k in range(2):
            for y in range(8):
                part = values[k][:, 40 * y : 40 * y + 40]
                tile = jnp.concatenate(
                    [part[0:16], part[16:32], part[32:48], jnp.zeros((16, 8), F32)], axis=1
                )
                ey = levels[k][:, 40 * y : 40 * y + 40]
                ey = jnp.concatenate([ey, ey, ey, jnp.zeros((1, 8), F32)], axis=1)
                full = jnp.concatenate([tile] + vectors + [ey, tail], axis=0)
                out[y, 2 * pair + k] = full.astype(jnp.int32).astype(I16)
        return carry

    lax.fori_loop(0, 4, body, 0)


def final_sum(blocks, loss, grad, gain, shift):
    y_at = lax.axis_index("y")
    weights = jnp.zeros((16, 128), F32)
    vectors = jnp.zeros((8, 128), F32)
    mine = jnp.zeros((1, 1), F32)
    row = lax.broadcasted_iota(jnp.int32, (8, 128), 0)
    for pair in range(8):
        part = jnp.zeros((16, 128), F32)
        vector = jnp.zeros((8, 128), F32)
        margin = jnp.zeros((1, 1), F32)
        for z in range(8):
            q = blocks[pair, z].astype(jnp.int32)
            v = q.astype(F32)
            tail = q[16:24]
            part = part + v[0:16] * pow2(tail[6:7] - 15)
            factor = pow2(tail[7:8] - 15)
            vector = vector + v[16:24] * jnp.where(row < 3, factor[:, 0:1], factor[:, 1:2])
            margin = margin + (v[23:24, 2:3] + v[23:24, 3:4] * (1.0 / 32768.0)) * factor[:, 4:5]
        margin = BETA * (margin / float(PIXELS * C))
        scale = BETA * jax.nn.sigmoid(margin) * (2.0 / (8 * C))
        weights = weights + scale * part
        vectors = vectors + scale * vector
        mine = jnp.where(y_at == pair, margin, mine)
    near = jnp.exp(-jnp.abs(mine))
    one = 1.0 + near
    log1p = jnp.where(one == 1.0, near, jnp.log(one) * near / jnp.where(one == 1.0, 1.0, one - 1.0))
    loss[...] = jnp.maximum(mine, 0.0) + log1p
    tall = jnp.concatenate([weights, jnp.roll(weights, -40, 1), jnp.roll(weights, -80, 1)], axis=0)
    tall = jnp.concatenate([tall, jnp.zeros((80, 128), F32)], axis=0)
    grad[...] = tall.T[0:40, 0:BLK]
    for out, k in ((gain, 0), (shift, 3)):
        pieces = [vectors[k : k + 1], vectors[k + 1 : k + 2], vectors[k + 2 : k + 3, 0:64]]
        out[...] = jnp.concatenate(pieces, axis=1).reshape(C)


def local(
    timesteps, features_win, features_lose, noise_win, noise_lose, conv_weight, ref_weight,
    norm_gain, norm_shift, ref_gain, ref_shift, time_weight,
):
    fw, fl = features_win[0], features_lose[0]
    strip = (2, TW, C)
    rows, columns = ("x", "zl"), ("zh", "core")
    up = [((i + 1) % 8, i) for i in range(8)]
    down = [(i, (i + 1) % 8) for i in range(8)]
    outward = [(i, (i + 1) % 8 if i % 2 else (i + 7) % 8) for i in range(8)]
    beyond = [(i, (i + 2) % 8 if i % 2 else (i + 6) % 8) for i in range(8)]
    swap = [(0, 1), (1, 0)]

    stats, bias, first, last, here = call(
        stats_and_time,
        [((64, 128), F32), ((8, C), F32), (strip, BF16), (strip, BF16)]
        + [((2, 2 * TH, TW, C), BF16)],
        [
            pltpu.VMEM((C, C), F32),
            pltpu.SMEM((1,), jnp.int32),
            pltpu.SemaphoreType.DMA((6,)),
        ],
        flops=10**7,
        nbytes=10**6,
        far=range(6),
        grant=57,
    )(timesteps, fw, fl, noise_win[0], noise_lose[0], time_weight)
    top = lax.ppermute(last, rows, down)
    bottom = lax.ppermute(first, rows, up)
    side, mine = call(
        outer_column_and_tile,
        [(strip, BF16), ((2, 2 * TH + 2, TW, C), BF16)],
        flops=10**10,
        nbytes=10**6,
    )(top, bottom, here)
    stats, side, mine = lax.optimization_barrier((stats, side, mine))
    stats = lax.all_to_all(stats, ("x", "zl", "zh", "core"), 0, 0, tiled=True)
    my_side = lax.ppermute(side, columns, outward)
    their_side = lax.ppermute(side, columns, beyond)
    theirs = lax.ppermute(mine, "core", swap)

    cols, cot, small = call(
        forward,
        [((4 * PIX, TAPS * C), BF16), ((4 * PIX, C), BF16), ((8, WIDE), F32)],
        [
            pltpu.VMEM((4, TH + 2, 24, C), F32),
            pltpu.VMEM((TH + 2, 24, C), F32),
            pltpu.VMEM((2, TH + 2, 24, C), F32),
            pltpu.VMEM((TAPS, C, C), BF16),
            pltpu.VMEM((TAPS, C, C), BF16),
        ]
        + [pltpu.VMEM((C,), F32)] * 4
        + [pltpu.SemaphoreType.DMA((6,))],
        flops=2 * 10**9,
        nbytes=10**7,
        far=range(6, 12),
    )(
        stats, bias, mine, theirs, my_side, their_side, norm_gain, norm_shift, ref_gain, ref_shift,
        conv_weight, ref_weight,
    )
    other = lax.ppermute(small, "core", swap)
    block = (32, 48, C)
    (blocks,) = call(
        kernel_gradient,
        [(block, F32)],
        [pltpu.VMEM((TAPS * C + 8, C), F32)],
        flops=10**9,
        nbytes=10**7,
    )(cols, cot)
    (blocks,) = call(
        pack_blocks, [((4, 20, 48, 128), I16)], [pltpu.VMEM((4, 8, WIDE), F32)]
    )(blocks, small, other)
    blocks = lax.all_to_all(blocks, "x", 0, 0, tiled=True)
    (sums,) = call(chip_sum, [((8, 8, 24, 128), I16)])(blocks)
    sums = lax.all_to_all(sums.reshape(64, 24, 128), ("y", "zl", "zh"), 0, 0, tiled=True)
    loss, grad, gain, shift = call(
        final_sum, [((1, 1), F32), ((40, BLK), F32), ((C,), F32), ((C,), F32)]
    )(sums.reshape(8, 8, 24, 128))
    return loss.reshape(1), grad, gain, shift


def solution(mesh):
    fine = Mesh(mesh.devices.reshape(8, 4, 2, 4, 2), ("y", "x", "zl", "zh", "core"))
    image = P("y", ("x", "zl"), ("zh", "core"), None)
    return jax.shard_map(
        local,
        mesh=fine,
        in_specs=(P("y"), image, image, image, image) + (P(),) * 7,
        out_specs=(P("y"), P("y", ("x", "zl", "zh", "core")), P(), P()),
        check_vma=False,
    )
```

```python
import functools
import math

import jax
import jax.numpy as jnp
from jax import lax
from jax.experimental import pallas as pl
from jax.experimental.pallas import tpu as pltpu
from jax.sharding import Mesh
from jax.sharding import PartitionSpec as P

C = 320
GROUPS = 32
TAPS = 9
TH, TW = 8, 16
PIX = TH * TW
WIDE = 2 * C
BLK = 45
PIXELS = 64 * 128
BETA = 40.0
F32 = jnp.float32
BF16 = jnp.bfloat16
I16 = jnp.int16
HIGHEST = lax.Precision.HIGHEST


def call(kernel, outs, scratch=(), flops=0, nbytes=0, far=(), far_outs=(), grant=28):
    def run(*args):
        specs = [
            pl.BlockSpec(memory_space=pltpu.HBM if i in far else pltpu.VMEM) for i in range(len(args))
        ]
        return pl.pallas_call(
            kernel,
            out_shape=[jax.ShapeDtypeStruct(s, d) for s, d in outs],
            in_specs=specs,
            out_specs=[
                pl.BlockSpec(memory_space=pltpu.HBM if i in far_outs else pltpu.VMEM)
                for i in range(len(outs))
            ],
            scratch_shapes=list(scratch),
            compiler_params=pltpu.CompilerParams(vmem_limit_bytes=grant * 2**20),
            cost_estimate=pl.CostEstimate(flops=flops, bytes_accessed=nbytes, transcendentals=0),
        )(*args)

    return run


def pow2(n):
    size = jnp.abs(n)
    out = jnp.ones(n.shape, F32)
    for bit in range(7):
        step = jnp.where(n < 0, 0.5 ** (2**bit) if bit < 7 else 0.0, 2.0 ** (2**bit))
        out = out * jnp.where((size & (1 << bit)) != 0, step, 1.0)
    return out


def exponent(peak):
    level = jnp.log(jnp.maximum(peak, 1e-30)) * (1.0 / math.log(2.0))
    return jnp.clip(jnp.ceil(level + 0.01), -100.0, 100.0).astype(jnp.int32)


def rounded(values, exps):
    return jnp.round(values * pow2(15 - exps))


def split_small(small):
    exps = exponent(jnp.abs(small))
    scaled = small * pow2(15 - exps)
    high = jnp.round(scaled)
    low = jnp.round((scaled - high) * 32768.0)
    return high, low, exps.astype(F32)


def side_by_side(one, two):
    return jnp.concatenate([one[:, 0:256], two[:, 0:256], one[:, 256:C], two[:, 256:C]], axis=1)


def apart(both):
    one = jnp.concatenate([both[:, 0:256], both[:, 512:576]], axis=1)
    two = jnp.concatenate([both[:, 256:512], both[:, 576:640]], axis=1)
    return one, two


def packed_pair(pair):
    exps = exponent(jnp.max(jnp.abs(pair), axis=0, keepdims=True))
    q = rounded(pair, exps)
    row = lax.broadcasted_iota(jnp.int32, (8, WIDE), 0)
    tail = jnp.where(row == 5, exps.astype(F32), q[40:48])
    q = jnp.concatenate([q[0:40], tail], axis=0)
    return q.astype(jnp.int32).astype(I16)


def unpacked_pair(q):
    v = q.astype(F32) * pow2(q[45:46] - 15)
    row = lax.broadcasted_iota(jnp.int32, (8, WIDE), 0)
    return jnp.concatenate([v[0:40], jnp.where(row < BLK - 40, v[40:48], 0.0)], axis=0)


def tiles_of(pair):
    return [4 * pair, 4 * pair + 1, 4 * pair + 2, 4 * pair + 3, 16 + pair]


def edge_rows(fw, fl, first, last, sems):
    copies = []
    for k, ref in enumerate((fw, fl)):
        copies.append(pltpu.make_async_copy(ref.at[0], first.at[k], sems.at[2 * k]))
        copies.append(pltpu.make_async_copy(ref.at[TH - 1], last.at[k], sems.at[2 * k + 1]))
    for copy in copies:
        copy.start()
    for copy in copies:
        copy.wait()


def stats_and_time(
    step, fw, fl, nw, nl, time_weight, stats, bias, here, table, number, sems
):
    copies = [
        pltpu.make_async_copy(fw, here.at[0, pl.ds(0, TH)], sems.at[0]),
        pltpu.make_async_copy(fl, here.at[1, pl.ds(0, TH)], sems.at[1]),
        pltpu.make_async_copy(step, number, sems.at[2]),
        pltpu.make_async_copy(time_weight, table, sems.at[3]),
        pltpu.make_async_copy(nw, here.at[0, pl.ds(TH, TH)], sems.at[4]),
        pltpu.make_async_copy(nl, here.at[1, pl.ds(TH, TH)], sems.at[5]),
    ]
    for copy in copies:
        copy.start()
    copies[0].wait()
    copies[1].wait()
    total = jnp.zeros((8, 128), F32)
    rows = lax.broadcasted_iota(jnp.int32, (C, 128), 0)
    lanes = lax.broadcasted_iota(jnp.int32, (C, 128), 1)
    size = C // GROUPS
    for k in range(2):
        x = here[k, 0:TH].astype(F32).reshape(PIX, C)
        sums = jnp.sum(x, axis=0, keepdims=True)
        squares = jnp.sum(x * x, axis=0, keepdims=True)
        for j, part in enumerate((sums, squares)):
            group = lanes - GROUPS * (2 * k + j)
            member = (group >= 0) & (group < GROUPS)
            member = member & (rows >= group * size) & (rows < group * size + size)
            total = total + jnp.dot(
                jnp.broadcast_to(part, (8, C)),
                member.astype(F32),
                precision=HIGHEST,
                preferred_element_type=F32,
            )
    stats[...] = jnp.broadcast_to(total[0:1], stats.shape)
    half = C // 2
    lane = lax.broadcasted_iota(jnp.int32, (8, C), 1)
    place = jnp.where(lane < half, lane, lane - half).astype(F32)
    frequency = jnp.exp(-math.log(10000.0) * place / half)
    copies[2].wait()
    angles = number[0].astype(F32) * frequency
    sinusoid = jnp.where(lane < half, jnp.cos(angles), jnp.sin(angles))
    gate = sinusoid * jax.nn.sigmoid(sinusoid)
    copies[3].wait()
    bias[...] = jnp.dot(gate, table[...], precision=HIGHEST, preferred_element_type=F32)
    copies[4].wait()
    copies[5].wait()


def outer_column_and_tile(top, bottom, here, side, tile):
    core = lax.axis_index("core")
    for s in range(2):
        tile[s, 0] = top[s]
        tile[s, 1 : TH + 1] = here[s, 0:TH]
        tile[s, TH + 1] = bottom[s]
        tile[s, TH + 2 :] = here[s, TH:]
        x = [tile[s, r].astype(F32) for r in range(TH + 2)]
        column = [
            jnp.concatenate([v[col : col + 1] for v in x] + [jnp.zeros((6, C), F32)], axis=0)
            for col in (0, TW - 1)
        ]
        side[s] = jnp.where(core == 0, column[0], column[1]).astype(BF16)


def valid_pixels(core):
    row_at = 2 * lax.axis_index("x") + lax.axis_index("zl")
    col_at = 2 * lax.axis_index("zh") + core
    column = lax.broadcasted_iota(jnp.int32, (24, C), 0)
    inside = (column < TW + 2) & ((column > 0) | (col_at > 0))
    inside = inside & ((column < TW + 1) | (col_at < 7))

    def valid(r):
        if r == 0:
            return inside & (row_at > 0)
        if r == TH + 1:
            return inside & (row_at < 7)
        return inside

    return valid


def activate(normed, f, valid, g, b, act):
    for r in range(TH + 2):
        pre = normed[f, r] * g + b
        act[r] = jnp.where(valid(r), pre * jax.nn.sigmoid(pre), 0.0)


def spread_columns(act, cols, f):
    for t in range(TAPS):
        a, c = t // 3, t % 3
        piece = act[a : a + TH, c : c + TW, :].reshape(PIX, C).astype(BF16)
        cols[f * PIX : (f + 1) * PIX, C * t : C * (t + 1)] = piece


def target(tile, s):
    noise = tile[s, TH + 2 : 2 * TH + 2].astype(F32)
    return (tile[s, 1 : TH + 1].astype(F32) - noise).reshape(PIX, C)


def signed_squares(resid):
    return jnp.sum(resid[0] * resid[0] - resid[1] * resid[1], axis=0, keepdims=True)


def kernel_gradient(
    stats, bias, mine, theirs, my_side, their_side, gain_far, shift_far, weight_far,
    out_far, normed_far, cot_out, margin_out, out, normed, others, act, cols, cot, grad, parts, weight,
    gain, shift, sems,
):
    pairs = [(gain_far, gain), (shift_far, shift), (weight_far, weight)]
    copies = [pltpu.make_async_copy(a, b, sems.at[i]) for i, (a, b) in enumerate(pairs)]
    for copy in copies:
        copy.start()
    core = lax.axis_index("core")

    total = jnp.broadcast_to(jnp.sum(stats[...], axis=0, keepdims=True), (8, 128))
    groups = lax.broadcasted_iota(jnp.int32, (128, C), 0)
    chans = lax.broadcasted_iota(jnp.int32, (128, C), 1)
    size = C // GROUPS
    entries = float(PIXELS * size)

    def by_channel(k):
        group = groups - GROUPS * k
        member = (group >= 0) & (group < GROUPS)
        member = member & (chans >= group * size) & (chans < group * size + size)
        spread = jnp.dot(total, member.astype(F32), precision=HIGHEST, preferred_element_type=F32)
        return spread[0:1] / entries

    means, scales = [], []
    for s in range(2):
        mean, square = by_channel(2 * s), by_channel(2 * s + 1)
        means.append(mean)
        scales.append(lax.rsqrt(square - mean * mean + 1e-05))

    tiles = (mine, theirs)
    sides = (my_side, their_side)
    fields = (normed, others)
    for w in range(2):
        field = fields[w]
        for s in range(2):
            here, beside = tiles[w], tiles[1 - w]
            field[s, :, TW + 2 :, :] = jnp.zeros((TH + 2, 22 - TW, C), F32)
            field[s, :, 1 : TW + 1, :] = (here[s, 0 : TH + 2].astype(F32) - means[s]) * scales[s]
            outer = (sides[w][s].astype(F32) - means[s]) * scales[s]
            is_left = core == w
            for r in range(TH + 2):
                near = (beside[s, r].astype(F32) - means[s]) * scales[s]
                out_px = outer[r : r + 1]
                field[s, r, 0:1, :] = jnp.where(is_left, out_px, near[TW - 1 : TW])
                field[s, r, TW + 1 : TW + 2, :] = jnp.where(is_left, near[0:1], out_px)

    keep = pltpu.make_async_copy(normed, normed_far, sems.at[3])
    keep.start()
    copies[0].wait()
    copies[1].wait()
    g, b = gain[...].reshape(1, C), shift[...].reshape(1, C) + bias[0:1]
    for w in range(2):
        valid = valid_pixels(core if w == 0 else 1 - core)
        for s in range(2):
            activate(fields[w], s, valid, g, b, act)
            spread_columns(act, cols, 2 * w + s)
    copies[2].wait()
    conv = jnp.dot(
        cols[...], weight[...].reshape(TAPS * C, C), preferred_element_type=F32
    )
    resid = [target(tiles[f // 2], f % 2) + conv[PIX * f : PIX * (f + 1)] for f in range(4)]
    margin_out[...] = jnp.broadcast_to(signed_squares(resid[0:2]), (8, C))
    for f in range(4):
        cot[PIX * f : PIX * (f + 1)] = (resid[f] if f % 2 == 0 else -resid[f]).astype(BF16)
    cot_out[...] = cot[0 : 2 * PIX]

    grad[0 : TAPS * C, :] = lax.dot_general(
        cols[...], cot[...], (((0,), (0,)), ((), ())), preferred_element_type=F32
    )
    row = lax.broadcasted_iota(jnp.int32, (48, C), 0)
    for parity in range(2):

        @pl.when(core == parity)
        def _():
            for q in range(32):
                start = BLK * (2 * q + parity)
                parts[q] = jnp.where(row < BLK, grad[start : start + 48, :], 0.0)

    def body(dest, carry):
        for pair in range(4):
            q = 8 * dest + 2 * pair
            packed = packed_pair(side_by_side(parts[q], parts[q + 1]))
            for k, tile in enumerate(tiles_of(pair)):
                out[dest, tile] = packed[:, 128 * k : 128 * k + 128]
        pltpu.make_async_copy(out.at[dest], out_far.at[dest], sems.at[4 + dest]).start()
        return carry

    lax.fori_loop(0, 4, body, 0)
    for dest in range(4):
        pltpu.make_async_copy(out.at[dest], out_far.at[dest], sems.at[4 + dest]).wait()
    keep.wait()


def small_sums(*refs):
    far, small, near = refs[0:11], refs[11], refs[12:23]
    act, cols, back, sems = refs[23:27]
    normed, cot, margin_in, bias, mine, gain, shift, ref_gain, ref_shift, weight, ref_weight = near
    copies = [pltpu.make_async_copy(far[i], near[i], sems.at[i]) for i in range(11)]
    for copy in copies:
        copy.start()
    for i in (0, 3, 4, 7, 8):
        copies[i].wait()
    valid = valid_pixels(lax.axis_index("core"))
    time_row = bias[0:1]
    g, b = ref_gain[...].reshape(1, C), ref_shift[...].reshape(1, C) + time_row
    for s in range(2):
        activate(normed, s, valid, g, b, act)
        spread_columns(act, cols, s)
    copies[10].wait()
    conv = jnp.dot(
        cols[...], ref_weight[...].reshape(TAPS * C, C), preferred_element_type=F32
    )
    resid = [target(mine, s) + conv[PIX * s : PIX * (s + 1)] for s in range(2)]
    copies[2].wait()
    margin = margin_in[0:1] - signed_squares(resid)

    back[...] = jnp.zeros_like(back)
    for i in (1, 5, 6, 9):
        copies[i].wait()
    for t in range(TAPS):
        a, c = t // 3, t % 3
        term = lax.dot_general(
            cot[...], weight[t], (((1,), (1,)), ((), ())), preferred_element_type=F32
        )
        for s in range(2):
            back[s, a : a + TH, c : c + TW, :] += term[s * PIX : (s + 1) * PIX].reshape(TH, TW, C)
    g, b = gain[...].reshape(1, C), shift[...].reshape(1, C) + time_row
    gains = jnp.zeros((24, C), F32)
    shifts = jnp.zeros((24, C), F32)
    for s in range(2):
        for r in range(TH + 2):
            pre = normed[s, r] * g + b
            gate = jax.nn.sigmoid(pre)
            slope = gate * (1.0 + pre * (1.0 - gate))
            dpre = jnp.where(valid(r), back[s, r] * slope, 0.0)
            gains = gains + dpre * normed[s, r]
            shifts = shifts + dpre
    gains = jnp.sum(gains, axis=0, keepdims=True)
    shifts = jnp.sum(shifts, axis=0, keepdims=True)
    margin = jnp.broadcast_to(jnp.sum(margin, axis=1, keepdims=True), (1, WIDE))
    small[...] = jnp.concatenate(
        [side_by_side(gains, shifts), margin, jnp.zeros((6, WIDE), F32)], axis=0
    )


def core_sum(one, two, out):
    out[...] = one[...] + two[...]


def chip_sum(blocks, small0, small1, small2, small3, out):
    def pair_of(source, pair, rows):
        parts = [blocks[source, tile].astype(jnp.int32)[rows] for tile in tiles_of(pair)]
        return jnp.concatenate(parts, axis=1)

    small = (small0[...] + small1[...]) + (small2[...] + small3[...])
    high, low, exps = split_small(small[:, 0:128])
    lane = lax.broadcasted_iota(jnp.int32, (1, 128), 1)
    tail = jnp.zeros((1, 128), F32)
    vectors = []
    for k, vector in enumerate(apart(small[0:1])):
        e = exponent(jnp.max(jnp.abs(vector), axis=1, keepdims=True))
        q = rounded(vector, e)
        q = jnp.concatenate([q, jnp.zeros((1, 64), F32)], axis=1)
        vectors += [q[:, 0:128], q[:, 128:256], q[:, 256:384]]
        tail = jnp.where(lane == k, e.astype(F32), tail)
    for k, part in enumerate((high, low, exps)):
        tail = jnp.where(lane == 2 + k, part[1:2], tail)

    def body(pair, carry):
        both = jnp.zeros((48, WIDE), F32)
        for source in range(4):
            both = both + unpacked_pair(pair_of(source, pair, slice(0, 48)))
        e = exponent(jnp.max(jnp.abs(both), axis=0, keepdims=True))
        values = apart(rounded(both, e))
        levels = apart(e.astype(F32))
        for k in range(2):
            for y in range(8):
                part = values[k][:, 40 * y : 40 * y + 40]
                tile = jnp.concatenate(
                    [part[0:16], part[16:32], part[32:48], jnp.zeros((16, 8), F32)], axis=1
                )
                ey = levels[k][:, 40 * y : 40 * y + 40]
                ey = jnp.concatenate([ey, ey, ey, jnp.zeros((1, 8), F32)], axis=1)
                full = jnp.concatenate([tile] + vectors + [ey, tail], axis=0)
                out[y, 2 * pair + k] = full.astype(jnp.int32).astype(I16)
        return carry

    lax.fori_loop(0, 4, body, 0)


def final_sum(blocks, loss, grad, gain, shift):
    y_at = lax.axis_index("y")
    weights = jnp.zeros((16, 128), F32)
    vectors = jnp.zeros((8, 128), F32)
    mine = jnp.zeros((1, 1), F32)
    row = lax.broadcasted_iota(jnp.int32, (8, 128), 0)
    for pair in range(8):
        part = jnp.zeros((16, 128), F32)
        vector = jnp.zeros((8, 128), F32)
        margin = jnp.zeros((1, 1), F32)
        for z in range(8):
            q = blocks[pair, z].astype(jnp.int32)
            v = q.astype(F32)
            tail = q[16:24]
            part = part + v[0:16] * pow2(tail[6:7] - 15)
            factor = pow2(tail[7:8] - 15)
            vector = vector + v[16:24] * jnp.where(row < 3, factor[:, 0:1], factor[:, 1:2])
            margin = margin + (v[23:24, 2:3] + v[23:24, 3:4] * (1.0 / 32768.0)) * factor[:, 4:5]
        margin = BETA * (margin / float(PIXELS * C))
        scale = BETA * jax.nn.sigmoid(margin) * (2.0 / (8 * C))
        weights = weights + scale * part
        vectors = vectors + scale * vector
        mine = jnp.where(y_at == pair, margin, mine)
    near = jnp.exp(-jnp.abs(mine))
    one = 1.0 + near
    log1p = jnp.where(one == 1.0, near, jnp.log(one) * near / jnp.where(one == 1.0, 1.0, one - 1.0))
    loss[...] = jnp.maximum(mine, 0.0) + log1p
    tall = jnp.concatenate([weights, jnp.roll(weights, -40, 1), jnp.roll(weights, -80, 1)], axis=0)
    tall = jnp.concatenate([tall, jnp.zeros((80, 128), F32)], axis=0)
    grad[...] = tall.T[0:40, 0:BLK]
    for out, k in ((gain, 0), (shift, 3)):
        pieces = [vectors[k : k + 1], vectors[k + 1 : k + 2], vectors[k + 2 : k + 3, 0:64]]
        out[...] = jnp.concatenate(pieces, axis=1).reshape(C)


def local(
    timesteps, features_win, features_lose, noise_win, noise_lose, conv_weight, ref_weight,
    norm_gain, norm_shift, ref_gain, ref_shift, time_weight,
):
    fw, fl = features_win[0], features_lose[0]
    strip = (2, TW, C)
    rows, columns = ("x", "zl"), ("zh", "core")
    up = [((i + 1) % 8, i) for i in range(8)]
    down = [(i, (i + 1) % 8) for i in range(8)]
    outward = [(i, (i + 1) % 8 if i % 2 else (i + 7) % 8) for i in range(8)]
    beyond = [(i, (i + 2) % 8 if i % 2 else (i + 6) % 8) for i in range(8)]
    swap = [(0, 1), (1, 0)]

    first, last = call(
        edge_rows,
        [(strip, BF16), (strip, BF16)],
        [pltpu.SemaphoreType.DMA((4,))],
        far=(0, 1),
        grant=57,
    )(fw, fl)
    top = lax.ppermute(last, rows, down)
    bottom = lax.ppermute(first, rows, up)
    stats, bias, here = call(
        stats_and_time,
        [((64, 128), F32), ((8, C), F32), ((2, 2 * TH, TW, C), BF16)],
        [
            pltpu.VMEM((C, C), F32),
            pltpu.SMEM((1,), jnp.int32),
            pltpu.SemaphoreType.DMA((6,)),
        ],
        flops=10**9,
        nbytes=10**6,
        far=range(6),
        grant=57,
    )(timesteps, fw, fl, noise_win[0], noise_lose[0], time_weight)
    side, mine = call(
        outer_column_and_tile,
        [(strip, BF16), ((2, 2 * TH + 2, TW, C), BF16)],
        flops=10**9,
        nbytes=10**6,
        grant=57,
    )(top, bottom, here)
    stats, side, mine = lax.optimization_barrier((stats, side, mine))
    stats = lax.all_to_all(stats, ("x", "zl", "zh", "core"), 0, 0, tiled=True)
    my_side = lax.ppermute(side, columns, outward)
    their_side = lax.ppermute(side, columns, beyond)
    theirs = lax.ppermute(mine, "core", swap)

    field = (2, TH + 2, 24, C)
    blocks, normed, cot, margin = call(
        kernel_gradient,
        [((4, 20, 48, 128), I16), (field, F32), ((2 * PIX, C), BF16), ((8, C), F32)],
        [
            pltpu.VMEM((4, 20, 48, 128), I16),
            pltpu.VMEM(field, F32),
            pltpu.VMEM(field, F32),
            pltpu.VMEM((TH + 2, 24, C), F32),
            pltpu.VMEM((4 * PIX, TAPS * C), BF16),
            pltpu.VMEM((4 * PIX, C), BF16),
            pltpu.VMEM((TAPS * C + 8, C), F32),
            pltpu.VMEM((32, 48, C), F32),
            pltpu.VMEM((TAPS, C, C), BF16),
            pltpu.VMEM((C,), F32),
            pltpu.VMEM((C,), F32),
            pltpu.SemaphoreType.DMA((8,)),
        ],
        flops=2 * 10**9,
        nbytes=10**7,
        far=(6, 7, 8),
        far_outs=(0, 1),
        grant=55,
    )(stats, bias, mine, theirs, my_side, their_side, norm_gain, norm_shift, conv_weight)
    blocks = lax.all_to_all(blocks, "x", 0, 0, tiled=True)
    near = (
        normed, cot, margin, bias, mine, norm_gain, norm_shift, ref_gain, ref_shift, conv_weight,
        ref_weight,
    )
    (small,) = call(
        small_sums,
        [((8, WIDE), F32)],
        [pltpu.VMEM(v.shape, v.dtype) for v in near]
        + [
            pltpu.VMEM((TH + 2, 24, C), F32),
            pltpu.VMEM((2 * PIX, TAPS * C), BF16),
            pltpu.VMEM(field, F32),
            pltpu.SemaphoreType.DMA((11,)),
        ],
        flops=10**9,
        nbytes=10**7,
        far=range(11),
        grant=57,
    )(*near)
    (small,) = call(core_sum, [((8, WIDE), F32)])(small, lax.ppermute(small, "core", swap))
    smalls = [small] + [
        lax.ppermute(small, "x", [(i, (i + k) % 4) for i in range(4)]) for k in (1, 2, 3)
    ]
    (sums,) = call(chip_sum, [((8, 8, 24, 128), I16)])(blocks, *smalls)
    sums = lax.all_to_all(sums.reshape(64, 24, 128), ("y", "zl", "zh"), 0, 0, tiled=True)
    loss, grad, gain, shift = call(
        final_sum, [((1, 1), F32), ((40, BLK), F32), ((C,), F32), ((C,), F32)]
    )(sums.reshape(8, 8, 24, 128))
    return loss.reshape(1), grad, gain, shift


def solution(mesh):
    fine = Mesh(mesh.devices.reshape(8, 4, 2, 4, 2), ("y", "x", "zl", "zh", "core"))
    image = P("y", ("x", "zl"), ("zh", "core"), None)
    return jax.shard_map(
        local,
        mesh=fine,
        in_specs=(P("y"), image, image, image, image) + (P(),) * 7,
        out_specs=(P("y"), P("y", ("x", "zl", "zh", "core")), P(), P()),
        check_vma=False,
    )
```

```python
import functools
import math

import jax
import jax.numpy as jnp
from jax import lax
from jax.experimental import pallas as pl
from jax.experimental.pallas import tpu as pltpu
from jax.sharding import Mesh
from jax.sharding import PartitionSpec as P

C = 320
GROUPS = 32
TAPS = 9
TH, TW = 8, 16
PIX = TH * TW
WIDE = 2 * C
BLK = 45
PIXELS = 64 * 128
BETA = 40.0
F32 = jnp.float32
BF16 = jnp.bfloat16
I16 = jnp.int16
HIGHEST = lax.Precision.HIGHEST


def call(kernel, outs, scratch=(), flops=0, nbytes=0, far=(), grant=28):
    def run(*args):
        specs = [
            pl.BlockSpec(memory_space=pltpu.HBM if i in far else pltpu.VMEM) for i in range(len(args))
        ]
        return pl.pallas_call(
            kernel,
            out_shape=[jax.ShapeDtypeStruct(s, d) for s, d in outs],
            in_specs=specs,
            out_specs=[pl.BlockSpec(memory_space=pltpu.VMEM) for _ in outs],
            scratch_shapes=list(scratch),
            compiler_params=pltpu.CompilerParams(vmem_limit_bytes=grant * 2**20),
            cost_estimate=pl.CostEstimate(flops=flops, bytes_accessed=nbytes, transcendentals=0),
        )(*args)

    return run


def pow2(n):
    size = jnp.abs(n)
    out = jnp.ones(n.shape, F32)
    for bit in range(7):
        step = jnp.where(n < 0, 0.5 ** (2**bit) if bit < 7 else 0.0, 2.0 ** (2**bit))
        out = out * jnp.where((size & (1 << bit)) != 0, step, 1.0)
    return out


def exponent(peak):
    level = jnp.log(jnp.maximum(peak, 1e-30)) * (1.0 / math.log(2.0))
    return jnp.clip(jnp.ceil(level + 0.01), -100.0, 100.0).astype(jnp.int32)


def rounded(values, exps):
    return jnp.round(values * pow2(15 - exps))


def split_small(small):
    exps = exponent(jnp.abs(small))
    scaled = small * pow2(15 - exps)
    high = jnp.round(scaled)
    low = jnp.round((scaled - high) * 32768.0)
    return high, low, exps.astype(F32)


def side_by_side(one, two):
    return jnp.concatenate([one[:, 0:256], two[:, 0:256], one[:, 256:C], two[:, 256:C]], axis=1)


def apart(both):
    one = jnp.concatenate([both[:, 0:256], both[:, 512:576]], axis=1)
    two = jnp.concatenate([both[:, 256:512], both[:, 576:640]], axis=1)
    return one, two


def write_extras(extra, small):
    high, low, exps = split_small(small)
    lane = lax.broadcasted_iota(jnp.int32, (1, WIDE), 1)
    extra[...] = jnp.zeros_like(extra)
    extra[0, 0:1] = high[0:1]
    extra[0, 1:2] = low[0:1]
    extra[1, 0:1] = exps[0:1]
    margin = jnp.where(lane == 1, low[1:2], exps[1:2])
    extra[1, 1:2] = jnp.where(lane == 0, high[1:2], margin)


def read_extras(tails):
    high, low, exps = tails[0][6:7], tails[0][7:8], tails[1][6:7]
    sums = (high.astype(F32) + low.astype(F32) * (1.0 / 32768.0)) * pow2(exps - 15)
    row = tails[1][7:8]
    value = row.astype(F32)
    margin = (value[:, 0:1] + value[:, 1:2] * (1.0 / 32768.0)) * pow2(row[:, 2:3] - 15)
    margin = jnp.broadcast_to(margin, (1, WIDE))
    return jnp.concatenate([sums, margin, jnp.zeros((6, WIDE), F32)], axis=0)


def packed_pair(pair, extra):
    exps = exponent(jnp.max(jnp.abs(pair), axis=0, keepdims=True))
    q = rounded(pair, exps)
    row = lax.broadcasted_iota(jnp.int32, (8, WIDE), 0)
    tail = jnp.where(row == 5, exps.astype(F32), q[40:48])
    tail = jnp.where(row == 6, extra[0:1], tail)
    tail = jnp.where(row == 7, extra[1:2], tail)
    q = jnp.concatenate([q[0:40], tail], axis=0)
    return q.astype(jnp.int32).astype(I16)


def unpacked_pair(q):
    v = q.astype(F32) * pow2(q[45:46] - 15)
    row = lax.broadcasted_iota(jnp.int32, (8, WIDE), 0)
    return jnp.concatenate([v[0:40], jnp.where(row < BLK - 40, v[40:48], 0.0)], axis=0)


def tiles_of(pair):
    return [4 * pair, 4 * pair + 1, 4 * pair + 2, 4 * pair + 3, 8 + pair]


def statistics(fw, fl, nw, nl, stats, first, last, here, sems):
    copies = [
        pltpu.make_async_copy(fw, here.at[0, pl.ds(0, TH)], sems.at[0]),
        pltpu.make_async_copy(fl, here.at[1, pl.ds(0, TH)], sems.at[1]),
        pltpu.make_async_copy(nw, here.at[0, pl.ds(TH, TH)], sems.at[2]),
        pltpu.make_async_copy(nl, here.at[1, pl.ds(TH, TH)], sems.at[3]),
    ]
    for copy in copies:
        copy.start()
    copies[0].wait()
    copies[1].wait()
    total = jnp.zeros((8, 128), F32)
    rows = lax.broadcasted_iota(jnp.int32, (C, 128), 0)
    lanes = lax.broadcasted_iota(jnp.int32, (C, 128), 1)
    size = C // GROUPS
    for k in range(2):
        first[k] = here[k, 0]
        last[k] = here[k, TH - 1]
        x = here[k, 0:TH].astype(F32).reshape(PIX, C)
        sums = jnp.sum(x, axis=0, keepdims=True)
        squares = jnp.sum(x * x, axis=0, keepdims=True)
        for j, part in enumerate((sums, squares)):
            group = lanes - GROUPS * (2 * k + j)
            member = (group >= 0) & (group < GROUPS)
            member = member & (rows >= group * size) & (rows < group * size + size)
            total = total + jnp.dot(
                jnp.broadcast_to(part, (8, C)),
                member.astype(F32),
                precision=HIGHEST,
                preferred_element_type=F32,
            )
    stats[...] = jnp.broadcast_to(total[0:1], stats.shape)
    copies[2].wait()
    copies[3].wait()


def time_bias(step, time_weight, bias, number, table, sems):
    copies = [
        pltpu.make_async_copy(step, number, sems.at[0]),
        pltpu.make_async_copy(time_weight, table, sems.at[1]),
    ]
    for copy in copies:
        copy.start()
    half = C // 2
    lane = lax.broadcasted_iota(jnp.int32, (8, C), 1)
    place = jnp.where(lane < half, lane, lane - half).astype(F32)
    frequency = jnp.exp(-math.log(10000.0) * place / half)
    copies[0].wait()
    angles = number[0].astype(F32) * frequency
    sinusoid = jnp.where(lane < half, jnp.cos(angles), jnp.sin(angles))
    gate = sinusoid * jax.nn.sigmoid(sinusoid)
    copies[1].wait()
    bias[...] = jnp.dot(gate, table[...], precision=HIGHEST, preferred_element_type=F32)


def moments_and_tile(stats, top, bottom, here, moments, side, tile):
    core = lax.axis_index("core")

    total = jnp.broadcast_to(jnp.sum(stats[...], axis=0, keepdims=True), (8, 128))
    groups = lax.broadcasted_iota(jnp.int32, (128, C), 0)
    chans = lax.broadcasted_iota(jnp.int32, (128, C), 1)
    size = C // GROUPS
    entries = float(PIXELS * size)

    def by_channel(k):
        group = groups - GROUPS * k
        member = (group >= 0) & (group < GROUPS)
        member = member & (chans >= group * size) & (chans < group * size + size)
        spread = jnp.dot(total, member.astype(F32), precision=HIGHEST, preferred_element_type=F32)
        return spread[0:1] / entries

    means, scales = [], []
    for s in range(2):
        mean, square = by_channel(2 * s), by_channel(2 * s + 1)
        means.append(mean)
        scales.append(lax.rsqrt(square - mean * mean + 1e-05))
    moments[...] = jnp.concatenate(
        [means[0], scales[0], means[1], scales[1], jnp.zeros((4, C), F32)], axis=0
    )

    for s in range(2):
        tile[s, 0] = top[s]
        tile[s, 1 : TH + 1] = here[s, 0:TH]
        tile[s, TH + 1] = bottom[s]
        tile[s, TH + 2 :] = here[s, TH:]
        x = [tile[s, r].astype(F32) for r in range(TH + 2)]
        column = [
            jnp.concatenate([v[col : col + 1] for v in x] + [jnp.zeros((6, C), F32)], axis=0)
            for col in (0, TW - 1)
        ]
        side[s] = jnp.where(core == 0, column[0], column[1]).astype(BF16)


def forward(
    moments, bias, mine, theirs, my_side, their_side, gain_far, shift_far, ref_gain_far, ref_shift_far,
    weight_far, ref_far, cols, cot_out, small, field, act, back, weight, ref_weight, gain, shift,
    ref_gain, ref_shift, sems,
):
    pairs = [
        (ref_gain_far, ref_gain), (ref_shift_far, ref_shift), (gain_far, gain), (shift_far, shift),
        (ref_far, ref_weight), (weight_far, weight),
    ]
    copies = [pltpu.make_async_copy(a, b, sems.at[i]) for i, (a, b) in enumerate(pairs)]
    for copy in copies:
        copy.start()
    core = lax.axis_index("core")
    row_at = 2 * lax.axis_index("x") + lax.axis_index("zl")
    chip_at = 2 * lax.axis_index("zh")
    col_at = (chip_at + core, chip_at + 1 - core)

    means = [moments[2 * s : 2 * s + 1] for s in range(2)]
    scales = [moments[2 * s + 1 : 2 * s + 2] for s in range(2)]

    tiles = (mine, theirs)
    sides = (my_side, their_side)
    for w in range(2):
        for s in range(2):
            here, beside = tiles[w], tiles[1 - w]
            f = 2 * w + s
            field[f, :, TW + 2 :, :] = jnp.zeros((TH + 2, 22 - TW, C), F32)
            field[f, :, 1 : TW + 1, :] = here[s, 0 : TH + 2].astype(F32)
            outer = sides[w][s].astype(F32)
            is_left = core == w
            for r in range(TH + 2):
                near = beside[s, r].astype(F32)
                out = outer[r : r + 1]
                field[f, r, 0:1, :] = jnp.where(is_left, out, near[TW - 1 : TW])
                field[f, r, TW + 1 : TW + 2, :] = jnp.where(is_left, near[0:1], out)

    column = lax.broadcasted_iota(jnp.int32, (24, C), 0)
    inside = []
    for w in range(2):
        ok = (column < TW + 2) & ((column > 0) | (col_at[w] > 0))
        inside.append(ok & ((column < TW + 1) | (col_at[w] < 7)))

    def valid(w, r):
        if r == 0:
            return inside[w] & (row_at > 0)
        if r == TH + 1:
            return inside[w] & (row_at < 7)
        return inside[w]

    def pre_act(f, r, g, b):
        normed = (field[f, r] - means[f % 2]) * scales[f % 2]
        return normed, normed * g + b

    def columns_of(fields, g, b):
        for f in fields:
            for r in range(TH + 2):
                _, pre = pre_act(f, r, g, b)
                act[r] = jnp.where(valid(f // 2, r), pre * jax.nn.sigmoid(pre), 0.0)
            for t in range(TAPS):
                a, c = t // 3, t % 3
                piece = act[a : a + TH, c : c + TW, :].reshape(PIX, C).astype(BF16)
                cols[f * PIX : (f + 1) * PIX, C * t : C * (t + 1)] = piece

    def base(f):
        tile, s = tiles[f // 2], f % 2
        noise = tile[s, TH + 2 : 2 * TH + 2].astype(F32)
        return (tile[s, 1 : TH + 1].astype(F32) - noise).reshape(PIX, C)

    def residual(fields, kernel):
        conv = jnp.dot(
            cols[0 : PIX * len(fields)],
            kernel[...].reshape(TAPS * C, C),
            preferred_element_type=F32,
        )
        return [base(f) + conv[PIX * f : PIX * (f + 1)] for f in fields]

    def signed_squares(resid):
        return jnp.sum(resid[0] * resid[0] - resid[1] * resid[1], axis=0, keepdims=True)

    time_row = bias[0:1]
    for copy in copies[0:4]:
        copy.wait()
    columns_of((0, 1), ref_gain[...].reshape(1, C), ref_shift[...].reshape(1, C) + time_row)
    copies[4].wait()
    resid = residual((0, 1), ref_weight)
    margin = -signed_squares(resid)
    g, b = gain[...].reshape(1, C), shift[...].reshape(1, C) + time_row
    columns_of((0, 1, 2, 3), g, b)
    copies[5].wait()
    resid = residual((0, 1, 2, 3), weight)
    margin = margin + signed_squares(resid)
    for f in range(4):
        cot_out[PIX * f : PIX * (f + 1)] = (resid[f] if f % 2 == 0 else -resid[f]).astype(BF16)

    cot = cot_out[0 : 2 * PIX]
    back[...] = jnp.zeros_like(back)
    for t in range(TAPS):
        a, c = t // 3, t % 3
        term = lax.dot_general(
            cot, weight[t], (((1,), (1,)), ((), ())), preferred_element_type=F32
        )
        for s in range(2):
            back[s, a : a + TH, c : c + TW, :] += term[s * PIX : (s + 1) * PIX].reshape(TH, TW, C)
    gains = jnp.zeros((24, C), F32)
    shifts = jnp.zeros((24, C), F32)
    for s in range(2):
        for r in range(TH + 2):
            normed, pre = pre_act(s, r, g, b)
            gate = jax.nn.sigmoid(pre)
            slope = gate * (1.0 + pre * (1.0 - gate))
            dpre = jnp.where(valid(0, r), back[s, r] * slope, 0.0)
            gains = gains + dpre * normed
            shifts = shifts + dpre
    gains = jnp.sum(gains, axis=0, keepdims=True)
    shifts = jnp.sum(shifts, axis=0, keepdims=True)
    margin = jnp.broadcast_to(jnp.sum(margin, axis=1, keepdims=True), (1, WIDE))
    small[...] = jnp.concatenate(
        [side_by_side(gains, shifts), margin, jnp.zeros((6, WIDE), F32)], axis=0
    )


def kernel_gradient(cols, cot, out, grad):
    grad[0 : TAPS * C, :] = lax.dot_general(
        cols[...], cot[...], (((0,), (0,)), ((), ())), preferred_element_type=F32
    )
    row = lax.broadcasted_iota(jnp.int32, (48, C), 0)
    for core in range(2):

        @pl.when(lax.axis_index("core") == core)
        def _():
            for q in range(32):
                start = BLK * (2 * q + core)
                out[q] = jnp.where(row < BLK, grad[start : start + 48, :], 0.0)


def pack_blocks(blocks, small, other, out, extra):
    write_extras(extra, small[...] + other[...])

    def body(dest, carry):
        for pair in range(2):
            q = 4 * dest + 2 * pair
            packed = packed_pair(side_by_side(blocks[q], blocks[q + 1]), extra[pair])
            for k, tile in enumerate(tiles_of(pair)):
                out[dest, tile] = packed[:, 128 * k : 128 * k + 128]
        return carry

    lax.fori_loop(0, 8, body, 0)


def chip_sum(blocks, out):
    def pair_of(source, pair, rows):
        parts = [blocks[source, tile].astype(jnp.int32)[rows] for tile in tiles_of(pair)]
        return jnp.concatenate(parts, axis=1)

    tail_rows = slice(40, 48)
    small = jnp.zeros((8, WIDE), F32)
    for source in range(8):
        small = small + read_extras([pair_of(source, k, tail_rows) for k in range(2)])
    high, low, exps = split_small(small[:, 0:128])
    lane = lax.broadcasted_iota(jnp.int32, (1, 128), 1)
    tail = jnp.zeros((1, 128), F32)
    vectors = []
    for k, vector in enumerate(apart(small[0:1])):
        e = exponent(jnp.max(jnp.abs(vector), axis=1, keepdims=True))
        q = rounded(vector, e)
        q = jnp.concatenate([q, jnp.zeros((1, 64), F32)], axis=1)
        vectors += [q[:, 0:128], q[:, 128:256], q[:, 256:384]]
        tail = jnp.where(lane == k, e.astype(F32), tail)
    for k, part in enumerate((high, low, exps)):
        tail = jnp.where(lane == 2 + k, part[1:2], tail)

    def body(pair, carry):
        both = jnp.zeros((48, WIDE), F32)
        for source in range(8):
            both = both + unpacked_pair(pair_of(source, pair, slice(0, 48)))
        e = exponent(jnp.max(jnp.abs(both), axis=0, keepdims=True))
        values = apart(rounded(both, e))
        levels = apart(e.astype(F32))
        for k in range(2):
            for y in range(8):
                part = values[k][:, 40 * y : 40 * y + 40]
                tile = jnp.concatenate(
                    [part[0:16], part[16:32], part[32:48], jnp.zeros((16, 8), F32)], axis=1
                )
                ey = levels[k][:, 40 * y : 40 * y + 40]
                ey = jnp.concatenate([ey, ey, ey, jnp.zeros((1, 8), F32)], axis=1)
                full = jnp.concatenate([tile] + vectors + [ey, tail], axis=0)
                out[y, 2 * pair + k] = full.astype(jnp.int32).astype(I16)
        return carry

    lax.fori_loop(0, 2, body, 0)


def final_sum(blocks, loss, grad, gain, shift):
    y_at = lax.axis_index("y")
    weights = jnp.zeros((16, 128), F32)
    vectors = jnp.zeros((8, 128), F32)
    mine = jnp.zeros((1, 1), F32)
    row = lax.broadcasted_iota(jnp.int32, (8, 128), 0)
    for pair in range(8):
        part = jnp.zeros((16, 128), F32)
        vector = jnp.zeros((8, 128), F32)
        margin = jnp.zeros((1, 1), F32)
        for z in range(4):
            q = blocks[pair, z].astype(jnp.int32)
            v = q.astype(F32)
            tail = q[16:24]
            part = part + v[0:16] * pow2(tail[6:7] - 15)
            factor = pow2(tail[7:8] - 15)
            vector = vector + v[16:24] * jnp.where(row < 3, factor[:, 0:1], factor[:, 1:2])
            margin = margin + (v[23:24, 2:3] + v[23:24, 3:4] * (1.0 / 32768.0)) * factor[:, 4:5]
        margin = BETA * (margin / float(PIXELS * C))
        scale = BETA * jax.nn.sigmoid(margin) * (2.0 / (8 * C))
        weights = weights + scale * part
        vectors = vectors + scale * vector
        mine = jnp.where(y_at == pair, margin, mine)
    near = jnp.exp(-jnp.abs(mine))
    one = 1.0 + near
    log1p = jnp.where(one == 1.0, near, jnp.log(one) * near / jnp.where(one == 1.0, 1.0, one - 1.0))
    loss[...] = jnp.maximum(mine, 0.0) + log1p
    tall = jnp.concatenate([weights, jnp.roll(weights, -40, 1), jnp.roll(weights, -80, 1)], axis=0)
    tall = jnp.concatenate([tall, jnp.zeros((80, 128), F32)], axis=0)
    grad[...] = tall.T[0:40, 0:BLK]
    for out, k in ((gain, 0), (shift, 3)):
        pieces = [vectors[k : k + 1], vectors[k + 1 : k + 2], vectors[k + 2 : k + 3, 0:64]]
        out[...] = jnp.concatenate(pieces, axis=1).reshape(C)


def local(
    timesteps, features_win, features_lose, noise_win, noise_lose, conv_weight, ref_weight,
    norm_gain, norm_shift, ref_gain, ref_shift, time_weight,
):
    fw, fl = features_win[0], features_lose[0]
    strip = (2, TW, C)
    rows, columns = ("x", "zl"), ("zh", "core")
    up = [((i + 1) % 8, i) for i in range(8)]
    down = [(i, (i + 1) % 8) for i in range(8)]
    outward = [(i, (i + 1) % 8 if i % 2 else (i + 7) % 8) for i in range(8)]
    beyond = [(i, (i + 2) % 8 if i % 2 else (i + 6) % 8) for i in range(8)]
    swap = [(0, 1), (1, 0)]

    stats, first, last, here = call(
        statistics,
        [((64, 128), F32), (strip, BF16), (strip, BF16), ((2, 2 * TH, TW, C), BF16)],
        [pltpu.SemaphoreType.DMA((4,))],
        flops=10**7,
        nbytes=10**6,
        far=range(4),
        grant=57,
    )(fw, fl, noise_win[0], noise_lose[0])
    stats = lax.all_to_all(stats, ("x", "zl", "zh", "core"), 0, 0, tiled=True)
    top = lax.ppermute(last, rows, down)
    bottom = lax.ppermute(first, rows, up)
    (bias,) = call(
        time_bias,
        [((8, C), F32)],
        [pltpu.SMEM((1,), jnp.int32), pltpu.VMEM((C, C), F32), pltpu.SemaphoreType.DMA((2,))],
        flops=10**7,
        nbytes=10**6,
        far=(0, 1),
    )(timesteps, time_weight)
    moments, side, mine = call(
        moments_and_tile,
        [((8, C), F32), (strip, BF16), ((2, 2 * TH + 2, TW, C), BF16)],
        flops=2 * 10**10,
        nbytes=10**6,
    )(stats, top, bottom, here)
    my_side = lax.ppermute(side, columns, outward)
    their_side = lax.ppermute(side, columns, beyond)
    theirs = lax.ppermute(mine, "core", swap)

    cols, cot, small = call(
        forward,
        [((4 * PIX, TAPS * C), BF16), ((4 * PIX, C), BF16), ((8, WIDE), F32)],
        [
            pltpu.VMEM((4, TH + 2, 24, C), F32),
            pltpu.VMEM((TH + 2, 24, C), F32),
            pltpu.VMEM((2, TH + 2, 24, C), F32),
            pltpu.VMEM((TAPS, C, C), BF16),
            pltpu.VMEM((TAPS, C, C), BF16),
        ]
        + [pltpu.VMEM((C,), F32)] * 4
        + [pltpu.SemaphoreType.DMA((6,))],
        flops=2 * 10**9,
        nbytes=10**7,
        far=range(6, 12),
    )(
        moments, bias, mine, theirs, my_side, their_side, norm_gain, norm_shift, ref_gain, ref_shift,
        conv_weight, ref_weight,
    )
    other = lax.ppermute(small, "core", swap)
    block = (32, 48, C)
    (blocks,) = call(
        kernel_gradient,
        [(block, F32)],
        [pltpu.VMEM((TAPS * C + 8, C), F32)],
        flops=10**9,
        nbytes=10**7,
    )(cols, cot)
    (blocks,) = call(
        pack_blocks, [((8, 10, 48, 128), I16)], [pltpu.VMEM((2, 8, WIDE), F32)]
    )(blocks, small, other)
    blocks = lax.all_to_all(blocks, ("x", "zl"), 0, 0, tiled=True)
    (sums,) = call(chip_sum, [((8, 4, 24, 128), I16)])(blocks)
    sums = lax.all_to_all(sums.reshape(32, 24, 128), ("y", "zh"), 0, 0, tiled=True)
    loss, grad, gain, shift = call(
        final_sum, [((1, 1), F32), ((40, BLK), F32), ((C,), F32), ((C,), F32)]
    )(sums.reshape(8, 4, 24, 128))
    return loss.reshape(1), grad, gain, shift


def solution(mesh):
    fine = Mesh(mesh.devices.reshape(8, 4, 2, 4, 2), ("y", "x", "zl", "zh", "core"))
    image = P("y", ("x", "zl"), ("zh", "core"), None)
    return jax.shard_map(
        local,
        mesh=fine,
        in_specs=(P("y"), image, image, image, image) + (P(),) * 7,
        out_specs=(P("y"), P("y", ("x", "zl", "zh", "core")), P(), P()),
        check_vma=False,
    )
```

```python
import functools
import math

import jax
import jax.numpy as jnp
from jax import lax
from jax.experimental import pallas as pl
from jax.experimental.pallas import tpu as pltpu
from jax.sharding import Mesh
from jax.sharding import PartitionSpec as P

C = 320
GROUPS = 32
TAPS = 9
TH, TW = 8, 16
PIX = TH * TW
WIDE = 2 * C
BLK = 45
PIXELS = 64 * 128
BETA = 40.0
F32 = jnp.float32
BF16 = jnp.bfloat16
I16 = jnp.int16
HIGHEST = lax.Precision.HIGHEST


def call(kernel, outs, scratch=(), flops=0, nbytes=0, far=(), grant=28):
    def run(*args):
        specs = [
            pl.BlockSpec(memory_space=pltpu.HBM if i in far else pltpu.VMEM) for i in range(len(args))
        ]
        return pl.pallas_call(
            kernel,
            out_shape=[jax.ShapeDtypeStruct(s, d) for s, d in outs],
            in_specs=specs,
            out_specs=[pl.BlockSpec(memory_space=pltpu.VMEM) for _ in outs],
            scratch_shapes=list(scratch),
            compiler_params=pltpu.CompilerParams(vmem_limit_bytes=grant * 2**20),
            cost_estimate=pl.CostEstimate(flops=flops, bytes_accessed=nbytes, transcendentals=0),
        )(*args)

    return run


def pow2(n):
    size = jnp.abs(n)
    out = jnp.ones(n.shape, F32)
    for bit in range(7):
        step = jnp.where(n < 0, 0.5 ** (2**bit) if bit < 7 else 0.0, 2.0 ** (2**bit))
        out = out * jnp.where((size & (1 << bit)) != 0, step, 1.0)
    return out


def exponent(peak):
    level = jnp.log(jnp.maximum(peak, 1e-30)) * (1.0 / math.log(2.0))
    return jnp.clip(jnp.ceil(level + 0.01), -100.0, 100.0).astype(jnp.int32)


def rounded(values, exps):
    return jnp.round(values * pow2(15 - exps))


def split_small(small):
    exps = exponent(jnp.abs(small))
    scaled = small * pow2(15 - exps)
    high = jnp.round(scaled)
    low = jnp.round((scaled - high) * 32768.0)
    return high, low, exps.astype(F32)


def side_by_side(one, two):
    return jnp.concatenate([one[:, 0:256], two[:, 0:256], one[:, 256:C], two[:, 256:C]], axis=1)


def apart(both):
    one = jnp.concatenate([both[:, 0:256], both[:, 512:576]], axis=1)
    two = jnp.concatenate([both[:, 256:512], both[:, 576:640]], axis=1)
    return one, two


def write_extras(extra, small):
    high, low, exps = split_small(small)
    lane = lax.broadcasted_iota(jnp.int32, (1, WIDE), 1)
    extra[...] = jnp.zeros_like(extra)
    extra[0, 0:1] = high[0:1]
    extra[0, 1:2] = low[0:1]
    extra[1, 0:1] = exps[0:1]
    margin = jnp.where(lane == 1, low[1:2], exps[1:2])
    extra[1, 1:2] = jnp.where(lane == 0, high[1:2], margin)


def read_extras(tails):
    high, low, exps = tails[0][6:7], tails[0][7:8], tails[1][6:7]
    sums = (high.astype(F32) + low.astype(F32) * (1.0 / 32768.0)) * pow2(exps - 15)
    row = tails[1][7:8]
    value = row.astype(F32)
    margin = (value[:, 0:1] + value[:, 1:2] * (1.0 / 32768.0)) * pow2(row[:, 2:3] - 15)
    margin = jnp.broadcast_to(margin, (1, WIDE))
    return jnp.concatenate([sums, margin, jnp.zeros((6, WIDE), F32)], axis=0)


def packed_pair(pair, extra):
    exps = exponent(jnp.max(jnp.abs(pair), axis=0, keepdims=True))
    q = rounded(pair, exps)
    row = lax.broadcasted_iota(jnp.int32, (8, WIDE), 0)
    tail = jnp.where(row == 5, exps.astype(F32), q[40:48])
    tail = jnp.where(row == 6, extra[0:1], tail)
    tail = jnp.where(row == 7, extra[1:2], tail)
    q = jnp.concatenate([q[0:40], tail], axis=0)
    return q.astype(jnp.int32).astype(I16)


def unpacked_pair(q):
    v = q.astype(F32) * pow2(q[45:46] - 15)
    row = lax.broadcasted_iota(jnp.int32, (8, WIDE), 0)
    return jnp.concatenate([v[0:40], jnp.where(row < BLK - 40, v[40:48], 0.0)], axis=0)


def tiles_of(pair):
    return [4 * pair, 4 * pair + 1, 4 * pair + 2, 4 * pair + 3, 8 + pair]


def statistics(fw, fl, nw, nl, stats, first, last, edge, here, sems):
    copies = [
        pltpu.make_async_copy(fw, here.at[0, pl.ds(0, TH)], sems.at[0]),
        pltpu.make_async_copy(fl, here.at[1, pl.ds(0, TH)], sems.at[1]),
        pltpu.make_async_copy(nw, here.at[0, pl.ds(TH, TH)], sems.at[2]),
        pltpu.make_async_copy(nl, here.at[1, pl.ds(TH, TH)], sems.at[3]),
    ]
    for copy in copies:
        copy.start()
    copies[0].wait()
    copies[1].wait()
    total = jnp.zeros((8, 128), F32)
    rows = lax.broadcasted_iota(jnp.int32, (C, 128), 0)
    lanes = lax.broadcasted_iota(jnp.int32, (C, 128), 1)
    size = C // GROUPS
    for k in range(2):
        first[k] = here[k, 0]
        last[k] = here[k, TH - 1]
        field = here[k, 0:TH].astype(F32)
        x = field.reshape(PIX, C)
        sums = jnp.sum(x, axis=0, keepdims=True)
        squares = jnp.sum(x * x, axis=0, keepdims=True)
        for j, part in enumerate((sums, squares)):
            group = lanes - GROUPS * (2 * k + j)
            member = (group >= 0) & (group < GROUPS)
            member = member & (rows >= group * size) & (rows < group * size + size)
            total = total + jnp.dot(
                jnp.broadcast_to(part, (8, C)),
                member.astype(F32),
                precision=HIGHEST,
                preferred_element_type=F32,
            )
        column = [
            jnp.concatenate([field[r, col : col + 1] for r in range(TH)], axis=0)
            for col in (0, TW - 1)
        ]
        column = jnp.where(lax.axis_index("core") == 0, column[0], column[1])
        edge[k] = jnp.concatenate([column, jnp.zeros((8, C), F32)], axis=0).astype(BF16)
    stats[...] = jnp.broadcast_to(total[0:1], stats.shape)
    copies[2].wait()
    copies[3].wait()


def time_bias(step, time_weight, bias, number, table, sems):
    copies = [
        pltpu.make_async_copy(step, number, sems.at[0]),
        pltpu.make_async_copy(time_weight, table, sems.at[1]),
    ]
    for copy in copies:
        copy.start()
    half = C // 2
    lane = lax.broadcasted_iota(jnp.int32, (8, C), 1)
    place = jnp.where(lane < half, lane, lane - half).astype(F32)
    frequency = jnp.exp(-math.log(10000.0) * place / half)
    copies[0].wait()
    angles = number[0].astype(F32) * frequency
    sinusoid = jnp.where(lane < half, jnp.cos(angles), jnp.sin(angles))
    gate = sinusoid * jax.nn.sigmoid(sinusoid)
    copies[1].wait()
    bias[...] = jnp.dot(gate, table[...], precision=HIGHEST, preferred_element_type=F32)


def outer_column(top, bottom, edge, side):
    core = lax.axis_index("core")
    for s in range(2):
        above, below = top[s].astype(F32), bottom[s].astype(F32)
        above = jnp.where(core == 0, above[0:1], above[TW - 1 : TW])
        below = jnp.where(core == 0, below[0:1], below[TW - 1 : TW])
        column = [above, edge[s].astype(F32)[0:TH], below, jnp.zeros((6, C), F32)]
        side[s] = jnp.concatenate(column, axis=0).astype(BF16)


def moments_and_tile(stats, top, bottom, side, here, moments, tile):
    total = jnp.broadcast_to(jnp.sum(stats[...], axis=0, keepdims=True), (8, 128))
    groups = lax.broadcasted_iota(jnp.int32, (128, C), 0)
    chans = lax.broadcasted_iota(jnp.int32, (128, C), 1)
    size = C // GROUPS
    entries = float(PIXELS * size)

    def by_channel(k):
        group = groups - GROUPS * k
        member = (group >= 0) & (group < GROUPS)
        member = member & (chans >= group * size) & (chans < group * size + size)
        spread = jnp.dot(total, member.astype(F32), precision=HIGHEST, preferred_element_type=F32)
        return spread[0:1] / entries

    means, scales = [], []
    for s in range(2):
        mean, square = by_channel(2 * s), by_channel(2 * s + 1)
        means.append(mean)
        scales.append(lax.rsqrt(square - mean * mean + 1e-05))
    moments[...] = jnp.concatenate(
        [means[0], scales[0], means[1], scales[1], jnp.zeros((4, C), F32)], axis=0
    )

    for s in range(2):
        tile[s, 0] = top[s]
        tile[s, 1 : TH + 1] = here[s, 0:TH]
        tile[s, TH + 1] = bottom[s]
        tile[s, TH + 2 : 2 * TH + 2] = here[s, TH:]
        tile[s, 2 * TH + 2] = side[s]


def forward(
    moments, bias, mine, theirs, gain_far, shift_far, ref_gain_far, ref_shift_far,
    weight_far, ref_far, cols, cot_out, small, field, act, back, weight, ref_weight, gain, shift,
    ref_gain, ref_shift, sems,
):
    pairs = [
        (ref_gain_far, ref_gain), (ref_shift_far, ref_shift), (gain_far, gain), (shift_far, shift),
        (ref_far, ref_weight), (weight_far, weight),
    ]
    copies = [pltpu.make_async_copy(a, b, sems.at[i]) for i, (a, b) in enumerate(pairs)]
    for copy in copies:
        copy.start()
    core = lax.axis_index("core")
    row_at = 2 * lax.axis_index("x") + lax.axis_index("zl")
    chip_at = 2 * lax.axis_index("zh")
    col_at = (chip_at + core, chip_at + 1 - core)

    means = [moments[2 * s : 2 * s + 1] for s in range(2)]
    scales = [moments[2 * s + 1 : 2 * s + 2] for s in range(2)]

    tiles = (mine, theirs)
    for w in range(2):
        for s in range(2):
            here, beside = tiles[w], tiles[1 - w]
            f = 2 * w + s
            field[f, :, TW + 2 :, :] = jnp.zeros((TH + 2, 22 - TW, C), F32)
            field[f, :, 1 : TW + 1, :] = here[s, 0 : TH + 2].astype(F32)
            outer = here[s, 2 * TH + 2].astype(F32)
            is_left = core == w
            for r in range(TH + 2):
                near = beside[s, r].astype(F32)
                out = outer[r : r + 1]
                field[f, r, 0:1, :] = jnp.where(is_left, out, near[TW - 1 : TW])
                field[f, r, TW + 1 : TW + 2, :] = jnp.where(is_left, near[0:1], out)

    column = lax.broadcasted_iota(jnp.int32, (24, C), 0)
    inside = []
    for w in range(2):
        ok = (column < TW + 2) & ((column > 0) | (col_at[w] > 0))
        inside.append(ok & ((column < TW + 1) | (col_at[w] < 7)))

    def valid(w, r):
        if r == 0:
            return inside[w] & (row_at > 0)
        if r == TH + 1:
            return inside[w] & (row_at < 7)
        return inside[w]

    def pre_act(f, r, g, b):
        normed = (field[f, r] - means[f % 2]) * scales[f % 2]
        return normed, normed * g + b

    def columns_of(fields, g, b):
        for f in fields:
            for r in range(TH + 2):
                _, pre = pre_act(f, r, g, b)
                act[r] = jnp.where(valid(f // 2, r), pre * jax.nn.sigmoid(pre), 0.0)
            for t in range(TAPS):
                a, c = t // 3, t % 3
                piece = act[a : a + TH, c : c + TW, :].reshape(PIX, C).astype(BF16)
                cols[f * PIX : (f + 1) * PIX, C * t : C * (t + 1)] = piece

    def base(f):
        tile, s = tiles[f // 2], f % 2
        noise = tile[s, TH + 2 : 2 * TH + 2].astype(F32)
        return (tile[s, 1 : TH + 1].astype(F32) - noise).reshape(PIX, C)

    def residual(fields, kernel):
        conv = jnp.dot(
            cols[0 : PIX * len(fields)],
            kernel[...].reshape(TAPS * C, C),
            preferred_element_type=F32,
        )
        return [base(f) + conv[PIX * f : PIX * (f + 1)] for f in fields]

    def signed_squares(resid):
        return jnp.sum(resid[0] * resid[0] - resid[1] * resid[1], axis=0, keepdims=True)

    time_row = bias[0:1]
    for copy in copies[0:4]:
        copy.wait()
    columns_of((0, 1), ref_gain[...].reshape(1, C), ref_shift[...].reshape(1, C) + time_row)
    copies[4].wait()
    resid = residual((0, 1), ref_weight)
    margin = -signed_squares(resid)
    g, b = gain[...].reshape(1, C), shift[...].reshape(1, C) + time_row
    columns_of((0, 1, 2, 3), g, b)
    copies[5].wait()
    resid = residual((0, 1, 2, 3), weight)
    margin = margin + signed_squares(resid)
    for f in range(4):
        cot_out[PIX * f : PIX * (f + 1)] = (resid[f] if f % 2 == 0 else -resid[f]).astype(BF16)

    cot = cot_out[0 : 2 * PIX]
    back[...] = jnp.zeros_like(back)
    for t in range(TAPS):
        a, c = t // 3, t % 3
        term = lax.dot_general(
            cot, weight[t], (((1,), (1,)), ((), ())), preferred_element_type=F32
        )
        for s in range(2):
            back[s, a : a + TH, c : c + TW, :] += term[s * PIX : (s + 1) * PIX].reshape(TH, TW, C)
    gains = jnp.zeros((24, C), F32)
    shifts = jnp.zeros((24, C), F32)
    for s in range(2):
        for r in range(TH + 2):
            normed, pre = pre_act(s, r, g, b)
            gate = jax.nn.sigmoid(pre)
            slope = gate * (1.0 + pre * (1.0 - gate))
            dpre = jnp.where(valid(0, r), back[s, r] * slope, 0.0)
            gains = gains + dpre * normed
            shifts = shifts + dpre
    gains = jnp.sum(gains, axis=0, keepdims=True)
    shifts = jnp.sum(shifts, axis=0, keepdims=True)
    margin = jnp.broadcast_to(jnp.sum(margin, axis=1, keepdims=True), (1, WIDE))
    small[...] = jnp.concatenate(
        [side_by_side(gains, shifts), margin, jnp.zeros((6, WIDE), F32)], axis=0
    )


def kernel_gradient(cols, cot, out, grad):
    grad[0 : TAPS * C, :] = lax.dot_general(
        cols[...], cot[...], (((0,), (0,)), ((), ())), preferred_element_type=F32
    )
    row = lax.broadcasted_iota(jnp.int32, (48, C), 0)
    for core in range(2):

        @pl.when(lax.axis_index("core") == core)
        def _():
            for q in range(32):
                start = BLK * (2 * q + core)
                out[q] = jnp.where(row < BLK, grad[start : start + 48, :], 0.0)


def pack_blocks(blocks, small, other, out, extra):
    write_extras(extra, small[...] + other[...])

    def body(dest, carry):
        for pair in range(2):
            q = 4 * dest + 2 * pair
            packed = packed_pair(side_by_side(blocks[q], blocks[q + 1]), extra[pair])
            for k, tile in enumerate(tiles_of(pair)):
                out[dest, tile] = packed[:, 128 * k : 128 * k + 128]
        return carry

    lax.fori_loop(0, 8, body, 0)


def chip_sum(blocks, out):
    def pair_of(source, pair, rows):
        parts = [blocks[source, tile].astype(jnp.int32)[rows] for tile in tiles_of(pair)]
        return jnp.concatenate(parts, axis=1)

    tail_rows = slice(40, 48)
    small = jnp.zeros((8, WIDE), F32)
    for source in range(8):
        small = small + read_extras([pair_of(source, k, tail_rows) for k in range(2)])
    high, low, exps = split_small(small[:, 0:128])
    lane = lax.broadcasted_iota(jnp.int32, (1, 128), 1)
    tail = jnp.zeros((1, 128), F32)
    vectors = []
    for k, vector in enumerate(apart(small[0:1])):
        e = exponent(jnp.max(jnp.abs(vector), axis=1, keepdims=True))
        q = rounded(vector, e)
        q = jnp.concatenate([q, jnp.zeros((1, 64), F32)], axis=1)
        vectors += [q[:, 0:128], q[:, 128:256], q[:, 256:384]]
        tail = jnp.where(lane == k, e.astype(F32), tail)
    for k, part in enumerate((high, low, exps)):
        tail = jnp.where(lane == 2 + k, part[1:2], tail)

    def body(pair, carry):
        both = jnp.zeros((48, WIDE), F32)
        for source in range(8):
            both = both + unpacked_pair(pair_of(source, pair, slice(0, 48)))
        e = exponent(jnp.max(jnp.abs(both), axis=0, keepdims=True))
        values = apart(rounded(both, e))
        levels = apart(e.astype(F32))
        for k in range(2):
            for y in range(8):
                part = values[k][:, 40 * y : 40 * y + 40]
                tile = jnp.concatenate(
                    [part[0:16], part[16:32], part[32:48], jnp.zeros((16, 8), F32)], axis=1
                )
                ey = levels[k][:, 40 * y : 40 * y + 40]
                ey = jnp.concatenate([ey, ey, ey, jnp.zeros((1, 8), F32)], axis=1)
                full = jnp.concatenate([tile] + vectors + [ey, tail], axis=0)
                out[y, 2 * pair + k] = full.astype(jnp.int32).astype(I16)
        return carry

    lax.fori_loop(0, 2, body, 0)


def final_sum(blocks, loss, grad, gain, shift):
    y_at = lax.axis_index("y")
    weights = jnp.zeros((16, 128), F32)
    vectors = jnp.zeros((8, 128), F32)
    mine = jnp.zeros((1, 1), F32)
    row = lax.broadcasted_iota(jnp.int32, (8, 128), 0)
    for pair in range(8):
        part = jnp.zeros((16, 128), F32)
        vector = jnp.zeros((8, 128), F32)
        margin = jnp.zeros((1, 1), F32)
        for z in range(4):
            q = blocks[pair, z].astype(jnp.int32)
            v = q.astype(F32)
            tail = q[16:24]
            part = part + v[0:16] * pow2(tail[6:7] - 15)
            factor = pow2(tail[7:8] - 15)
            vector = vector + v[16:24] * jnp.where(row < 3, factor[:, 0:1], factor[:, 1:2])
            margin = margin + (v[23:24, 2:3] + v[23:24, 3:4] * (1.0 / 32768.0)) * factor[:, 4:5]
        margin = BETA * (margin / float(PIXELS * C))
        scale = BETA * jax.nn.sigmoid(margin) * (2.0 / (8 * C))
        weights = weights + scale * part
        vectors = vectors + scale * vector
        mine = jnp.where(y_at == pair, margin, mine)
    near = jnp.exp(-jnp.abs(mine))
    one = 1.0 + near
    log1p = jnp.where(one == 1.0, near, jnp.log(one) * near / jnp.where(one == 1.0, 1.0, one - 1.0))
    loss[...] = jnp.maximum(mine, 0.0) + log1p
    tall = jnp.concatenate([weights, jnp.roll(weights, -40, 1), jnp.roll(weights, -80, 1)], axis=0)
    tall = jnp.concatenate([tall, jnp.zeros((80, 128), F32)], axis=0)
    grad[...] = tall.T[0:40, 0:BLK]
    for out, k in ((gain, 0), (shift, 3)):
        pieces = [vectors[k : k + 1], vectors[k + 1 : k + 2], vectors[k + 2 : k + 3, 0:64]]
        out[...] = jnp.concatenate(pieces, axis=1).reshape(C)


def local(
    timesteps, features_win, features_lose, noise_win, noise_lose, conv_weight, ref_weight,
    norm_gain, norm_shift, ref_gain, ref_shift, time_weight,
):
    fw, fl = features_win[0], features_lose[0]
    strip = (2, TW, C)
    rows, columns = ("x", "zl"), ("zh", "core")
    up = [((i + 1) % 8, i) for i in range(8)]
    down = [(i, (i + 1) % 8) for i in range(8)]
    outward = [(i, (i + 1) % 8 if i % 2 else (i + 7) % 8) for i in range(8)]
    swap = [(0, 1), (1, 0)]

    stats, first, last, edge, here = call(
        statistics,
        [((64, 128), F32)] + [(strip, BF16)] * 3 + [((2, 2 * TH, TW, C), BF16)],
        [pltpu.SemaphoreType.DMA((4,))],
        flops=10**7,
        nbytes=10**6,
        far=range(4),
        grant=57,
    )(fw, fl, noise_win[0], noise_lose[0])
    stats = lax.all_to_all(stats, ("x", "zl", "zh", "core"), 0, 0, tiled=True)
    top = lax.ppermute(last, rows, down)
    bottom = lax.ppermute(first, rows, up)
    (bias,) = call(
        time_bias,
        [((8, C), F32)],
        [pltpu.SMEM((1,), jnp.int32), pltpu.VMEM((C, C), F32), pltpu.SemaphoreType.DMA((2,))],
        flops=10**7,
        nbytes=10**6,
        far=(0, 1),
    )(timesteps, time_weight)
    (side,) = call(outer_column, [(strip, BF16)])(top, bottom, edge)
    side = lax.ppermute(side, columns, outward)
    moments, mine = call(
        moments_and_tile,
        [((8, C), F32), ((2, 2 * TH + 3, TW, C), BF16)],
        flops=2 * 10**10,
        nbytes=10**6,
    )(stats, top, bottom, side, here)
    theirs = lax.ppermute(mine, "core", swap)

    cols, cot, small = call(
        forward,
        [((4 * PIX, TAPS * C), BF16), ((4 * PIX, C), BF16), ((8, WIDE), F32)],
        [
            pltpu.VMEM((4, TH + 2, 24, C), F32),
            pltpu.VMEM((TH + 2, 24, C), F32),
            pltpu.VMEM((2, TH + 2, 24, C), F32),
            pltpu.VMEM((TAPS, C, C), BF16),
            pltpu.VMEM((TAPS, C, C), BF16),
        ]
        + [pltpu.VMEM((C,), F32)] * 4
        + [pltpu.SemaphoreType.DMA((6,))],
        flops=2 * 10**9,
        nbytes=10**7,
        far=range(4, 10),
    )(
        moments, bias, mine, theirs, norm_gain, norm_shift, ref_gain, ref_shift,
        conv_weight, ref_weight,
    )
    other = lax.ppermute(small, "core", swap)
    block = (32, 48, C)
    (blocks,) = call(
        kernel_gradient,
        [(block, F32)],
        [pltpu.VMEM((TAPS * C + 8, C), F32)],
        flops=10**9,
        nbytes=10**7,
    )(cols, cot)
    (blocks,) = call(
        pack_blocks, [((8, 10, 48, 128), I16)], [pltpu.VMEM((2, 8, WIDE), F32)]
    )(blocks, small, other)
    blocks = lax.all_to_all(blocks, ("x", "zl"), 0, 0, tiled=True)
    (sums,) = call(chip_sum, [((8, 4, 24, 128), I16)])(blocks)
    sums = lax.all_to_all(sums.reshape(32, 24, 128), ("y", "zh"), 0, 0, tiled=True)
    loss, grad, gain, shift = call(
        final_sum, [((1, 1), F32), ((40, BLK), F32), ((C,), F32), ((C,), F32)]
    )(sums.reshape(8, 4, 24, 128))
    return loss.reshape(1), grad, gain, shift


def solution(mesh):
    fine = Mesh(mesh.devices.reshape(8, 4, 2, 4, 2), ("y", "x", "zl", "zh", "core"))
    image = P("y", ("x", "zl"), ("zh", "core"), None)
    return jax.shard_map(
        local,
        mesh=fine,
        in_specs=(P("y"), image, image, image, image) + (P(),) * 7,
        out_specs=(P("y"), P("y", ("x", "zl", "zh", "core")), P(), P()),
        check_vma=False,
    )
```

```python
import functools
import math

import jax
import jax.numpy as jnp
from jax import lax
from jax.experimental import pallas as pl
from jax.experimental.pallas import tpu as pltpu
from jax.sharding import Mesh
from jax.sharding import PartitionSpec as P

C = 320
GROUPS = 32
TAPS = 9
TH, TW = 8, 16
PIX = TH * TW
WIDE = 2 * C
BLK = 45
PIXELS = 64 * 128
BETA = 40.0
F32 = jnp.float32
BF16 = jnp.bfloat16
I16 = jnp.int16
HIGHEST = lax.Precision.HIGHEST


def call(kernel, outs, scratch=(), flops=0, nbytes=0, far=(), grant=28):
    def run(*args):
        specs = [
            pl.BlockSpec(memory_space=pltpu.HBM if i in far else pltpu.VMEM) for i in range(len(args))
        ]
        return pl.pallas_call(
            kernel,
            out_shape=[jax.ShapeDtypeStruct(s, d) for s, d in outs],
            in_specs=specs,
            out_specs=[pl.BlockSpec(memory_space=pltpu.VMEM) for _ in outs],
            scratch_shapes=list(scratch),
            compiler_params=pltpu.CompilerParams(vmem_limit_bytes=grant * 2**20),
            cost_estimate=pl.CostEstimate(flops=flops, bytes_accessed=nbytes, transcendentals=0),
        )(*args)

    return run


def pow2(n):
    size = jnp.abs(n)
    out = jnp.ones(n.shape, F32)
    for bit in range(7):
        step = jnp.where(n < 0, 0.5 ** (2**bit) if bit < 7 else 0.0, 2.0 ** (2**bit))
        out = out * jnp.where((size & (1 << bit)) != 0, step, 1.0)
    return out


def exponent(peak):
    level = jnp.log(jnp.maximum(peak, 1e-30)) * (1.0 / math.log(2.0))
    return jnp.clip(jnp.ceil(level + 0.01), -100.0, 100.0).astype(jnp.int32)


def rounded(values, exps):
    return jnp.round(values * pow2(15 - exps))


def split_small(small):
    exps = exponent(jnp.abs(small))
    scaled = small * pow2(15 - exps)
    high = jnp.round(scaled)
    low = jnp.round((scaled - high) * 32768.0)
    return high, low, exps.astype(F32)


def side_by_side(one, two):
    return jnp.concatenate([one[:, 0:256], two[:, 0:256], one[:, 256:C], two[:, 256:C]], axis=1)


def apart(both):
    one = jnp.concatenate([both[:, 0:256], both[:, 512:576]], axis=1)
    two = jnp.concatenate([both[:, 256:512], both[:, 576:640]], axis=1)
    return one, two


def write_extras(extra, small):
    high, low, exps = split_small(small)
    lane = lax.broadcasted_iota(jnp.int32, (1, WIDE), 1)
    extra[...] = jnp.zeros_like(extra)
    extra[0, 0:1] = high[0:1]
    extra[0, 1:2] = low[0:1]
    extra[1, 0:1] = exps[0:1]
    margin = jnp.where(lane == 1, low[1:2], exps[1:2])
    extra[1, 1:2] = jnp.where(lane == 0, high[1:2], margin)


def read_extras(tails):
    high, low, exps = tails[0][6:7], tails[0][7:8], tails[1][6:7]
    sums = (high.astype(F32) + low.astype(F32) * (1.0 / 32768.0)) * pow2(exps - 15)
    row = tails[1][7:8]
    value = row.astype(F32)
    margin = (value[:, 0:1] + value[:, 1:2] * (1.0 / 32768.0)) * pow2(row[:, 2:3] - 15)
    margin = jnp.broadcast_to(margin, (1, WIDE))
    return jnp.concatenate([sums, margin, jnp.zeros((6, WIDE), F32)], axis=0)


def packed_pair(pair, extra):
    exps = exponent(jnp.max(jnp.abs(pair), axis=0, keepdims=True))
    q = rounded(pair, exps)
    row = lax.broadcasted_iota(jnp.int32, (8, WIDE), 0)
    tail = jnp.where(row == 5, exps.astype(F32), q[40:48])
    tail = jnp.where(row == 6, extra[0:1], tail)
    tail = jnp.where(row == 7, extra[1:2], tail)
    q = jnp.concatenate([q[0:40], tail], axis=0)
    return q.astype(jnp.int32).astype(I16)


def unpacked_pair(q):
    v = q.astype(F32) * pow2(q[45:46] - 15)
    row = lax.broadcasted_iota(jnp.int32, (8, WIDE), 0)
    return jnp.concatenate([v[0:40], jnp.where(row < BLK - 40, v[40:48], 0.0)], axis=0)


def tiles_of(pair):
    return [4 * pair, 4 * pair + 1, 4 * pair + 2, 4 * pair + 3, 8 + pair]


def edge_rows(fw, fl, first, last, sems):
    copies = []
    for k, ref in enumerate((fw, fl)):
        copies.append(pltpu.make_async_copy(ref.at[0], first.at[k], sems.at[2 * k]))
        copies.append(pltpu.make_async_copy(ref.at[TH - 1], last.at[k], sems.at[2 * k + 1]))
    for copy in copies:
        copy.start()
    for copy in copies:
        copy.wait()


def statistics(fw, fl, nw, nl, stats, edge, here, sems):
    copies = [
        pltpu.make_async_copy(fw, here.at[0, pl.ds(0, TH)], sems.at[0]),
        pltpu.make_async_copy(fl, here.at[1, pl.ds(0, TH)], sems.at[1]),
        pltpu.make_async_copy(nw, here.at[0, pl.ds(TH, TH)], sems.at[2]),
        pltpu.make_async_copy(nl, here.at[1, pl.ds(TH, TH)], sems.at[3]),
    ]
    for copy in copies:
        copy.start()
    copies[0].wait()
    copies[1].wait()
    total = jnp.zeros((8, 128), F32)
    rows = lax.broadcasted_iota(jnp.int32, (C, 128), 0)
    lanes = lax.broadcasted_iota(jnp.int32, (C, 128), 1)
    size = C // GROUPS
    for k in range(2):
        field = here[k, 0:TH].astype(F32)
        x = field.reshape(PIX, C)
        sums = jnp.sum(x, axis=0, keepdims=True)
        squares = jnp.sum(x * x, axis=0, keepdims=True)
        for j, part in enumerate((sums, squares)):
            group = lanes - GROUPS * (2 * k + j)
            member = (group >= 0) & (group < GROUPS)
            member = member & (rows >= group * size) & (rows < group * size + size)
            total = total + jnp.dot(
                jnp.broadcast_to(part, (8, C)),
                member.astype(F32),
                precision=HIGHEST,
                preferred_element_type=F32,
            )
        column = [
            jnp.concatenate([field[r, col : col + 1] for r in range(TH)], axis=0)
            for col in (0, TW - 1)
        ]
        column = jnp.where(lax.axis_index("core") == 0, column[0], column[1])
        edge[k] = jnp.concatenate([column, jnp.zeros((8, C), F32)], axis=0).astype(BF16)
    stats[...] = jnp.broadcast_to(total[0:1], stats.shape)
    copies[2].wait()
    copies[3].wait()


def time_bias(step, time_weight, bias, number, table, sems):
    copies = [
        pltpu.make_async_copy(step, number, sems.at[0]),
        pltpu.make_async_copy(time_weight, table, sems.at[1]),
    ]
    for copy in copies:
        copy.start()
    half = C // 2
    lane = lax.broadcasted_iota(jnp.int32, (8, C), 1)
    place = jnp.where(lane < half, lane, lane - half).astype(F32)
    frequency = jnp.exp(-math.log(10000.0) * place / half)
    copies[0].wait()
    angles = number[0].astype(F32) * frequency
    sinusoid = jnp.where(lane < half, jnp.cos(angles), jnp.sin(angles))
    gate = sinusoid * jax.nn.sigmoid(sinusoid)
    copies[1].wait()
    bias[...] = jnp.dot(gate, table[...], precision=HIGHEST, preferred_element_type=F32)


def outer_column(top, bottom, edge, side):
    core = lax.axis_index("core")
    for s in range(2):
        above, below = top[s].astype(F32), bottom[s].astype(F32)
        above = jnp.where(core == 0, above[0:1], above[TW - 1 : TW])
        below = jnp.where(core == 0, below[0:1], below[TW - 1 : TW])
        column = [above, edge[s].astype(F32)[0:TH], below, jnp.zeros((6, C), F32)]
        side[s] = jnp.concatenate(column, axis=0).astype(BF16)


def sums_and_tile(stats, top, bottom, side, here, totals, tile):
    total = jnp.sum(stats[...], axis=0, keepdims=True)
    totals[...] = jnp.broadcast_to(total, (8, 128))
    high = total.astype(BF16).astype(F32)
    middle = (total - high).astype(BF16).astype(F32)
    low = total - high - middle
    parts = jnp.concatenate([high, middle, low, jnp.zeros((3, 128), F32)], axis=0)
    parts = jnp.concatenate([parts, jnp.zeros((6, C - 128), F32)], axis=1)
    column = side[0].astype(F32)[0 : TH + 2]
    tile[0, 2 * TH + 2] = jnp.concatenate([column, parts], axis=0).astype(BF16)
    tile[1, 2 * TH + 2] = side[1]
    for s in range(2):
        tile[s, 0] = top[s]
        tile[s, 1 : TH + 1] = here[s, 0:TH]
        tile[s, TH + 1] = bottom[s]
        tile[s, TH + 2 : 2 * TH + 2] = here[s, TH:]


def forward(
    totals, bias, mine, theirs, gain_far, shift_far, ref_gain_far, ref_shift_far,
    weight_far, ref_far, cols, cot_out, small, field, act, back, slope, shifted, weight, ref_weight, gain, shift,
    ref_gain, ref_shift, sems,
):
    pairs = [
        (ref_gain_far, ref_gain), (ref_shift_far, ref_shift), (gain_far, gain), (shift_far, shift),
        (ref_far, ref_weight), (weight_far, weight),
    ]
    copies = [pltpu.make_async_copy(a, b, sems.at[i]) for i, (a, b) in enumerate(pairs)]
    for copy in copies:
        copy.start()
    core = lax.axis_index("core")
    row_at = 2 * lax.axis_index("x") + lax.axis_index("zl")
    chip_at = 2 * lax.axis_index("zh")
    col_at = (chip_at + core, chip_at + 1 - core)

    parts = theirs[0, 2 * TH + 2].astype(F32)[TH + 2 : TH + 5, 0:128]
    total = totals[...] + ((parts[0:1] + parts[1:2]) + parts[2:3])
    groups = lax.broadcasted_iota(jnp.int32, (128, C), 0)
    chans = lax.broadcasted_iota(jnp.int32, (128, C), 1)
    size = C // GROUPS
    entries = float(PIXELS * size)

    def by_channel(k):
        group = groups - GROUPS * k
        member = (group >= 0) & (group < GROUPS)
        member = member & (chans >= group * size) & (chans < group * size + size)
        spread = jnp.dot(total, member.astype(F32), precision=HIGHEST, preferred_element_type=F32)
        return spread[0:1] / entries

    means, scales = [], []
    for s in range(2):
        mean, square = by_channel(2 * s), by_channel(2 * s + 1)
        means.append(mean)
        scales.append(lax.rsqrt(square - mean * mean + 1e-05))

    tiles = (mine, theirs)
    for w in range(2):
        for s in range(2):
            here, beside = tiles[w], tiles[1 - w]
            f = 2 * w + s
            field[f, :, TW + 2 :, :] = jnp.zeros((TH + 2, 22 - TW, C), F32)
            field[f, :, 1 : TW + 1, :] = (here[s, 0 : TH + 2].astype(F32) - means[s]) * scales[s]
            outer = (here[s, 2 * TH + 2].astype(F32) - means[s]) * scales[s]
            is_left = core == w
            for r in range(TH + 2):
                near = (beside[s, r].astype(F32) - means[s]) * scales[s]
                out = outer[r : r + 1]
                field[f, r, 0:1, :] = jnp.where(is_left, out, near[TW - 1 : TW])
                field[f, r, TW + 1 : TW + 2, :] = jnp.where(is_left, near[0:1], out)

    column = lax.broadcasted_iota(jnp.int32, (24, C), 0)
    inside = []
    for w in range(2):
        ok = (column < TW + 2) & ((column > 0) | (col_at[w] > 0))
        inside.append(ok & ((column < TW + 1) | (col_at[w] < 7)))

    def valid(w, r):
        if r == 0:
            return inside[w] & (row_at > 0)
        if r == TH + 1:
            return inside[w] & (row_at < 7)
        return inside[w]

    def columns_of(fields, g, b, slope=None):
        for f in fields:
            for r in range(TH + 2):
                pre = field[f, r] * g + b
                gate = jax.nn.sigmoid(pre)
                value = pre * gate
                act[r] = jnp.where(valid(f // 2, r), value, 0.0)
                if slope is not None and f < 2:
                    slope[f, r] = jnp.where(valid(0, r), gate + value * (1.0 - gate), 0.0)
                for c in range(3):
                    piece = act[r, c : c + TW, :].astype(BF16)
                    for a in range(3):
                        if 0 <= r - a < TH:
                            at, t = f * PIX + TW * (r - a), 3 * a + c
                            cols[at : at + TW, C * t : C * (t + 1)] = piece

    def base(f):
        tile, s = tiles[f // 2], f % 2
        noise = tile[s, TH + 2 : 2 * TH + 2].astype(F32)
        return (tile[s, 1 : TH + 1].astype(F32) - noise).reshape(PIX, C)

    def residual(fields, kernel):
        conv = jnp.dot(
            cols[0 : PIX * len(fields)],
            kernel[...].reshape(TAPS * C, C),
            preferred_element_type=F32,
        )
        return [base(f) + conv[PIX * f : PIX * (f + 1)] for f in fields]

    def signed_squares(resid):
        return jnp.sum(resid[0] * resid[0] - resid[1] * resid[1], axis=0, keepdims=True)

    time_row = bias[0:1]
    for copy in copies[0:4]:
        copy.wait()
    columns_of((0, 1), ref_gain[...].reshape(1, C), ref_shift[...].reshape(1, C) + time_row)
    copies[4].wait()
    resid = residual((0, 1), ref_weight)
    margin = -signed_squares(resid)
    g, b = gain[...].reshape(1, C), shift[...].reshape(1, C) + time_row
    columns_of((0, 1, 2, 3), g, b, slope)
    copies[5].wait()
    resid = residual((0, 1, 2, 3), weight)
    margin = margin + signed_squares(resid)
    for f in range(4):
        cot_out[PIX * f : PIX * (f + 1)] = (resid[f] if f % 2 == 0 else -resid[f]).astype(BF16)

    cot = cot_out[0 : 2 * PIX]
    back[...] = jnp.zeros_like(back)
    for c in range(3):
        shifted[...] = jnp.zeros_like(shifted)
        for a in range(3):
            term = lax.dot_general(
                cot, weight[3 * a + c], (((1,), (1,)), ((), ())), preferred_element_type=F32
            )
            for s in range(2):
                shifted[s, a : a + TH] += term[s * PIX : (s + 1) * PIX].reshape(TH, TW, C)
        back[:, :, c : c + TW, :] += shifted[...]
    gains = jnp.zeros((24, C), F32)
    shifts = jnp.zeros((24, C), F32)
    for s in range(2):
        for r in range(TH + 2):
            dpre = back[s, r] * slope[s, r]
            gains = gains + dpre * field[s, r]
            shifts = shifts + dpre
    gains = jnp.sum(gains, axis=0, keepdims=True)
    shifts = jnp.sum(shifts, axis=0, keepdims=True)
    margin = jnp.broadcast_to(jnp.sum(margin, axis=1, keepdims=True), (1, WIDE))
    small[...] = jnp.concatenate(
        [side_by_side(gains, shifts), margin, jnp.zeros((6, WIDE), F32)], axis=0
    )


def kernel_gradient(cols, cot, out, grad):
    grad[0 : TAPS * C, :] = lax.dot_general(
        cols[...], cot[...], (((0,), (0,)), ((), ())), preferred_element_type=F32
    )
    row = lax.broadcasted_iota(jnp.int32, (48, C), 0)
    for core in range(2):

        @pl.when(lax.axis_index("core") == core)
        def _():
            for q in range(32):
                start = BLK * (2 * q + core)
                out[q] = jnp.where(row < BLK, grad[start : start + 48, :], 0.0)


def pack_blocks(blocks, small, other, out, extra):
    write_extras(extra, small[...] + other[...])

    def body(dest, carry):
        for pair in range(2):
            q = 4 * dest + 2 * pair
            packed = packed_pair(side_by_side(blocks[q], blocks[q + 1]), extra[pair])
            for k, tile in enumerate(tiles_of(pair)):
                out[dest, tile] = packed[:, 128 * k : 128 * k + 128]
        return carry

    lax.fori_loop(0, 8, body, 0)


def chip_sum(blocks, out):
    def pair_of(source, pair, rows):
        parts = [blocks[source, tile].astype(jnp.int32)[rows] for tile in tiles_of(pair)]
        return jnp.concatenate(parts, axis=1)

    tail_rows = slice(40, 48)
    small = jnp.zeros((8, WIDE), F32)
    for source in range(8):
        small = small + read_extras([pair_of(source, k, tail_rows) for k in range(2)])
    high, low, exps = split_small(small[:, 0:128])
    lane = lax.broadcasted_iota(jnp.int32, (1, 128), 1)
    tail = jnp.zeros((1, 128), F32)
    vectors = []
    for k, vector in enumerate(apart(small[0:1])):
        e = exponent(jnp.max(jnp.abs(vector), axis=1, keepdims=True))
        q = rounded(vector, e)
        q = jnp.concatenate([q, jnp.zeros((1, 64), F32)], axis=1)
        vectors += [q[:, 0:128], q[:, 128:256], q[:, 256:384]]
        tail = jnp.where(lane == k, e.astype(F32), tail)
    for k, part in enumerate((high, low, exps)):
        tail = jnp.where(lane == 2 + k, part[1:2], tail)

    def body(pair, carry):
        both = jnp.zeros((48, WIDE), F32)
        for source in range(8):
            both = both + unpacked_pair(pair_of(source, pair, slice(0, 48)))
        e = exponent(jnp.max(jnp.abs(both), axis=0, keepdims=True))
        values = apart(rounded(both, e))
        levels = apart(e.astype(F32))
        for k in range(2):
            for y in range(8):
                part = values[k][:, 40 * y : 40 * y + 40]
                tile = jnp.concatenate(
                    [part[0:16], part[16:32], part[32:48], jnp.zeros((16, 8), F32)], axis=1
                )
                ey = levels[k][:, 40 * y : 40 * y + 40]
                ey = jnp.concatenate([ey, ey, ey, jnp.zeros((1, 8), F32)], axis=1)
                full = jnp.concatenate([tile] + vectors + [ey, tail], axis=0)
                out[y, 2 * pair + k] = full.astype(jnp.int32).astype(I16)
        return carry

    lax.fori_loop(0, 2, body, 0)


def final_sum(blocks, loss, grad, gain, shift):
    y_at = lax.axis_index("y")
    weights = jnp.zeros((16, 128), F32)
    vectors = jnp.zeros((8, 128), F32)
    mine = jnp.zeros((1, 1), F32)
    row = lax.broadcasted_iota(jnp.int32, (8, 128), 0)
    for pair in range(8):
        part = jnp.zeros((16, 128), F32)
        vector = jnp.zeros((8, 128), F32)
        margin = jnp.zeros((1, 1), F32)
        for z in range(4):
            q = blocks[pair, z].astype(jnp.int32)
            v = q.astype(F32)
            tail = q[16:24]
            part = part + v[0:16] * pow2(tail[6:7] - 15)
            factor = pow2(tail[7:8] - 15)
            vector = vector + v[16:24] * jnp.where(row < 3, factor[:, 0:1], factor[:, 1:2])
            margin = margin + (v[23:24, 2:3] + v[23:24, 3:4] * (1.0 / 32768.0)) * factor[:, 4:5]
        margin = BETA * (margin / float(PIXELS * C))
        scale = BETA * jax.nn.sigmoid(margin) * (2.0 / (8 * C))
        weights = weights + scale * part
        vectors = vectors + scale * vector
        mine = jnp.where(y_at == pair, margin, mine)
    near = jnp.exp(-jnp.abs(mine))
    one = 1.0 + near
    log1p = jnp.where(one == 1.0, near, jnp.log(one) * near / jnp.where(one == 1.0, 1.0, one - 1.0))
    loss[...] = jnp.maximum(mine, 0.0) + log1p
    tall = jnp.concatenate([weights, jnp.roll(weights, -40, 1), jnp.roll(weights, -80, 1)], axis=0)
    tall = jnp.concatenate([tall, jnp.zeros((80, 128), F32)], axis=0)
    grad[...] = tall.T[0:40, 0:BLK]
    for out, k in ((gain, 0), (shift, 3)):
        pieces = [vectors[k : k + 1], vectors[k + 1 : k + 2], vectors[k + 2 : k + 3, 0:64]]
        out[...] = jnp.concatenate(pieces, axis=1).reshape(C)


def local(
    timesteps, features_win, features_lose, noise_win, noise_lose, conv_weight, ref_weight,
    norm_gain, norm_shift, ref_gain, ref_shift, time_weight,
):
    fw, fl = features_win[0], features_lose[0]
    strip = (2, TW, C)
    rows, columns = ("x", "zl"), ("zh", "core")
    up = [((i + 1) % 8, i) for i in range(8)]
    down = [(i, (i + 1) % 8) for i in range(8)]
    outward = [(i, (i + 1) % 8 if i % 2 else (i + 7) % 8) for i in range(8)]
    swap = [(0, 1), (1, 0)]

    first, last = call(
        edge_rows,
        [(strip, BF16), (strip, BF16)],
        [pltpu.SemaphoreType.DMA((4,))],
        far=(0, 1),
        grant=57,
    )(fw, fl)
    top = lax.ppermute(last, rows, down)
    bottom = lax.ppermute(first, rows, up)
    stats, edge, here = call(
        statistics,
        [((32, 128), F32), (strip, BF16), ((2, 2 * TH, TW, C), BF16)],
        [pltpu.SemaphoreType.DMA((4,))],
        flops=10**7,
        nbytes=10**6,
        far=range(4),
        grant=57,
    )(fw, fl, noise_win[0], noise_lose[0])
    stats = lax.all_to_all(stats, ("x", "zl", "zh"), 0, 0, tiled=True)
    (bias,) = call(
        time_bias,
        [((8, C), F32)],
        [pltpu.SMEM((1,), jnp.int32), pltpu.VMEM((C, C), F32), pltpu.SemaphoreType.DMA((2,))],
        flops=10**7,
        nbytes=10**6,
        far=(0, 1),
    )(timesteps, time_weight)
    (side,) = call(outer_column, [(strip, BF16)])(top, bottom, edge)
    side = lax.ppermute(side, columns, outward)
    totals, mine = call(
        sums_and_tile,
        [((8, 128), F32), ((2, 2 * TH + 3, TW, C), BF16)],
        flops=2 * 10**10,
        nbytes=10**6,
    )(stats, top, bottom, side, here)
    theirs = lax.ppermute(mine, "core", swap)

    cols, cot, small = call(
        forward,
        [((4 * PIX, TAPS * C), BF16), ((4 * PIX, C), BF16), ((8, WIDE), F32)],
        [
            pltpu.VMEM((4, TH + 2, 24, C), F32),
            pltpu.VMEM((TH + 2, 24, C), F32),
            pltpu.VMEM((2, TH + 2, 24, C), F32),
            pltpu.VMEM((2, TH + 2, 24, C), F32),
            pltpu.VMEM((2, TH + 2, TW, C), F32),
            pltpu.VMEM((TAPS, C, C), BF16),
            pltpu.VMEM((TAPS, C, C), BF16),
        ]
        + [pltpu.VMEM((C,), F32)] * 4
        + [pltpu.SemaphoreType.DMA((6,))],
        flops=2 * 10**9,
        nbytes=10**7,
        far=range(4, 10),
    )(
        totals, bias, mine, theirs, norm_gain, norm_shift, ref_gain, ref_shift,
        conv_weight, ref_weight,
    )
    other = lax.ppermute(small, "core", swap)
    block = (32, 48, C)
    (blocks,) = call(
        kernel_gradient,
        [(block, F32)],
        [pltpu.VMEM((TAPS * C + 8, C), F32)],
        flops=10**9,
        nbytes=10**7,
    )(cols, cot)
    (blocks,) = call(
        pack_blocks, [((8, 10, 48, 128), I16)], [pltpu.VMEM((2, 8, WIDE), F32)]
    )(blocks, small, other)
    blocks = lax.all_to_all(blocks, ("x", "zl"), 0, 0, tiled=True)
    (sums,) = call(chip_sum, [((8, 4, 24, 128), I16)])(blocks)
    sums = lax.all_to_all(sums.reshape(32, 24, 128), ("y", "zh"), 0, 0, tiled=True)
    loss, grad, gain, shift = call(
        final_sum, [((1, 1), F32), ((40, BLK), F32), ((C,), F32), ((C,), F32)]
    )(sums.reshape(8, 4, 24, 128))
    return loss.reshape(1), grad, gain, shift


def solution(mesh):
    fine = Mesh(mesh.devices.reshape(8, 4, 2, 4, 2), ("y", "x", "zl", "zh", "core"))
    image = P("y", ("x", "zl"), ("zh", "core"), None)
    return jax.shard_map(
        local,
        mesh=fine,
        in_specs=(P("y"), image, image, image, image) + (P(),) * 7,
        out_specs=(P("y"), P("y", ("x", "zl", "zh", "core")), P(), P()),
        check_vma=False,
    )
```

```python
import functools
import math

import jax
import jax.numpy as jnp
from jax import lax
from jax.experimental import pallas as pl
from jax.experimental.pallas import tpu as pltpu
from jax.sharding import Mesh
from jax.sharding import PartitionSpec as P

C = 320
GROUPS = 32
TAPS = 9
TH, TW = 8, 16
PIX = TH * TW
WIDE = 2 * C
BLK = 45
PIXELS = 64 * 128
BETA = 40.0
F32 = jnp.float32
BF16 = jnp.bfloat16
I16 = jnp.int16
HIGHEST = lax.Precision.HIGHEST


def call(kernel, outs, scratch=(), flops=0, nbytes=0, far=(), far_outs=(), grant=28):
    def run(*args):
        specs = [
            pl.BlockSpec(memory_space=pltpu.HBM if i in far else pltpu.VMEM) for i in range(len(args))
        ]
        return pl.pallas_call(
            kernel,
            out_shape=[jax.ShapeDtypeStruct(s, d) for s, d in outs],
            in_specs=specs,
            out_specs=[
                pl.BlockSpec(memory_space=pltpu.HBM if i in far_outs else pltpu.VMEM)
                for i in range(len(outs))
            ],
            scratch_shapes=list(scratch),
            compiler_params=pltpu.CompilerParams(vmem_limit_bytes=grant * 2**20),
            cost_estimate=pl.CostEstimate(flops=flops, bytes_accessed=nbytes, transcendentals=0),
        )(*args)

    return run


def pow2(n):
    size = jnp.abs(n)
    out = jnp.ones(n.shape, F32)
    for bit in range(7):
        step = jnp.where(n < 0, 0.5 ** (2**bit) if bit < 7 else 0.0, 2.0 ** (2**bit))
        out = out * jnp.where((size & (1 << bit)) != 0, step, 1.0)
    return out


def exponent(peak):
    level = jnp.log(jnp.maximum(peak, 1e-30)) * (1.0 / math.log(2.0))
    return jnp.clip(jnp.ceil(level + 0.01), -100.0, 100.0).astype(jnp.int32)


def rounded(values, exps):
    return jnp.round(values * pow2(15 - exps))


def split_small(small):
    exps = exponent(jnp.abs(small))
    scaled = small * pow2(15 - exps)
    high = jnp.round(scaled)
    low = jnp.round((scaled - high) * 32768.0)
    return high, low, exps.astype(F32)


def side_by_side(one, two):
    return jnp.concatenate([one[:, 0:256], two[:, 0:256], one[:, 256:C], two[:, 256:C]], axis=1)


def apart(both):
    one = jnp.concatenate([both[:, 0:256], both[:, 512:576]], axis=1)
    two = jnp.concatenate([both[:, 256:512], both[:, 576:640]], axis=1)
    return one, two


def write_extras(extra, small):
    high, low, exps = split_small(small)
    lane = lax.broadcasted_iota(jnp.int32, (1, WIDE), 1)
    extra[...] = jnp.zeros_like(extra)
    extra[0, 0:1] = high[0:1]
    extra[0, 1:2] = low[0:1]
    extra[1, 0:1] = exps[0:1]
    margin = jnp.where(lane == 1, low[1:2], exps[1:2])
    extra[1, 1:2] = jnp.where(lane == 0, high[1:2], margin)


def read_extras(tails):
    high, low, exps = tails[0][6:7], tails[0][7:8], tails[1][6:7]
    sums = (high.astype(F32) + low.astype(F32) * (1.0 / 32768.0)) * pow2(exps - 15)
    row = tails[1][7:8]
    value = row.astype(F32)
    margin = (value[:, 0:1] + value[:, 1:2] * (1.0 / 32768.0)) * pow2(row[:, 2:3] - 15)
    margin = jnp.broadcast_to(margin, (1, WIDE))
    return jnp.concatenate([sums, margin, jnp.zeros((6, WIDE), F32)], axis=0)


def packed_pair(pair, extra):
    exps = exponent(jnp.max(jnp.abs(pair), axis=0, keepdims=True))
    q = rounded(pair, exps)
    row = lax.broadcasted_iota(jnp.int32, (8, WIDE), 0)
    tail = jnp.where(row == 5, exps.astype(F32), q[40:48])
    tail = jnp.where(row == 6, extra[0:1], tail)
    tail = jnp.where(row == 7, extra[1:2], tail)
    q = jnp.concatenate([q[0:40], tail], axis=0)
    return q.astype(jnp.int32).astype(I16)


def unpacked_pair(q):
    v = q.astype(F32) * pow2(q[45:46] - 15)
    row = lax.broadcasted_iota(jnp.int32, (8, WIDE), 0)
    return jnp.concatenate([v[0:40], jnp.where(row < BLK - 40, v[40:48], 0.0)], axis=0)


def tiles_of(pair):
    return [4 * pair, 4 * pair + 1, 4 * pair + 2, 4 * pair + 3, 8 + pair]


def edge_rows(fw, fl, first, last, sems):
    copies = []
    for k, ref in enumerate((fw, fl)):
        copies.append(pltpu.make_async_copy(ref.at[0], first.at[k], sems.at[2 * k]))
        copies.append(pltpu.make_async_copy(ref.at[TH - 1], last.at[k], sems.at[2 * k + 1]))
    for copy in copies:
        copy.start()
    for copy in copies:
        copy.wait()


def statistics(fw, fl, nw, nl, stats, edge, here, near, sems):
    copies = [pltpu.make_async_copy(f, near.at[k], sems.at[k]) for k, f in enumerate((fw, fl))]
    for k, (f, n) in enumerate(((fw, nw), (fl, nl))):
        copies.append(
            pltpu.make_async_copy(f, here.at[k, pl.ds(0, TH)], sems.at[2 + 2 * k])
        )
        copies.append(
            pltpu.make_async_copy(n, here.at[k, pl.ds(TH, TH)], sems.at[3 + 2 * k])
        )
    for copy in copies:
        copy.start()
    copies[0].wait()
    copies[1].wait()
    total = jnp.zeros((8, 128), F32)
    rows = lax.broadcasted_iota(jnp.int32, (C, 128), 0)
    lanes = lax.broadcasted_iota(jnp.int32, (C, 128), 1)
    size = C // GROUPS
    for k in range(2):
        field = near[k].astype(F32)
        x = field.reshape(PIX, C)
        sums = jnp.sum(x, axis=0, keepdims=True)
        squares = jnp.sum(x * x, axis=0, keepdims=True)
        for j, part in enumerate((sums, squares)):
            group = lanes - GROUPS * (2 * k + j)
            member = (group >= 0) & (group < GROUPS)
            member = member & (rows >= group * size) & (rows < group * size + size)
            total = total + jnp.dot(
                jnp.broadcast_to(part, (8, C)),
                member.astype(F32),
                precision=HIGHEST,
                preferred_element_type=F32,
            )
        column = [
            jnp.concatenate([field[r, col : col + 1] for r in range(TH)], axis=0)
            for col in (0, TW - 1)
        ]
        column = jnp.where(lax.axis_index("core") == 0, column[0], column[1])
        edge[k] = jnp.concatenate([column, jnp.zeros((8, C), F32)], axis=0).astype(BF16)
    stats[...] = jnp.broadcast_to(total[0:1], stats.shape)
    for copy in copies[2:]:
        copy.wait()


def time_bias(step, time_weight, bias, number, table, sems):
    copies = [
        pltpu.make_async_copy(step, number, sems.at[0]),
        pltpu.make_async_copy(time_weight, table, sems.at[1]),
    ]
    for copy in copies:
        copy.start()
    half = C // 2
    lane = lax.broadcasted_iota(jnp.int32, (8, C), 1)
    place = jnp.where(lane < half, lane, lane - half).astype(F32)
    frequency = jnp.exp(-math.log(10000.0) * place / half)
    copies[0].wait()
    angles = number[0].astype(F32) * frequency
    sinusoid = jnp.where(lane < half, jnp.cos(angles), jnp.sin(angles))
    gate = sinusoid * jax.nn.sigmoid(sinusoid)
    copies[1].wait()
    bias[...] = jnp.dot(gate, table[...], precision=HIGHEST, preferred_element_type=F32)


def outer_column(top, bottom, edge, side):
    core = lax.axis_index("core")
    for s in range(2):
        above, below = top[s].astype(F32), bottom[s].astype(F32)
        above = jnp.where(core == 0, above[0:1], above[TW - 1 : TW])
        below = jnp.where(core == 0, below[0:1], below[TW - 1 : TW])
        column = [above, edge[s].astype(F32)[0:TH], below, jnp.zeros((6, C), F32)]
        side[s] = jnp.concatenate(column, axis=0).astype(BF16)


def sums_and_tile(stats, top, bottom, side, here, totals, tile):
    total = jnp.sum(stats[...], axis=0, keepdims=True)
    totals[...] = jnp.broadcast_to(total, (8, 128))
    high = total.astype(BF16).astype(F32)
    middle = (total - high).astype(BF16).astype(F32)
    low = total - high - middle
    parts = jnp.concatenate([high, middle, low, jnp.zeros((3, 128), F32)], axis=0)
    parts = jnp.concatenate([parts, jnp.zeros((6, C - 128), F32)], axis=1)
    column = side[0].astype(F32)[0 : TH + 2]
    tile[0, 2 * TH + 2] = jnp.concatenate([column, parts], axis=0).astype(BF16)
    tile[1, 2 * TH + 2] = side[1]
    for s in range(2):
        tile[s, 0] = top[s]
        tile[s, 1 : TH + 1] = here[s, 0:TH]
        tile[s, TH + 1] = bottom[s]
        tile[s, TH + 2 : 2 * TH + 2] = here[s, TH:]


def forward(
    totals, bias, mine, theirs, gain_far, shift_far, ref_gain_far, ref_shift_far,
    weight_far, ref_far, cols, cot_out, small, field, act, back, slope, shifted, weight, ref_weight, gain, shift,
    ref_gain, ref_shift, sems,
):
    pairs = [
        (ref_gain_far, ref_gain), (ref_shift_far, ref_shift), (gain_far, gain), (shift_far, shift),
        (ref_far, ref_weight), (weight_far, weight),
    ]
    copies = [pltpu.make_async_copy(a, b, sems.at[i]) for i, (a, b) in enumerate(pairs)]
    for copy in copies:
        copy.start()
    core = lax.axis_index("core")
    row_at = 2 * lax.axis_index("x") + lax.axis_index("zl")
    chip_at = 2 * lax.axis_index("zh")
    col_at = (chip_at + core, chip_at + 1 - core)

    parts = theirs[0, 2 * TH + 2].astype(F32)[TH + 2 : TH + 5, 0:128]
    total = totals[...] + ((parts[0:1] + parts[1:2]) + parts[2:3])
    groups = lax.broadcasted_iota(jnp.int32, (128, C), 0)
    chans = lax.broadcasted_iota(jnp.int32, (128, C), 1)
    size = C // GROUPS
    entries = float(PIXELS * size)

    def by_channel(k):
        group = groups - GROUPS * k
        member = (group >= 0) & (group < GROUPS)
        member = member & (chans >= group * size) & (chans < group * size + size)
        spread = jnp.dot(total, member.astype(F32), precision=HIGHEST, preferred_element_type=F32)
        return spread[0:1] / entries

    means, scales = [], []
    for s in range(2):
        mean, square = by_channel(2 * s), by_channel(2 * s + 1)
        means.append(mean)
        scales.append(lax.rsqrt(square - mean * mean + 1e-05))

    tiles = (mine, theirs)
    for w in range(2):
        for s in range(2):
            here, beside = tiles[w], tiles[1 - w]
            f = 2 * w + s
            field[f, :, TW + 2 :, :] = jnp.zeros((TH + 2, 22 - TW, C), F32)
            field[f, :, 1 : TW + 1, :] = (here[s, 0 : TH + 2].astype(F32) - means[s]) * scales[s]
            outer = (here[s, 2 * TH + 2].astype(F32) - means[s]) * scales[s]
            is_left = core == w
            for r in range(TH + 2):
                near = (beside[s, r].astype(F32) - means[s]) * scales[s]
                out = outer[r : r + 1]
                field[f, r, 0:1, :] = jnp.where(is_left, out, near[TW - 1 : TW])
                field[f, r, TW + 1 : TW + 2, :] = jnp.where(is_left, near[0:1], out)

    column = lax.broadcasted_iota(jnp.int32, (24, C), 0)
    inside = []
    for w in range(2):
        ok = (column < TW + 2) & ((column > 0) | (col_at[w] > 0))
        inside.append(ok & ((column < TW + 1) | (col_at[w] < 7)))

    def valid(w, r):
        if r == 0:
            return inside[w] & (row_at > 0)
        if r == TH + 1:
            return inside[w] & (row_at < 7)
        return inside[w]

    def columns_of(fields, g, b, slope=None):
        for f in fields:
            for r in range(TH + 2):
                pre = field[f, r] * g + b
                gate = jax.nn.sigmoid(pre)
                value = pre * gate
                act[r] = jnp.where(valid(f // 2, r), value, 0.0)
                if slope is not None and f < 2:
                    slope[f, r] = jnp.where(valid(0, r), gate + value * (1.0 - gate), 0.0)
                for c in range(3):
                    piece = act[r, c : c + TW, :].astype(BF16)
                    for a in range(3):
                        if 0 <= r - a < TH:
                            at, t = f * PIX + TW * (r - a), 3 * a + c
                            cols[at : at + TW, C * t : C * (t + 1)] = piece

    def base(f):
        tile, s = tiles[f // 2], f % 2
        noise = tile[s, TH + 2 : 2 * TH + 2].astype(F32)
        return (tile[s, 1 : TH + 1].astype(F32) - noise).reshape(PIX, C)

    def residual(fields, kernel):
        conv = jnp.dot(
            cols[0 : PIX * len(fields)],
            kernel[...].reshape(TAPS * C, C),
            preferred_element_type=F32,
        )
        return [base(f) + conv[PIX * f : PIX * (f + 1)] for f in fields]

    def signed_squares(resid):
        return jnp.sum(resid[0] * resid[0] - resid[1] * resid[1], axis=0, keepdims=True)

    time_row = bias[0:1]
    for copy in copies[0:4]:
        copy.wait()
    columns_of((0, 1), ref_gain[...].reshape(1, C), ref_shift[...].reshape(1, C) + time_row)
    copies[4].wait()
    resid = residual((0, 1), ref_weight)
    margin = -signed_squares(resid)
    g, b = gain[...].reshape(1, C), shift[...].reshape(1, C) + time_row
    columns_of((0, 1, 2, 3), g, b, slope)
    copies[5].wait()
    resid = residual((0, 1, 2, 3), weight)
    margin = margin + signed_squares(resid)
    for f in range(4):
        cot_out[PIX * f : PIX * (f + 1)] = (resid[f] if f % 2 == 0 else -resid[f]).astype(BF16)

    cot = cot_out[0 : 2 * PIX]
    back[...] = jnp.zeros_like(back)
    for c in range(3):
        shifted[...] = jnp.zeros_like(shifted)
        for a in range(3):
            term = lax.dot_general(
                cot, weight[3 * a + c], (((1,), (1,)), ((), ())), preferred_element_type=F32
            )
            for s in range(2):
                shifted[s, a : a + TH] += term[s * PIX : (s + 1) * PIX].reshape(TH, TW, C)
        back[:, :, c : c + TW, :] += shifted[...]
    gains = jnp.zeros((24, C), F32)
    shifts = jnp.zeros((24, C), F32)
    for s in range(2):
        for r in range(TH + 2):
            dpre = back[s, r] * slope[s, r]
            gains = gains + dpre * field[s, r]
            shifts = shifts + dpre
    gains = jnp.sum(gains, axis=0, keepdims=True)
    shifts = jnp.sum(shifts, axis=0, keepdims=True)
    margin = jnp.broadcast_to(jnp.sum(margin, axis=1, keepdims=True), (1, WIDE))
    small[...] = jnp.concatenate(
        [side_by_side(gains, shifts), margin, jnp.zeros((6, WIDE), F32)], axis=0
    )


def kernel_gradient(cols, cot, out, grad):
    grad[0 : TAPS * C, :] = lax.dot_general(
        cols[...], cot[...], (((0,), (0,)), ((), ())), preferred_element_type=F32
    )
    row = lax.broadcasted_iota(jnp.int32, (48, C), 0)
    for core in range(2):

        @pl.when(lax.axis_index("core") == core)
        def _():
            for q in range(32):
                start = BLK * (2 * q + core)
                out[q] = jnp.where(row < BLK, grad[start : start + 48, :], 0.0)


def pack_blocks(blocks, small, other, out, extra):
    write_extras(extra, small[...] + other[...])

    def body(dest, carry):
        for pair in range(2):
            q = 4 * dest + 2 * pair
            packed = packed_pair(side_by_side(blocks[q], blocks[q + 1]), extra[pair])
            for k, tile in enumerate(tiles_of(pair)):
                out[dest, tile] = packed[:, 128 * k : 128 * k + 128]
        return carry

    lax.fori_loop(0, 8, body, 0)


def chip_sum(blocks, out):
    def pair_of(source, pair, rows):
        parts = [blocks[source, tile].astype(jnp.int32)[rows] for tile in tiles_of(pair)]
        return jnp.concatenate(parts, axis=1)

    tail_rows = slice(40, 48)
    small = jnp.zeros((8, WIDE), F32)
    for source in range(8):
        small = small + read_extras([pair_of(source, k, tail_rows) for k in range(2)])
    high, low, exps = split_small(small[:, 0:128])
    lane = lax.broadcasted_iota(jnp.int32, (1, 128), 1)
    tail = jnp.zeros((1, 128), F32)
    vectors = []
    for k, vector in enumerate(apart(small[0:1])):
        e = exponent(jnp.max(jnp.abs(vector), axis=1, keepdims=True))
        q = rounded(vector, e)
        q = jnp.concatenate([q, jnp.zeros((1, 64), F32)], axis=1)
        vectors += [q[:, 0:128], q[:, 128:256], q[:, 256:384]]
        tail = jnp.where(lane == k, e.astype(F32), tail)
    for k, part in enumerate((high, low, exps)):
        tail = jnp.where(lane == 2 + k, part[1:2], tail)

    def body(pair, carry):
        both = jnp.zeros((48, WIDE), F32)
        for source in range(8):
            both = both + unpacked_pair(pair_of(source, pair, slice(0, 48)))
        e = exponent(jnp.max(jnp.abs(both), axis=0, keepdims=True))
        values = apart(rounded(both, e))
        levels = apart(e.astype(F32))
        for k in range(2):
            for y in range(8):
                part = values[k][:, 40 * y : 40 * y + 40]
                tile = jnp.concatenate(
                    [part[0:16], part[16:32], part[32:48], jnp.zeros((16, 8), F32)], axis=1
                )
                ey = levels[k][:, 40 * y : 40 * y + 40]
                ey = jnp.concatenate([ey, ey, ey, jnp.zeros((1, 8), F32)], axis=1)
                full = jnp.concatenate([tile] + vectors + [ey, tail], axis=0)
                out[y, 2 * pair + k] = full.astype(jnp.int32).astype(I16)
        return carry

    lax.fori_loop(0, 2, body, 0)


def final_sum(blocks, loss, grad, gain, shift):
    y_at = lax.axis_index("y")
    weights = jnp.zeros((16, 128), F32)
    vectors = jnp.zeros((8, 128), F32)
    mine = jnp.zeros((1, 1), F32)
    row = lax.broadcasted_iota(jnp.int32, (8, 128), 0)
    for pair in range(8):
        part = jnp.zeros((16, 128), F32)
        vector = jnp.zeros((8, 128), F32)
        margin = jnp.zeros((1, 1), F32)
        for z in range(4):
            q = blocks[pair, z].astype(jnp.int32)
            v = q.astype(F32)
            tail = q[16:24]
            part = part + v[0:16] * pow2(tail[6:7] - 15)
            factor = pow2(tail[7:8] - 15)
            vector = vector + v[16:24] * jnp.where(row < 3, factor[:, 0:1], factor[:, 1:2])
            margin = margin + (v[23:24, 2:3] + v[23:24, 3:4] * (1.0 / 32768.0)) * factor[:, 4:5]
        margin = BETA * (margin / float(PIXELS * C))
        scale = BETA * jax.nn.sigmoid(margin) * (2.0 / (8 * C))
        weights = weights + scale * part
        vectors = vectors + scale * vector
        mine = jnp.where(y_at == pair, margin, mine)
    near = jnp.exp(-jnp.abs(mine))
    one = 1.0 + near
    log1p = jnp.where(one == 1.0, near, jnp.log(one) * near / jnp.where(one == 1.0, 1.0, one - 1.0))
    loss[...] = jnp.maximum(mine, 0.0) + log1p
    tall = jnp.concatenate([weights, jnp.roll(weights, -40, 1), jnp.roll(weights, -80, 1)], axis=0)
    tall = jnp.concatenate([tall, jnp.zeros((80, 128), F32)], axis=0)
    grad[...] = tall.T[0:40, 0:BLK]
    for out, k in ((gain, 0), (shift, 3)):
        pieces = [vectors[k : k + 1], vectors[k + 1 : k + 2], vectors[k + 2 : k + 3, 0:64]]
        out[...] = jnp.concatenate(pieces, axis=1).reshape(C)


def local(
    timesteps, features_win, features_lose, noise_win, noise_lose, conv_weight, ref_weight,
    norm_gain, norm_shift, ref_gain, ref_shift, time_weight,
):
    fw, fl = features_win[0], features_lose[0]
    strip = (2, TW, C)
    rows, columns = ("x", "zl"), ("zh", "core")
    up = [((i + 1) % 8, i) for i in range(8)]
    down = [(i, (i + 1) % 8) for i in range(8)]
    outward = [(i, (i + 1) % 8 if i % 2 else (i + 7) % 8) for i in range(8)]
    swap = [(0, 1), (1, 0)]

    first, last = call(
        edge_rows,
        [(strip, BF16), (strip, BF16)],
        [pltpu.SemaphoreType.DMA((4,))],
        far=(0, 1),
        far_outs=(0, 1),
        grant=57,
    )(fw, fl)
    top = lax.ppermute(last, rows, down)
    bottom = lax.ppermute(first, rows, up)
    stats, edge, here = call(
        statistics,
        [((32, 128), F32), (strip, BF16), ((2, 2 * TH, TW, C), BF16)],
        [pltpu.VMEM((2, TH, TW, C), BF16), pltpu.SemaphoreType.DMA((6,))],
        flops=10**7,
        nbytes=10**6,
        far=range(4),
        far_outs=(2,),
        grant=57,
    )(fw, fl, noise_win[0], noise_lose[0])
    stats = lax.all_to_all(stats, ("x", "zl", "zh"), 0, 0, tiled=True)
    (bias,) = call(
        time_bias,
        [((8, C), F32)],
        [pltpu.SMEM((1,), jnp.int32), pltpu.VMEM((C, C), F32), pltpu.SemaphoreType.DMA((2,))],
        flops=10**7,
        nbytes=10**6,
        far=(0, 1),
    )(timesteps, time_weight)
    (side,) = call(outer_column, [(strip, BF16)])(top, bottom, edge)
    side = lax.ppermute(side, columns, outward)
    totals, mine = call(
        sums_and_tile,
        [((8, 128), F32), ((2, 2 * TH + 3, TW, C), BF16)],
        flops=2 * 10**10,
        nbytes=10**6,
    )(stats, top, bottom, side, here)
    theirs = lax.ppermute(mine, "core", swap)

    cols, cot, small = call(
        forward,
        [((4 * PIX, TAPS * C), BF16), ((4 * PIX, C), BF16), ((8, WIDE), F32)],
        [
            pltpu.VMEM((4, TH + 2, 24, C), F32),
            pltpu.VMEM((TH + 2, 24, C), F32),
            pltpu.VMEM((2, TH + 2, 24, C), F32),
            pltpu.VMEM((2, TH + 2, 24, C), F32),
            pltpu.VMEM((2, TH + 2, TW, C), F32),
            pltpu.VMEM((TAPS, C, C), BF16),
            pltpu.VMEM((TAPS, C, C), BF16),
        ]
        + [pltpu.VMEM((C,), F32)] * 4
        + [pltpu.SemaphoreType.DMA((6,))],
        flops=2 * 10**9,
        nbytes=10**7,
        far=range(4, 10),
    )(
        totals, bias, mine, theirs, norm_gain, norm_shift, ref_gain, ref_shift,
        conv_weight, ref_weight,
    )
    other = lax.ppermute(small, "core", swap)
    block = (32, 48, C)
    (blocks,) = call(
        kernel_gradient,
        [(block, F32)],
        [pltpu.VMEM((TAPS * C + 8, C), F32)],
        flops=10**9,
        nbytes=10**7,
    )(cols, cot)
    (blocks,) = call(
        pack_blocks, [((8, 10, 48, 128), I16)], [pltpu.VMEM((2, 8, WIDE), F32)]
    )(blocks, small, other)
    blocks = lax.all_to_all(blocks, ("x", "zl"), 0, 0, tiled=True)
    (sums,) = call(chip_sum, [((8, 4, 24, 128), I16)])(blocks)
    sums = lax.all_to_all(sums.reshape(32, 24, 128), ("y", "zh"), 0, 0, tiled=True)
    loss, grad, gain, shift = call(
        final_sum, [((1, 1), F32), ((40, BLK), F32), ((C,), F32), ((C,), F32)]
    )(sums.reshape(8, 4, 24, 128))
    return loss.reshape(1), grad, gain, shift


def solution(mesh):
    fine = Mesh(mesh.devices.reshape(8, 4, 2, 4, 2), ("y", "x", "zl", "zh", "core"))
    image = P("y", ("x", "zl"), ("zh", "core"), None)
    return jax.shard_map(
        local,
        mesh=fine,
        in_specs=(P("y"), image, image, image, image) + (P(),) * 7,
        out_specs=(P("y"), P("y", ("x", "zl", "zh", "core")), P(), P()),
        check_vma=False,
    )
```

```python
import functools
import math

import jax
import jax.numpy as jnp
from jax import lax
from jax.experimental import pallas as pl
from jax.experimental.pallas import tpu as pltpu
from jax.sharding import Mesh
from jax.sharding import PartitionSpec as P

C = 320
GROUPS = 32
TAPS = 9
TH, TW = 8, 16
PIX = TH * TW
WIDE = 2 * C
BLK = 45
PIXELS = 64 * 128
BETA = 40.0
F32 = jnp.float32
BF16 = jnp.bfloat16
I16 = jnp.int16
HIGHEST = lax.Precision.HIGHEST


def call(kernel, outs, scratch=(), flops=0, nbytes=0, far=(), grant=28):
    def run(*args):
        specs = [
            pl.BlockSpec(memory_space=pltpu.HBM if i in far else pltpu.VMEM) for i in range(len(args))
        ]
        return pl.pallas_call(
            kernel,
            out_shape=[jax.ShapeDtypeStruct(s, d) for s, d in outs],
            in_specs=specs,
            out_specs=[pl.BlockSpec(memory_space=pltpu.VMEM) for _ in outs],
            scratch_shapes=list(scratch),
            compiler_params=pltpu.CompilerParams(vmem_limit_bytes=grant * 2**20),
            cost_estimate=pl.CostEstimate(flops=flops, bytes_accessed=nbytes, transcendentals=0),
        )(*args)

    return run


def pow2(n):
    size = jnp.abs(n)
    out = jnp.ones(n.shape, F32)
    for bit in range(7):
        step = jnp.where(n < 0, 0.5 ** (2**bit) if bit < 7 else 0.0, 2.0 ** (2**bit))
        out = out * jnp.where((size & (1 << bit)) != 0, step, 1.0)
    return out


def exponent(peak):
    level = jnp.log(jnp.maximum(peak, 1e-30)) * (1.0 / math.log(2.0))
    return jnp.clip(jnp.ceil(level + 0.01), -100.0, 100.0).astype(jnp.int32)


def rounded(values, exps):
    return jnp.round(values * pow2(15 - exps))


def split_small(small):
    exps = exponent(jnp.abs(small))
    scaled = small * pow2(15 - exps)
    high = jnp.round(scaled)
    low = jnp.round((scaled - high) * 32768.0)
    return high, low, exps.astype(F32)


def side_by_side(one, two):
    return jnp.concatenate([one[:, 0:256], two[:, 0:256], one[:, 256:C], two[:, 256:C]], axis=1)


def apart(both):
    one = jnp.concatenate([both[:, 0:256], both[:, 512:576]], axis=1)
    two = jnp.concatenate([both[:, 256:512], both[:, 576:640]], axis=1)
    return one, two


def write_extras(extra, small):
    high, low, exps = split_small(small)
    lane = lax.broadcasted_iota(jnp.int32, (1, WIDE), 1)
    extra[...] = jnp.zeros_like(extra)
    extra[0, 0:1] = high[0:1]
    extra[0, 1:2] = low[0:1]
    extra[1, 0:1] = exps[0:1]
    margin = jnp.where(lane == 1, low[1:2], exps[1:2])
    extra[1, 1:2] = jnp.where(lane == 0, high[1:2], margin)


def read_extras(tails):
    high, low, exps = tails[0][6:7], tails[0][7:8], tails[1][6:7]
    sums = (high.astype(F32) + low.astype(F32) * (1.0 / 32768.0)) * pow2(exps - 15)
    row = tails[1][7:8]
    value = row.astype(F32)
    margin = (value[:, 0:1] + value[:, 1:2] * (1.0 / 32768.0)) * pow2(row[:, 2:3] - 15)
    margin = jnp.broadcast_to(margin, (1, WIDE))
    return jnp.concatenate([sums, margin, jnp.zeros((6, WIDE), F32)], axis=0)


def packed_pair(pair, extra):
    exps = exponent(jnp.max(jnp.abs(pair), axis=0, keepdims=True))
    q = rounded(pair, exps)
    row = lax.broadcasted_iota(jnp.int32, (8, WIDE), 0)
    tail = jnp.where(row == 5, exps.astype(F32), q[40:48])
    tail = jnp.where(row == 6, extra[0:1], tail)
    tail = jnp.where(row == 7, extra[1:2], tail)
    q = jnp.concatenate([q[0:40], tail], axis=0)
    return q.astype(jnp.int32).astype(I16)


def unpacked_pair(q):
    v = q.astype(F32) * pow2(q[45:46] - 15)
    row = lax.broadcasted_iota(jnp.int32, (8, WIDE), 0)
    return jnp.concatenate([v[0:40], jnp.where(row < BLK - 40, v[40:48], 0.0)], axis=0)


def tiles_of(pair):
    return [4 * pair, 4 * pair + 1, 4 * pair + 2, 4 * pair + 3, 8 + pair]


def edge_rows(fw, fl, first, last, sems):
    copies = []
    for k, ref in enumerate((fw, fl)):
        copies.append(pltpu.make_async_copy(ref.at[0], first.at[k], sems.at[2 * k]))
        copies.append(pltpu.make_async_copy(ref.at[TH - 1], last.at[k], sems.at[2 * k + 1]))
    for copy in copies:
        copy.start()
    for copy in copies:
        copy.wait()


def statistics(fw, fl, nw, nl, stats, edge, here, sems):
    copies = [
        pltpu.make_async_copy(fw, here.at[0, pl.ds(0, TH)], sems.at[0]),
        pltpu.make_async_copy(fl, here.at[1, pl.ds(0, TH)], sems.at[1]),
        pltpu.make_async_copy(nw, here.at[0, pl.ds(TH, TH)], sems.at[2]),
        pltpu.make_async_copy(nl, here.at[1, pl.ds(TH, TH)], sems.at[3]),
    ]
    for copy in copies:
        copy.start()
    copies[0].wait()
    copies[1].wait()
    total = jnp.zeros((8, 128), F32)
    rows = lax.broadcasted_iota(jnp.int32, (C, 128), 0)
    lanes = lax.broadcasted_iota(jnp.int32, (C, 128), 1)
    size = C // GROUPS
    for k in range(2):
        field = here[k, 0:TH].astype(F32)
        x = field.reshape(PIX, C)
        sums = jnp.sum(x, axis=0, keepdims=True)
        squares = jnp.sum(x * x, axis=0, keepdims=True)
        for j, part in enumerate((sums, squares)):
            group = lanes - GROUPS * (2 * k + j)
            member = (group >= 0) & (group < GROUPS)
            member = member & (rows >= group * size) & (rows < group * size + size)
            total = total + jnp.dot(
                jnp.broadcast_to(part, (8, C)),
                member.astype(F32),
                precision=HIGHEST,
                preferred_element_type=F32,
            )
        column = [
            jnp.concatenate([field[r, col : col + 1] for r in range(TH)], axis=0)
            for col in (0, TW - 1)
        ]
        column = jnp.where(lax.axis_index("core") == 0, column[0], column[1])
        edge[k] = jnp.concatenate([column, jnp.zeros((8, C), F32)], axis=0).astype(BF16)
    stats[...] = jnp.broadcast_to(total[0:1], stats.shape)
    copies[2].wait()
    copies[3].wait()


def time_bias(step, time_weight, bias, number, table, sems):
    copies = [
        pltpu.make_async_copy(step, number, sems.at[0]),
        pltpu.make_async_copy(time_weight, table, sems.at[1]),
    ]
    for copy in copies:
        copy.start()
    half = C // 2
    lane = lax.broadcasted_iota(jnp.int32, (8, C), 1)
    place = jnp.where(lane < half, lane, lane - half).astype(F32)
    frequency = jnp.exp(-math.log(10000.0) * place / half)
    copies[0].wait()
    angles = number[0].astype(F32) * frequency
    sinusoid = jnp.where(lane < half, jnp.cos(angles), jnp.sin(angles))
    gate = sinusoid * jax.nn.sigmoid(sinusoid)
    copies[1].wait()
    bias[...] = jnp.dot(gate, table[...], precision=HIGHEST, preferred_element_type=F32)


def outer_column(top, bottom, edge, side):
    core = lax.axis_index("core")
    for s in range(2):
        above, below = top[s].astype(F32), bottom[s].astype(F32)
        above = jnp.where(core == 0, above[0:1], above[TW - 1 : TW])
        below = jnp.where(core == 0, below[0:1], below[TW - 1 : TW])
        column = [above, edge[s].astype(F32)[0:TH], below, jnp.zeros((6, C), F32)]
        side[s] = jnp.concatenate(column, axis=0).astype(BF16)


def sums_and_tile(stats, top, bottom, side, here, totals, tile):
    total = jnp.sum(stats[...], axis=0, keepdims=True)
    totals[...] = jnp.broadcast_to(total, (8, 128))
    high = total.astype(BF16).astype(F32)
    middle = (total - high).astype(BF16).astype(F32)
    low = total - high - middle
    parts = jnp.concatenate([high, middle, low, jnp.zeros((3, 128), F32)], axis=0)
    parts = jnp.concatenate([parts, jnp.zeros((6, C - 128), F32)], axis=1)
    column = side[0].astype(F32)[0 : TH + 2]
    tile[0, 2 * TH + 2] = jnp.concatenate([column, parts], axis=0).astype(BF16)
    tile[1, 2 * TH + 2] = side[1]
    for s in range(2):
        tile[s, 0] = top[s]
        tile[s, 1 : TH + 1] = here[s, 0:TH]
        tile[s, TH + 1] = bottom[s]
        tile[s, TH + 2 : 2 * TH + 2] = here[s, TH:]


def forward(
    totals, bias, mine, theirs, gain_far, shift_far, ref_gain_far, ref_shift_far,
    weight_far, ref_far, cols, cot_out, small, field, act, back, slope, shifted, weight, ref_weight, gain, shift,
    ref_gain, ref_shift, sems,
):
    pairs = [
        (ref_gain_far, ref_gain), (ref_shift_far, ref_shift), (gain_far, gain), (shift_far, shift),
        (ref_far, ref_weight), (weight_far, weight),
    ]
    copies = [pltpu.make_async_copy(a, b, sems.at[i]) for i, (a, b) in enumerate(pairs)]
    for copy in copies:
        copy.start()
    core = lax.axis_index("core")
    row_at = 2 * lax.axis_index("x") + lax.axis_index("zl")
    chip_at = 2 * lax.axis_index("zh")
    col_at = (chip_at + core, chip_at + 1 - core)

    parts = theirs[0, 2 * TH + 2].astype(F32)[TH + 2 : TH + 5, 0:128]
    total = totals[...] + ((parts[0:1] + parts[1:2]) + parts[2:3])
    groups = lax.broadcasted_iota(jnp.int32, (128, C), 0)
    chans = lax.broadcasted_iota(jnp.int32, (128, C), 1)
    size = C // GROUPS
    entries = float(PIXELS * size)

    def by_channel(k):
        group = groups - GROUPS * k
        member = (group >= 0) & (group < GROUPS)
        member = member & (chans >= group * size) & (chans < group * size + size)
        spread = jnp.dot(total, member.astype(F32), precision=HIGHEST, preferred_element_type=F32)
        return spread[0:1] / entries

    means, scales = [], []
    for s in range(2):
        mean, square = by_channel(2 * s), by_channel(2 * s + 1)
        means.append(mean)
        scales.append(lax.rsqrt(square - mean * mean + 1e-05))

    tiles = (mine, theirs)
    for w in range(2):
        for s in range(2):
            here, beside = tiles[w], tiles[1 - w]
            f = 2 * w + s
            field[f, :, TW + 2 :, :] = jnp.zeros((TH + 2, 22 - TW, C), F32)
            field[f, :, 1 : TW + 1, :] = (here[s, 0 : TH + 2].astype(F32) - means[s]) * scales[s]
            outer = (here[s, 2 * TH + 2].astype(F32) - means[s]) * scales[s]
            is_left = core == w
            for r in range(TH + 2):
                near = (beside[s, r].astype(F32) - means[s]) * scales[s]
                out = outer[r : r + 1]
                field[f, r, 0:1, :] = jnp.where(is_left, out, near[TW - 1 : TW])
                field[f, r, TW + 1 : TW + 2, :] = jnp.where(is_left, near[0:1], out)

    column = lax.broadcasted_iota(jnp.int32, (24, C), 0)
    inside = []
    for w in range(2):
        ok = (column < TW + 2) & ((column > 0) | (col_at[w] > 0))
        inside.append(ok & ((column < TW + 1) | (col_at[w] < 7)))

    def valid(w, r):
        if r == 0:
            return inside[w] & (row_at > 0)
        if r == TH + 1:
            return inside[w] & (row_at < 7)
        return inside[w]

    def columns_of(fields, g, b, slope=None):
        for f in fields:
            for r in range(TH + 2):
                pre = field[f, r] * g + b
                gate = jax.nn.sigmoid(pre)
                value = pre * gate
                act[r] = jnp.where(valid(f // 2, r), value, 0.0)
                if slope is not None and f < 2:
                    slope[f, r] = jnp.where(valid(0, r), gate + value * (1.0 - gate), 0.0)
                for c in range(3):
                    piece = act[r, c : c + TW, :].astype(BF16)
                    for a in range(3):
                        if 0 <= r - a < TH:
                            at, t = f * PIX + TW * (r - a), 3 * a + c
                            cols[at : at + TW, C * t : C * (t + 1)] = piece

    def base(f):
        tile, s = tiles[f // 2], f % 2
        noise = tile[s, TH + 2 : 2 * TH + 2].astype(F32)
        return (tile[s, 1 : TH + 1].astype(F32) - noise).reshape(PIX, C)

    def residual(fields, kernel):
        conv = jnp.dot(
            cols[0 : PIX * len(fields)],
            kernel[...].reshape(TAPS * C, C),
            preferred_element_type=F32,
        )
        return [base(f) + conv[PIX * f : PIX * (f + 1)] for f in fields]

    def signed_squares(resid):
        return jnp.sum(resid[0] * resid[0] - resid[1] * resid[1], axis=0, keepdims=True)

    time_row = bias[0:1]
    for copy in copies[0:4]:
        copy.wait()
    columns_of((0, 1), ref_gain[...].reshape(1, C), ref_shift[...].reshape(1, C) + time_row)
    copies[4].wait()
    resid = residual((0, 1), ref_weight)
    margin = -signed_squares(resid)
    g, b = gain[...].reshape(1, C), shift[...].reshape(1, C) + time_row
    columns_of((0, 1, 2, 3), g, b, slope)
    copies[5].wait()
    resid = residual((0, 1, 2, 3), weight)
    margin = margin + signed_squares(resid)
    for f in range(4):
        cot_out[PIX * f : PIX * (f + 1)] = (resid[f] if f % 2 == 0 else -resid[f]).astype(BF16)

    cot = cot_out[0 : 2 * PIX]
    back[...] = jnp.zeros_like(back)
    for c in range(3):
        shifted[...] = jnp.zeros_like(shifted)
        for a in range(3):
            term = lax.dot_general(
                cot, weight[3 * a + c], (((1,), (1,)), ((), ())), preferred_element_type=F32
            )
            for s in range(2):
                shifted[s, a : a + TH] += term[s * PIX : (s + 1) * PIX].reshape(TH, TW, C)
        back[:, :, c : c + TW, :] += shifted[...]
    gains = jnp.zeros((24, C), F32)
    shifts = jnp.zeros((24, C), F32)
    for s in range(2):
        for r in range(TH + 2):
            dpre = back[s, r] * slope[s, r]
            gains = gains + dpre * field[s, r]
            shifts = shifts + dpre
    gains = jnp.sum(gains, axis=0, keepdims=True)
    shifts = jnp.sum(shifts, axis=0, keepdims=True)
    margin = jnp.broadcast_to(jnp.sum(margin, axis=1, keepdims=True), (1, WIDE))
    small[...] = jnp.concatenate(
        [side_by_side(gains, shifts), margin, jnp.zeros((6, WIDE), F32)], axis=0
    )


def kernel_gradient(cols, cot, out, grad):
    grad[0 : TAPS * C, :] = lax.dot_general(
        cols[...], cot[...], (((0,), (0,)), ((), ())), preferred_element_type=F32
    )
    row = lax.broadcasted_iota(jnp.int32, (48, C), 0)
    for core in range(2):

        @pl.when(lax.axis_index("core") == core)
        def _():
            for q in range(32):
                start = BLK * (2 * q + core)
                out[q] = jnp.where(row < BLK, grad[start : start + 48, :], 0.0)


def pack_blocks(blocks, small, other, out, extra):
    write_extras(extra, small[...] + other[...])

    def body(dest, carry):
        for pair in range(2):
            q = 4 * dest + 2 * pair
            packed = packed_pair(side_by_side(blocks[q], blocks[q + 1]), extra[pair])
            for k, tile in enumerate(tiles_of(pair)):
                out[dest, tile] = packed[:, 128 * k : 128 * k + 128]
        return carry

    lax.fori_loop(0, 8, body, 0)


def chip_sum(blocks, out):
    def pair_of(source, pair, rows):
        parts = [blocks[source, tile].astype(jnp.int32)[rows] for tile in tiles_of(pair)]
        return jnp.concatenate(parts, axis=1)

    tail_rows = slice(40, 48)
    small = jnp.zeros((8, WIDE), F32)
    for source in range(8):
        small = small + read_extras([pair_of(source, k, tail_rows) for k in range(2)])
    high, low, exps = split_small(small[:, 0:128])
    lane = lax.broadcasted_iota(jnp.int32, (1, 128), 1)
    tail = jnp.zeros((1, 128), F32)
    vectors = []
    for k, vector in enumerate(apart(small[0:1])):
        e = exponent(jnp.max(jnp.abs(vector), axis=1, keepdims=True))
        q = rounded(vector, e)
        q = jnp.concatenate([q, jnp.zeros((1, 64), F32)], axis=1)
        vectors += [q[:, 0:128], q[:, 128:256], q[:, 256:384]]
        tail = jnp.where(lane == k, e.astype(F32), tail)
    for k, part in enumerate((high, low, exps)):
        tail = jnp.where(lane == 2 + k, part[1:2], tail)

    def body(pair, carry):
        both = jnp.zeros((48, WIDE), F32)
        for source in range(8):
            both = both + unpacked_pair(pair_of(source, pair, slice(0, 48)))
        e = exponent(jnp.max(jnp.abs(both), axis=0, keepdims=True))
        values = apart(rounded(both, e))
        levels = apart(e.astype(F32))
        for k in range(2):
            for y in range(8):
                part = values[k][:, 40 * y : 40 * y + 40]
                tile = jnp.concatenate(
                    [part[0:16], part[16:32], part[32:48], jnp.zeros((16, 8), F32)], axis=1
                )
                ey = levels[k][:, 40 * y : 40 * y + 40]
                ey = jnp.concatenate([ey, ey, ey, jnp.zeros((1, 8), F32)], axis=1)
                full = jnp.concatenate([tile] + vectors + [ey, tail], axis=0)
                out[y, 2 * pair + k] = full.astype(jnp.int32).astype(I16)
        return carry

    lax.fori_loop(0, 2, body, 0)


def final_sum(blocks, loss, grad, gain, shift):
    y_at = lax.axis_index("y")
    weights = jnp.zeros((16, 128), F32)
    vectors = jnp.zeros((8, 128), F32)
    mine = jnp.zeros((1, 1), F32)
    row = lax.broadcasted_iota(jnp.int32, (8, 128), 0)
    for pair in range(8):
        part = jnp.zeros((16, 128), F32)
        vector = jnp.zeros((8, 128), F32)
        margin = jnp.zeros((1, 1), F32)
        for z in range(4):
            q = blocks[pair, z].astype(jnp.int32)
            v = q.astype(F32)
            tail = q[16:24]
            part = part + v[0:16] * pow2(tail[6:7] - 15)
            factor = pow2(tail[7:8] - 15)
            vector = vector + v[16:24] * jnp.where(row < 3, factor[:, 0:1], factor[:, 1:2])
            margin = margin + (v[23:24, 2:3] + v[23:24, 3:4] * (1.0 / 32768.0)) * factor[:, 4:5]
        margin = BETA * (margin / float(PIXELS * C))
        scale = BETA * jax.nn.sigmoid(margin) * (2.0 / (8 * C))
        weights = weights + scale * part
        vectors = vectors + scale * vector
        mine = jnp.where(y_at == pair, margin, mine)
    near = jnp.exp(-jnp.abs(mine))
    one = 1.0 + near
    log1p = jnp.where(one == 1.0, near, jnp.log(one) * near / jnp.where(one == 1.0, 1.0, one - 1.0))
    loss[...] = jnp.maximum(mine, 0.0) + log1p
    tall = jnp.concatenate([weights, jnp.roll(weights, -40, 1), jnp.roll(weights, -80, 1)], axis=0)
    tall = jnp.concatenate([tall, jnp.zeros((80, 128), F32)], axis=0)
    grad[...] = tall.T[0:40, 0:BLK]
    for out, k in ((gain, 0), (shift, 3)):
        pieces = [vectors[k : k + 1], vectors[k + 1 : k + 2], vectors[k + 2 : k + 3, 0:64]]
        out[...] = jnp.concatenate(pieces, axis=1).reshape(C)


def local(
    timesteps, features_win, features_lose, noise_win, noise_lose, conv_weight, ref_weight,
    norm_gain, norm_shift, ref_gain, ref_shift, time_weight,
):
    fw, fl = features_win[0], features_lose[0]
    strip = (2, TW, C)
    rows, columns = ("x", "zl"), ("zh", "core")
    up = [((i + 1) % 8, i) for i in range(8)]
    down = [(i, (i + 1) % 8) for i in range(8)]
    outward = [(i, (i + 1) % 8 if i % 2 else (i + 7) % 8) for i in range(8)]
    swap = [(0, 1), (1, 0)]

    first, last = call(
        edge_rows,
        [(strip, BF16), (strip, BF16)],
        [pltpu.SemaphoreType.DMA((4,))],
        far=(0, 1),
        grant=57,
    )(fw, fl)
    top = lax.ppermute(last, rows, down)
    bottom = lax.ppermute(first, rows, up)
    stats, edge, here = call(
        statistics,
        [((32, 128), F32), (strip, BF16), ((2, 2 * TH, TW, C), BF16)],
        [pltpu.SemaphoreType.DMA((4,))],
        flops=10**7,
        nbytes=10**6,
        far=range(4),
        grant=57,
    )(fw, fl, noise_win[0], noise_lose[0])
    stats = lax.all_to_all(stats, ("x", "zl", "zh"), 0, 0, tiled=True)
    (bias,) = call(
        time_bias,
        [((8, C), F32)],
        [pltpu.SMEM((1,), jnp.int32), pltpu.VMEM((C, C), F32), pltpu.SemaphoreType.DMA((2,))],
        flops=10**10,
        nbytes=10**6,
        far=(0, 1),
    )(timesteps, time_weight)
    (side,) = call(outer_column, [(strip, BF16)], flops=10**10, nbytes=10**6)(
        top, bottom, edge
    )
    side = lax.ppermute(side, columns, outward)
    totals, mine = call(
        sums_and_tile,
        [((8, 128), F32), ((2, 2 * TH + 3, TW, C), BF16)],
        flops=2 * 10**10,
        nbytes=10**6,
    )(stats, top, bottom, side, here)
    theirs = lax.ppermute(mine, "core", swap)

    cols, cot, small = call(
        forward,
        [((4 * PIX, TAPS * C), BF16), ((4 * PIX, C), BF16), ((8, WIDE), F32)],
        [
            pltpu.VMEM((4, TH + 2, 24, C), F32),
            pltpu.VMEM((TH + 2, 24, C), F32),
            pltpu.VMEM((2, TH + 2, 24, C), F32),
            pltpu.VMEM((2, TH + 2, 24, C), F32),
            pltpu.VMEM((2, TH + 2, TW, C), F32),
            pltpu.VMEM((TAPS, C, C), BF16),
            pltpu.VMEM((TAPS, C, C), BF16),
        ]
        + [pltpu.VMEM((C,), F32)] * 4
        + [pltpu.SemaphoreType.DMA((6,))],
        flops=2 * 10**9,
        nbytes=10**7,
        far=range(4, 10),
    )(
        totals, bias, mine, theirs, norm_gain, norm_shift, ref_gain, ref_shift,
        conv_weight, ref_weight,
    )
    other = lax.ppermute(small, "core", swap)
    block = (32, 48, C)
    (blocks,) = call(
        kernel_gradient,
        [(block, F32)],
        [pltpu.VMEM((TAPS * C + 8, C), F32)],
        flops=10**9,
        nbytes=10**7,
    )(cols, cot)
    (blocks,) = call(
        pack_blocks, [((8, 10, 48, 128), I16)], [pltpu.VMEM((2, 8, WIDE), F32)]
    )(blocks, small, other)
    blocks = lax.all_to_all(blocks, ("x", "zl"), 0, 0, tiled=True)
    (sums,) = call(chip_sum, [((8, 4, 24, 128), I16)])(blocks)
    sums = lax.all_to_all(sums.reshape(32, 24, 128), ("y", "zh"), 0, 0, tiled=True)
    loss, grad, gain, shift = call(
        final_sum, [((1, 1), F32), ((40, BLK), F32), ((C,), F32), ((C,), F32)]
    )(sums.reshape(8, 4, 24, 128))
    return loss.reshape(1), grad, gain, shift


def solution(mesh):
    fine = Mesh(mesh.devices.reshape(8, 4, 2, 4, 2), ("y", "x", "zl", "zh", "core"))
    image = P("y", ("x", "zl"), ("zh", "core"), None)
    return jax.shard_map(
        local,
        mesh=fine,
        in_specs=(P("y"), image, image, image, image) + (P(),) * 7,
        out_specs=(P("y"), P("y", ("x", "zl", "zh", "core")), P(), P()),
        check_vma=False,
    )
```

```python
import functools
import math

import jax
import jax.numpy as jnp
from jax import lax
from jax.experimental import pallas as pl
from jax.experimental.pallas import tpu as pltpu
from jax.sharding import Mesh
from jax.sharding import PartitionSpec as P

C = 320
GROUPS = 32
TAPS = 9
TH, TW = 8, 16
PIX = TH * TW
WIDE = 2 * C
BLK = 45
PIXELS = 64 * 128
BETA = 40.0
F32 = jnp.float32
BF16 = jnp.bfloat16
I16 = jnp.int16
HIGHEST = lax.Precision.HIGHEST


def call(kernel, outs, scratch=(), flops=0, nbytes=0, far=(), grant=28):
    def run(*args):
        specs = [
            pl.BlockSpec(memory_space=pltpu.HBM if i in far else pltpu.VMEM) for i in range(len(args))
        ]
        return pl.pallas_call(
            kernel,
            out_shape=[jax.ShapeDtypeStruct(s, d) for s, d in outs],
            in_specs=specs,
            out_specs=[pl.BlockSpec(memory_space=pltpu.VMEM) for _ in outs],
            scratch_shapes=list(scratch),
            compiler_params=pltpu.CompilerParams(vmem_limit_bytes=grant * 2**20),
            cost_estimate=pl.CostEstimate(flops=flops, bytes_accessed=nbytes, transcendentals=0),
        )(*args)

    return run


def pow2(n):
    size = jnp.abs(n)
    out = jnp.ones(n.shape, F32)
    for bit in range(7):
        step = jnp.where(n < 0, 0.5 ** (2**bit) if bit < 7 else 0.0, 2.0 ** (2**bit))
        out = out * jnp.where((size & (1 << bit)) != 0, step, 1.0)
    return out


def exponent(peak):
    level = jnp.log(jnp.maximum(peak, 1e-30)) * (1.0 / math.log(2.0))
    return jnp.clip(jnp.ceil(level + 0.01), -100.0, 100.0).astype(jnp.int32)


def rounded(values, exps):
    return jnp.round(values * pow2(15 - exps))


def split_small(small):
    exps = exponent(jnp.abs(small))
    scaled = small * pow2(15 - exps)
    high = jnp.round(scaled)
    low = jnp.round((scaled - high) * 32768.0)
    return high, low, exps.astype(F32)


def side_by_side(one, two):
    return jnp.concatenate([one[:, 0:256], two[:, 0:256], one[:, 256:C], two[:, 256:C]], axis=1)


def apart(both):
    one = jnp.concatenate([both[:, 0:256], both[:, 512:576]], axis=1)
    two = jnp.concatenate([both[:, 256:512], both[:, 576:640]], axis=1)
    return one, two


def write_extras(extra, small):
    high, low, exps = split_small(small)
    lane = lax.broadcasted_iota(jnp.int32, (1, WIDE), 1)
    extra[...] = jnp.zeros_like(extra)
    extra[0, 0:1] = high[0:1]
    extra[0, 1:2] = low[0:1]
    extra[1, 0:1] = exps[0:1]
    margin = jnp.where(lane == 1, low[1:2], exps[1:2])
    extra[1, 1:2] = jnp.where(lane == 0, high[1:2], margin)


def read_extras(tails):
    high, low, exps = tails[0][6:7], tails[0][7:8], tails[1][6:7]
    sums = (high.astype(F32) + low.astype(F32) * (1.0 / 32768.0)) * pow2(exps - 15)
    row = tails[1][7:8]
    value = row.astype(F32)
    margin = (value[:, 0:1] + value[:, 1:2] * (1.0 / 32768.0)) * pow2(row[:, 2:3] - 15)
    margin = jnp.broadcast_to(margin, (1, WIDE))
    return jnp.concatenate([sums, margin, jnp.zeros((6, WIDE), F32)], axis=0)


def packed_pair(pair, extra):
    exps = exponent(jnp.max(jnp.abs(pair), axis=0, keepdims=True))
    q = rounded(pair, exps)
    row = lax.broadcasted_iota(jnp.int32, (8, WIDE), 0)
    tail = jnp.where(row == 5, exps.astype(F32), q[40:48])
    tail = jnp.where(row == 6, extra[0:1], tail)
    tail = jnp.where(row == 7, extra[1:2], tail)
    q = jnp.concatenate([q[0:40], tail], axis=0)
    return q.astype(jnp.int32).astype(I16)


def unpacked_pair(q):
    v = q.astype(F32) * pow2(q[45:46] - 15)
    row = lax.broadcasted_iota(jnp.int32, (8, WIDE), 0)
    return jnp.concatenate([v[0:40], jnp.where(row < BLK - 40, v[40:48], 0.0)], axis=0)


def tiles_of(pair):
    return [4 * pair, 4 * pair + 1, 4 * pair + 2, 4 * pair + 3, 8 + pair]


def edge_rows(fw, fl, first, last, sems):
    copies = []
    for k, ref in enumerate((fw, fl)):
        copies.append(pltpu.make_async_copy(ref.at[0], first.at[k], sems.at[2 * k]))
        copies.append(pltpu.make_async_copy(ref.at[TH - 1], last.at[k], sems.at[2 * k + 1]))
    for copy in copies:
        copy.start()
    for copy in copies:
        copy.wait()


def statistics(fw, fl, nw, nl, stats, edge, here, sems):
    copies = [
        pltpu.make_async_copy(fw, here.at[0, pl.ds(0, TH)], sems.at[0]),
        pltpu.make_async_copy(fl, here.at[1, pl.ds(0, TH)], sems.at[1]),
        pltpu.make_async_copy(nw, here.at[0, pl.ds(TH, TH)], sems.at[2]),
        pltpu.make_async_copy(nl, here.at[1, pl.ds(TH, TH)], sems.at[3]),
    ]
    for copy in copies:
        copy.start()
    copies[0].wait()
    copies[1].wait()
    total = jnp.zeros((8, 128), F32)
    rows = lax.broadcasted_iota(jnp.int32, (C, 128), 0)
    lanes = lax.broadcasted_iota(jnp.int32, (C, 128), 1)
    size = C // GROUPS
    for k in range(2):
        field = here[k, 0:TH].astype(F32)
        x = field.reshape(PIX, C)
        sums = jnp.sum(x, axis=0, keepdims=True)
        squares = jnp.sum(x * x, axis=0, keepdims=True)
        for j, part in enumerate((sums, squares)):
            group = lanes - GROUPS * (2 * k + j)
            member = (group >= 0) & (group < GROUPS)
            member = member & (rows >= group * size) & (rows < group * size + size)
            total = total + jnp.dot(
                jnp.broadcast_to(part, (8, C)),
                member.astype(F32),
                precision=HIGHEST,
                preferred_element_type=F32,
            )
        column = [
            jnp.concatenate([field[r, col : col + 1] for r in range(TH)], axis=0)
            for col in (0, TW - 1)
        ]
        column = jnp.where(lax.axis_index("core") == 0, column[0], column[1])
        edge[k] = jnp.concatenate([column, jnp.zeros((8, C), F32)], axis=0).astype(BF16)
    stats[...] = jnp.broadcast_to(total[0:1], stats.shape)
    copies[2].wait()
    copies[3].wait()


def time_bias(step, time_weight, bias, number, table, sems):
    copies = [
        pltpu.make_async_copy(step, number, sems.at[0]),
        pltpu.make_async_copy(time_weight, table, sems.at[1]),
    ]
    for copy in copies:
        copy.start()
    half = C // 2
    lane = lax.broadcasted_iota(jnp.int32, (8, C), 1)
    place = jnp.where(lane < half, lane, lane - half).astype(F32)
    frequency = jnp.exp(-math.log(10000.0) * place / half)
    copies[0].wait()
    angles = number[0].astype(F32) * frequency
    sinusoid = jnp.where(lane < half, jnp.cos(angles), jnp.sin(angles))
    gate = sinusoid * jax.nn.sigmoid(sinusoid)
    copies[1].wait()
    bias[...] = jnp.dot(gate, table[...], precision=HIGHEST, preferred_element_type=F32)


def outer_column(top, bottom, edge, side):
    core = lax.axis_index("core")
    for s in range(2):
        above, below = top[s].astype(F32), bottom[s].astype(F32)
        above = jnp.where(core == 0, above[0:1], above[TW - 1 : TW])
        below = jnp.where(core == 0, below[0:1], below[TW - 1 : TW])
        column = [above, edge[s].astype(F32)[0:TH], below, jnp.zeros((6, C), F32)]
        side[s] = jnp.concatenate(column, axis=0).astype(BF16)


def sums_and_tile(stats, top, bottom, side, here, totals, tile):
    total = jnp.sum(stats[...], axis=0, keepdims=True)
    totals[...] = jnp.broadcast_to(total, (8, 128))
    high = total.astype(BF16).astype(F32)
    middle = (total - high).astype(BF16).astype(F32)
    low = total - high - middle
    parts = jnp.concatenate([high, middle, low, jnp.zeros((3, 128), F32)], axis=0)
    parts = jnp.concatenate([parts, jnp.zeros((6, C - 128), F32)], axis=1)
    column = side[0].astype(F32)[0 : TH + 2]
    tile[0, 2 * TH + 2] = jnp.concatenate([column, parts], axis=0).astype(BF16)
    tile[1, 2 * TH + 2] = side[1]
    for s in range(2):
        tile[s, 0] = top[s]
        tile[s, 1 : TH + 1] = here[s, 0:TH]
        tile[s, TH + 1] = bottom[s]
        tile[s, TH + 2 : 2 * TH + 2] = here[s, TH:]


def forward(
    totals, bias, mine, theirs, gain_far, shift_far, ref_gain_far, ref_shift_far,
    weight_far, ref_far, cols, cot_out, small, field, act, back, slope, shifted, weight, ref_weight, gain, shift,
    ref_gain, ref_shift, sems,
):
    pairs = [
        (ref_gain_far, ref_gain), (ref_shift_far, ref_shift), (gain_far, gain), (shift_far, shift),
        (ref_far, ref_weight), (weight_far, weight),
    ]
    copies = [pltpu.make_async_copy(a, b, sems.at[i]) for i, (a, b) in enumerate(pairs)]
    for copy in copies:
        copy.start()
    core = lax.axis_index("core")
    row_at = 2 * lax.axis_index("x") + lax.axis_index("zl")
    chip_at = 2 * lax.axis_index("zh")
    col_at = (chip_at + core, chip_at + 1 - core)

    parts = theirs[0, 2 * TH + 2].astype(F32)[TH + 2 : TH + 5, 0:128]
    total = totals[...] + ((parts[0:1] + parts[1:2]) + parts[2:3])
    groups = lax.broadcasted_iota(jnp.int32, (128, C), 0)
    chans = lax.broadcasted_iota(jnp.int32, (128, C), 1)
    size = C // GROUPS
    entries = float(PIXELS * size)

    def by_channel(k):
        group = groups - GROUPS * k
        member = (group >= 0) & (group < GROUPS)
        member = member & (chans >= group * size) & (chans < group * size + size)
        spread = jnp.dot(total, member.astype(F32), precision=HIGHEST, preferred_element_type=F32)
        return spread[0:1] / entries

    means, scales = [], []
    for s in range(2):
        mean, square = by_channel(2 * s), by_channel(2 * s + 1)
        means.append(mean)
        scales.append(lax.rsqrt(square - mean * mean + 1e-05))

    tiles = (mine, theirs)
    for w in range(2):
        for s in range(2):
            here, beside = tiles[w], tiles[1 - w]
            f = 2 * w + s
            field[f, :, TW + 2 :, :] = jnp.zeros((TH + 2, 22 - TW, C), F32)
            field[f, :, 1 : TW + 1, :] = (here[s, 0 : TH + 2].astype(F32) - means[s]) * scales[s]
            outer = (here[s, 2 * TH + 2].astype(F32) - means[s]) * scales[s]
            is_left = core == w
            for r in range(TH + 2):
                near = (beside[s, r].astype(F32) - means[s]) * scales[s]
                out = outer[r : r + 1]
                field[f, r, 0:1, :] = jnp.where(is_left, out, near[TW - 1 : TW])
                field[f, r, TW + 1 : TW + 2, :] = jnp.where(is_left, near[0:1], out)

    column = lax.broadcasted_iota(jnp.int32, (24, C), 0)
    inside = []
    for w in range(2):
        ok = (column < TW + 2) & ((column > 0) | (col_at[w] > 0))
        inside.append(ok & ((column < TW + 1) | (col_at[w] < 7)))

    def valid(w, r):
        if r == 0:
            return inside[w] & (row_at > 0)
        if r == TH + 1:
            return inside[w] & (row_at < 7)
        return inside[w]

    def columns_of(fields, g, b, slope=None):
        for f in fields:
            for r in range(TH + 2):
                pre = field[f, r] * g + b
                gate = jax.nn.sigmoid(pre)
                value = pre * gate
                act[r] = jnp.where(valid(f // 2, r), value, 0.0)
                if slope is not None and f < 2:
                    slope[f, r] = jnp.where(valid(0, r), gate + value * (1.0 - gate), 0.0)
                for c in range(3):
                    piece = act[r, c : c + TW, :].astype(BF16)
                    for a in range(3):
                        if 0 <= r - a < TH:
                            at, t = f * PIX + TW * (r - a), 3 * a + c
                            cols[at : at + TW, C * t : C * (t + 1)] = piece

    def base(f):
        tile, s = tiles[f // 2], f % 2
        noise = tile[s, TH + 2 : 2 * TH + 2].astype(F32)
        return (tile[s, 1 : TH + 1].astype(F32) - noise).reshape(PIX, C)

    def residual(fields, kernel):
        conv = jnp.dot(
            cols[0 : PIX * len(fields)],
            kernel[...].reshape(TAPS * C, C),
            preferred_element_type=F32,
        )
        return [base(f) + conv[PIX * f : PIX * (f + 1)] for f in fields]

    def signed_squares(resid):
        return jnp.sum(resid[0] * resid[0] - resid[1] * resid[1], axis=0, keepdims=True)

    time_row = bias[0:1]
    for copy in copies[0:4]:
        copy.wait()
    columns_of((0, 1), ref_gain[...].reshape(1, C), ref_shift[...].reshape(1, C) + time_row)
    copies[4].wait()
    resid = residual((0, 1), ref_weight)
    margin = -signed_squares(resid)
    g, b = gain[...].reshape(1, C), shift[...].reshape(1, C) + time_row
    columns_of((0, 1, 2, 3), g, b, slope)
    copies[5].wait()
    resid = residual((0, 1, 2, 3), weight)
    margin = margin + signed_squares(resid)
    for f in range(4):
        cot_out[PIX * f : PIX * (f + 1)] = (resid[f] if f % 2 == 0 else -resid[f]).astype(BF16)

    cot = cot_out[0 : 2 * PIX]
    back[...] = jnp.zeros_like(back)
    terms = lax.dot_general(
        cot, weight[...].reshape(TAPS * C, C), (((1,), (1,)), ((), ())), preferred_element_type=F32
    )
    for c in range(3):
        for a in range(3):
            term = terms[:, C * (3 * a + c) : C * (3 * a + c + 1)]
            for s in range(2):
                part = term[s * PIX : (s + 1) * PIX].reshape(TH, TW, C)
                if a == 0:
                    shifted[s, 0:TH] = part
                    shifted[s, TH:] = jnp.zeros((2, TW, C), F32)
                else:
                    shifted[s, a : a + TH] += part
        back[:, :, c : c + TW, :] += shifted[...]
    gains = jnp.zeros((24, C), F32)
    shifts = jnp.zeros((24, C), F32)
    for s in range(2):
        for r in range(TH + 2):
            dpre = back[s, r] * slope[s, r]
            gains = gains + dpre * field[s, r]
            shifts = shifts + dpre
    gains = jnp.sum(gains, axis=0, keepdims=True)
    shifts = jnp.sum(shifts, axis=0, keepdims=True)
    margin = jnp.broadcast_to(jnp.sum(margin, axis=1, keepdims=True), (1, WIDE))
    small[...] = jnp.concatenate(
        [side_by_side(gains, shifts), margin, jnp.zeros((6, WIDE), F32)], axis=0
    )


def kernel_gradient(cols, cot, out, grad):
    grad[0 : TAPS * C, :] = lax.dot_general(
        cols[...], cot[...], (((0,), (0,)), ((), ())), preferred_element_type=F32
    )
    row = lax.broadcasted_iota(jnp.int32, (48, C), 0)
    for core in range(2):

        @pl.when(lax.axis_index("core") == core)
        def _():
            for q in range(32):
                start = BLK * (2 * q + core)
                out[q] = jnp.where(row < BLK, grad[start : start + 48, :], 0.0)


def pack_blocks(blocks, small, other, out, extra):
    write_extras(extra, small[...] + other[...])

    def body(dest, carry):
        for pair in range(2):
            q = 4 * dest + 2 * pair
            packed = packed_pair(side_by_side(blocks[q], blocks[q + 1]), extra[pair])
            for k, tile in enumerate(tiles_of(pair)):
                out[dest, tile] = packed[:, 128 * k : 128 * k + 128]
        return carry

    lax.fori_loop(0, 8, body, 0)


def chip_sum(blocks, out):
    def pair_of(source, pair, rows):
        parts = [blocks[source, tile].astype(jnp.int32)[rows] for tile in tiles_of(pair)]
        return jnp.concatenate(parts, axis=1)

    tail_rows = slice(40, 48)
    small = jnp.zeros((8, WIDE), F32)
    for source in range(8):
        small = small + read_extras([pair_of(source, k, tail_rows) for k in range(2)])
    high, low, exps = split_small(small[:, 0:128])
    lane = lax.broadcasted_iota(jnp.int32, (1, 128), 1)
    tail = jnp.zeros((1, 128), F32)
    vectors = []
    for k, vector in enumerate(apart(small[0:1])):
        e = exponent(jnp.max(jnp.abs(vector), axis=1, keepdims=True))
        q = rounded(vector, e)
        q = jnp.concatenate([q, jnp.zeros((1, 64), F32)], axis=1)
        vectors += [q[:, 0:128], q[:, 128:256], q[:, 256:384]]
        tail = jnp.where(lane == k, e.astype(F32), tail)
    for k, part in enumerate((high, low, exps)):
        tail = jnp.where(lane == 2 + k, part[1:2], tail)

    for pair in range(2):
        both = jnp.zeros((48, WIDE), F32)
        for source in range(8):
            both = both + unpacked_pair(pair_of(source, pair, slice(0, 48)))
        e = exponent(jnp.max(jnp.abs(both), axis=0, keepdims=True))
        values = apart(rounded(both, e))
        levels = apart(e.astype(F32))
        for k in range(2):
            for y in range(8):
                part = values[k][:, 40 * y : 40 * y + 40]
                tile = jnp.concatenate(
                    [part[0:16], part[16:32], part[32:48], jnp.zeros((16, 8), F32)], axis=1
                )
                ey = levels[k][:, 40 * y : 40 * y + 40]
                ey = jnp.concatenate([ey, ey, ey, jnp.zeros((1, 8), F32)], axis=1)
                full = jnp.concatenate([tile] + vectors + [ey, tail], axis=0)
                out[y, 2 * pair + k] = full.astype(jnp.int32).astype(I16)


def final_sum(blocks, loss, grad, gain, shift):
    y_at = lax.axis_index("y")
    weights = jnp.zeros((16, 128), F32)
    vectors = jnp.zeros((8, 128), F32)
    mine = jnp.zeros((1, 1), F32)
    row = lax.broadcasted_iota(jnp.int32, (8, 128), 0)
    for pair in range(8):
        part = jnp.zeros((16, 128), F32)
        vector = jnp.zeros((8, 128), F32)
        margin = jnp.zeros((1, 1), F32)
        for z in range(4):
            q = blocks[pair, z].astype(jnp.int32)
            v = q.astype(F32)
            tail = q[16:24]
            part = part + v[0:16] * pow2(tail[6:7] - 15)
            factor = pow2(tail[7:8] - 15)
            vector = vector + v[16:24] * jnp.where(row < 3, factor[:, 0:1], factor[:, 1:2])
            margin = margin + (v[23:24, 2:3] + v[23:24, 3:4] * (1.0 / 32768.0)) * factor[:, 4:5]
        margin = BETA * (margin / float(PIXELS * C))
        scale = BETA * jax.nn.sigmoid(margin) * (2.0 / (8 * C))
        weights = weights + scale * part
        vectors = vectors + scale * vector
        mine = jnp.where(y_at == pair, margin, mine)
    near = jnp.exp(-jnp.abs(mine))
    one = 1.0 + near
    log1p = jnp.where(one == 1.0, near, jnp.log(one) * near / jnp.where(one == 1.0, 1.0, one - 1.0))
    loss[...] = jnp.maximum(mine, 0.0) + log1p
    tall = jnp.concatenate([weights, jnp.roll(weights, -40, 1), jnp.roll(weights, -80, 1)], axis=0)
    tall = jnp.concatenate([tall, jnp.zeros((80, 128), F32)], axis=0)
    grad[...] = tall.T[0:40, 0:BLK]
    for out, k in ((gain, 0), (shift, 3)):
        pieces = [vectors[k : k + 1], vectors[k + 1 : k + 2], vectors[k + 2 : k + 3, 0:64]]
        out[...] = jnp.concatenate(pieces, axis=1).reshape(C)


def local(
    timesteps, features_win, features_lose, noise_win, noise_lose, conv_weight, ref_weight,
    norm_gain, norm_shift, ref_gain, ref_shift, time_weight,
):
    fw, fl = features_win[0], features_lose[0]
    strip = (2, TW, C)
    rows, columns = ("x", "zl"), ("zh", "core")
    up = [((i + 1) % 8, i) for i in range(8)]
    down = [(i, (i + 1) % 8) for i in range(8)]
    outward = [(i, (i + 1) % 8 if i % 2 else (i + 7) % 8) for i in range(8)]
    swap = [(0, 1), (1, 0)]

    first, last = call(
        edge_rows,
        [(strip, BF16), (strip, BF16)],
        [pltpu.SemaphoreType.DMA((4,))],
        far=(0, 1),
        grant=57,
    )(fw, fl)
    top = lax.ppermute(last, rows, down)
    bottom = lax.ppermute(first, rows, up)
    stats, edge, here = call(
        statistics,
        [((32, 128), F32), (strip, BF16), ((2, 2 * TH, TW, C), BF16)],
        [pltpu.SemaphoreType.DMA((4,))],
        flops=10**7,
        nbytes=10**6,
        far=range(4),
        grant=57,
    )(fw, fl, noise_win[0], noise_lose[0])
    stats = lax.all_to_all(stats, ("x", "zl", "zh"), 0, 0, tiled=True)
    (bias,) = call(
        time_bias,
        [((8, C), F32)],
        [pltpu.SMEM((1,), jnp.int32), pltpu.VMEM((C, C), F32), pltpu.SemaphoreType.DMA((2,))],
        flops=10**10,
        nbytes=10**6,
        far=(0, 1),
    )(timesteps, time_weight)
    (side,) = call(outer_column, [(strip, BF16)], flops=10**10, nbytes=10**6)(
        top, bottom, edge
    )
    side = lax.ppermute(side, columns, outward)
    totals, mine = call(
        sums_and_tile,
        [((8, 128), F32), ((2, 2 * TH + 3, TW, C), BF16)],
        flops=2 * 10**10,
        nbytes=10**6,
    )(stats, top, bottom, side, here)
    theirs = lax.ppermute(mine, "core", swap)

    cols, cot, small = call(
        forward,
        [((4 * PIX, TAPS * C), BF16), ((4 * PIX, C), BF16), ((8, WIDE), F32)],
        [
            pltpu.VMEM((4, TH + 2, 24, C), F32),
            pltpu.VMEM((TH + 2, 24, C), F32),
            pltpu.VMEM((2, TH + 2, 24, C), F32),
            pltpu.VMEM((2, TH + 2, 24, C), F32),
            pltpu.VMEM((2, TH + 2, TW, C), F32),
            pltpu.VMEM((TAPS, C, C), BF16),
            pltpu.VMEM((TAPS, C, C), BF16),
        ]
        + [pltpu.VMEM((C,), F32)] * 4
        + [pltpu.SemaphoreType.DMA((6,))],
        flops=2 * 10**9,
        nbytes=10**7,
        far=range(4, 10),
    )(
        totals, bias, mine, theirs, norm_gain, norm_shift, ref_gain, ref_shift,
        conv_weight, ref_weight,
    )
    other = lax.ppermute(small, "core", swap)
    block = (32, 48, C)
    (blocks,) = call(
        kernel_gradient,
        [(block, F32)],
        [pltpu.VMEM((TAPS * C + 8, C), F32)],
        flops=10**9,
        nbytes=10**7,
    )(cols, cot)
    (blocks,) = call(
        pack_blocks, [((8, 10, 48, 128), I16)], [pltpu.VMEM((2, 8, WIDE), F32)]
    )(blocks, small, other)
    blocks = lax.all_to_all(blocks, ("x", "zl"), 0, 0, tiled=True)
    (sums,) = call(chip_sum, [((8, 4, 24, 128), I16)])(blocks)
    sums = lax.all_to_all(sums.reshape(32, 24, 128), ("y", "zh"), 0, 0, tiled=True)
    loss, grad, gain, shift = call(
        final_sum, [((1, 1), F32), ((40, BLK), F32), ((C,), F32), ((C,), F32)]
    )(sums.reshape(8, 4, 24, 128))
    return loss.reshape(1), grad, gain, shift


def solution(mesh):
    fine = Mesh(mesh.devices.reshape(8, 4, 2, 4, 2), ("y", "x", "zl", "zh", "core"))
    image = P("y", ("x", "zl"), ("zh", "core"), None)
    return jax.shard_map(
        local,
        mesh=fine,
        in_specs=(P("y"), image, image, image, image) + (P(),) * 7,
        out_specs=(P("y"), P("y", ("x", "zl", "zh", "core")), P(), P()),
        check_vma=False,
    )
```

```python
import functools
import math

import jax
import jax.numpy as jnp
from jax import lax
from jax.experimental import pallas as pl
from jax.experimental.pallas import tpu as pltpu
from jax.sharding import Mesh
from jax.sharding import PartitionSpec as P

C = 320
GROUPS = 32
TAPS = 9
TH, TW = 8, 16
PIX = TH * TW
WIDE = 2 * C
BLK = 45
PIXELS = 64 * 128
BETA = 40.0
F32 = jnp.float32
BF16 = jnp.bfloat16
I16 = jnp.int16
HIGHEST = lax.Precision.HIGHEST


def call(kernel, outs, scratch=(), flops=0, nbytes=0, far=(), grant=28):
    def run(*args):
        specs = [
            pl.BlockSpec(memory_space=pltpu.HBM if i in far else pltpu.VMEM) for i in range(len(args))
        ]
        return pl.pallas_call(
            kernel,
            out_shape=[jax.ShapeDtypeStruct(s, d) for s, d in outs],
            in_specs=specs,
            out_specs=[pl.BlockSpec(memory_space=pltpu.VMEM) for _ in outs],
            scratch_shapes=list(scratch),
            compiler_params=pltpu.CompilerParams(vmem_limit_bytes=grant * 2**20),
            cost_estimate=pl.CostEstimate(flops=flops, bytes_accessed=nbytes, transcendentals=0),
        )(*args)

    return run


def pow2(n):
    size = jnp.abs(n)
    out = jnp.ones(n.shape, F32)
    for bit in range(7):
        step = jnp.where(n < 0, 0.5 ** (2**bit) if bit < 7 else 0.0, 2.0 ** (2**bit))
        out = out * jnp.where((size & (1 << bit)) != 0, step, 1.0)
    return out


def exponent(peak):
    level = jnp.log(jnp.maximum(peak, 1e-30)) * (1.0 / math.log(2.0))
    return jnp.clip(jnp.ceil(level + 0.01), -100.0, 100.0).astype(jnp.int32)


def rounded(values, exps):
    return jnp.round(values * pow2(15 - exps))


def split_small(small):
    exps = exponent(jnp.abs(small))
    scaled = small * pow2(15 - exps)
    high = jnp.round(scaled)
    low = jnp.round((scaled - high) * 32768.0)
    return high, low, exps.astype(F32)


def side_by_side(one, two):
    return jnp.concatenate([one[:, 0:256], two[:, 0:256], one[:, 256:C], two[:, 256:C]], axis=1)


def apart(both):
    one = jnp.concatenate([both[:, 0:256], both[:, 512:576]], axis=1)
    two = jnp.concatenate([both[:, 256:512], both[:, 576:640]], axis=1)
    return one, two


def write_extras(extra, small):
    high, low, exps = split_small(small)
    lane = lax.broadcasted_iota(jnp.int32, (1, WIDE), 1)
    extra[...] = jnp.zeros_like(extra)
    extra[0, 0:1] = high[0:1]
    extra[0, 1:2] = low[0:1]
    extra[1, 0:1] = exps[0:1]
    margin = jnp.where(lane == 1, low[1:2], exps[1:2])
    extra[1, 1:2] = jnp.where(lane == 0, high[1:2], margin)


def read_extras(tails):
    high, low, exps = tails[0][6:7], tails[0][7:8], tails[1][6:7]
    sums = (high.astype(F32) + low.astype(F32) * (1.0 / 32768.0)) * pow2(exps - 15)
    row = tails[1][7:8]
    value = row.astype(F32)
    margin = (value[:, 0:1] + value[:, 1:2] * (1.0 / 32768.0)) * pow2(row[:, 2:3] - 15)
    margin = jnp.broadcast_to(margin, (1, WIDE))
    return jnp.concatenate([sums, margin, jnp.zeros((6, WIDE), F32)], axis=0)


def packed_pair(pair, extra):
    exps = exponent(jnp.max(jnp.abs(pair), axis=0, keepdims=True))
    q = rounded(pair, exps)
    row = lax.broadcasted_iota(jnp.int32, (8, WIDE), 0)
    tail = jnp.where(row == 5, exps.astype(F32), q[40:48])
    tail = jnp.where(row == 6, extra[0:1], tail)
    tail = jnp.where(row == 7, extra[1:2], tail)
    q = jnp.concatenate([q[0:40], tail], axis=0)
    return q.astype(jnp.int32).astype(I16)


def unpacked_pair(q):
    v = q.astype(F32) * pow2(q[45:46] - 15)
    row = lax.broadcasted_iota(jnp.int32, (8, WIDE), 0)
    return jnp.concatenate([v[0:40], jnp.where(row < BLK - 40, v[40:48], 0.0)], axis=0)


def tiles_of(pair):
    return [4 * pair, 4 * pair + 1, 4 * pair + 2, 4 * pair + 3, 8 + pair]


def edge_rows(fw, fl, first, last, sems):
    copies = []
    for k, ref in enumerate((fw, fl)):
        copies.append(pltpu.make_async_copy(ref.at[0], first.at[k], sems.at[2 * k]))
        copies.append(pltpu.make_async_copy(ref.at[TH - 1], last.at[k], sems.at[2 * k + 1]))
    for copy in copies:
        copy.start()
    for copy in copies:
        copy.wait()


def statistics(fw, fl, nw, nl, stats, edge, here, sems):
    copies = [
        pltpu.make_async_copy(fw, here.at[0, pl.ds(0, TH)], sems.at[0]),
        pltpu.make_async_copy(fl, here.at[1, pl.ds(0, TH)], sems.at[1]),
        pltpu.make_async_copy(nw, here.at[0, pl.ds(TH, TH)], sems.at[2]),
        pltpu.make_async_copy(nl, here.at[1, pl.ds(TH, TH)], sems.at[3]),
    ]
    for copy in copies:
        copy.start()
    copies[0].wait()
    copies[1].wait()
    total = jnp.zeros((8, 128), F32)
    rows = lax.broadcasted_iota(jnp.int32, (C, 128), 0)
    lanes = lax.broadcasted_iota(jnp.int32, (C, 128), 1)
    size = C // GROUPS
    for k in range(2):
        field = here[k, 0:TH].astype(F32)
        x = field.reshape(PIX, C)
        sums = jnp.sum(x, axis=0, keepdims=True)
        squares = jnp.sum(x * x, axis=0, keepdims=True)
        for j, part in enumerate((sums, squares)):
            group = lanes - GROUPS * (2 * k + j)
            member = (group >= 0) & (group < GROUPS)
            member = member & (rows >= group * size) & (rows < group * size + size)
            total = total + jnp.dot(
                jnp.broadcast_to(part, (8, C)),
                member.astype(F32),
                precision=HIGHEST,
                preferred_element_type=F32,
            )
        column = [
            jnp.concatenate([field[r, col : col + 1] for r in range(TH)], axis=0)
            for col in (0, TW - 1)
        ]
        column = jnp.where(lax.axis_index("core") == 0, column[0], column[1])
        edge[k] = jnp.concatenate([column, jnp.zeros((8, C), F32)], axis=0).astype(BF16)
    stats[...] = jnp.broadcast_to(total[0:1], stats.shape)
    copies[2].wait()
    copies[3].wait()


def time_bias(step, time_weight, bias, number, table, sems):
    copies = [
        pltpu.make_async_copy(step, number, sems.at[0]),
        pltpu.make_async_copy(time_weight, table, sems.at[1]),
    ]
    for copy in copies:
        copy.start()
    half = C // 2
    lane = lax.broadcasted_iota(jnp.int32, (8, C), 1)
    place = jnp.where(lane < half, lane, lane - half).astype(F32)
    frequency = jnp.exp(-math.log(10000.0) * place / half)
    copies[0].wait()
    angles = number[0].astype(F32) * frequency
    sinusoid = jnp.where(lane < half, jnp.cos(angles), jnp.sin(angles))
    gate = sinusoid * jax.nn.sigmoid(sinusoid)
    copies[1].wait()
    bias[...] = jnp.dot(gate, table[...], precision=HIGHEST, preferred_element_type=F32)


def outer_column(top, bottom, edge, side):
    core = lax.axis_index("core")
    for s in range(2):
        above, below = top[s].astype(F32), bottom[s].astype(F32)
        above = jnp.where(core == 0, above[0:1], above[TW - 1 : TW])
        below = jnp.where(core == 0, below[0:1], below[TW - 1 : TW])
        column = [above, edge[s].astype(F32)[0:TH], below, jnp.zeros((6, C), F32)]
        side[s] = jnp.concatenate(column, axis=0).astype(BF16)


def sums_and_tile(stats, top, bottom, side, here, totals, tile):
    total = jnp.sum(stats[...], axis=0, keepdims=True)
    totals[...] = jnp.broadcast_to(total, (8, 128))
    high = total.astype(BF16).astype(F32)
    middle = (total - high).astype(BF16).astype(F32)
    low = total - high - middle
    parts = jnp.concatenate([high, middle, low, jnp.zeros((3, 128), F32)], axis=0)
    parts = jnp.concatenate([parts, jnp.zeros((6, C - 128), F32)], axis=1)
    column = side[0].astype(F32)[0 : TH + 2]
    tile[0, 2 * TH + 2] = jnp.concatenate([column, parts], axis=0).astype(BF16)
    tile[1, 2 * TH + 2] = side[1]
    for s in range(2):
        tile[s, 0] = top[s]
        tile[s, 1 : TH + 1] = here[s, 0:TH]
        tile[s, TH + 1] = bottom[s]
        tile[s, TH + 2 : 2 * TH + 2] = here[s, TH:]


def forward(
    totals, bias, mine, theirs, gain_far, shift_far, ref_gain_far, ref_shift_far,
    weight_far, ref_far, cols, cot_out, small, field, act, back, slope, shifted, weight, ref_weight, gain, shift,
    ref_gain, ref_shift, sems,
):
    pairs = [
        (ref_gain_far, ref_gain), (ref_shift_far, ref_shift), (gain_far, gain), (shift_far, shift),
        (ref_far, ref_weight), (weight_far, weight),
    ]
    copies = [pltpu.make_async_copy(a, b, sems.at[i]) for i, (a, b) in enumerate(pairs)]
    for copy in copies:
        copy.start()
    core = lax.axis_index("core")
    row_at = 2 * lax.axis_index("x") + lax.axis_index("zl")
    chip_at = 2 * lax.axis_index("zh")
    col_at = (chip_at + core, chip_at + 1 - core)

    parts = theirs[0, 2 * TH + 2].astype(F32)[TH + 2 : TH + 5, 0:128]
    total = totals[...] + ((parts[0:1] + parts[1:2]) + parts[2:3])
    groups = lax.broadcasted_iota(jnp.int32, (128, C), 0)
    chans = lax.broadcasted_iota(jnp.int32, (128, C), 1)
    size = C // GROUPS
    entries = float(PIXELS * size)

    def by_channel(k):
        group = groups - GROUPS * k
        member = (group >= 0) & (group < GROUPS)
        member = member & (chans >= group * size) & (chans < group * size + size)
        spread = jnp.dot(total, member.astype(F32), precision=HIGHEST, preferred_element_type=F32)
        return spread[0:1] / entries

    means, scales = [], []
    for s in range(2):
        mean, square = by_channel(2 * s), by_channel(2 * s + 1)
        means.append(mean)
        scales.append(lax.rsqrt(square - mean * mean + 1e-05))

    tiles = (mine, theirs)
    for w in range(2):
        for s in range(2):
            here, beside = tiles[w], tiles[1 - w]
            f = 2 * w + s
            field[f, :, TW + 2 :, :] = jnp.zeros((TH + 2, 22 - TW, C), F32)
            field[f, :, 1 : TW + 1, :] = (here[s, 0 : TH + 2].astype(F32) - means[s]) * scales[s]
            outer = (here[s, 2 * TH + 2].astype(F32) - means[s]) * scales[s]
            is_left = core == w
            for r in range(TH + 2):
                near = (beside[s, r].astype(F32) - means[s]) * scales[s]
                out = outer[r : r + 1]
                field[f, r, 0:1, :] = jnp.where(is_left, out, near[TW - 1 : TW])
                field[f, r, TW + 1 : TW + 2, :] = jnp.where(is_left, near[0:1], out)

    column = lax.broadcasted_iota(jnp.int32, (24, C), 0)
    inside = []
    for w in range(2):
        ok = (column < TW + 2) & ((column > 0) | (col_at[w] > 0))
        inside.append(ok & ((column < TW + 1) | (col_at[w] < 7)))

    def valid(w, r):
        if r == 0:
            return inside[w] & (row_at > 0)
        if r == TH + 1:
            return inside[w] & (row_at < 7)
        return inside[w]

    def columns_of(fields, g, b, slope=None):
        for f in fields:
            for r in range(TH + 2):
                pre = field[f, r] * g + b
                gate = jax.nn.sigmoid(pre)
                value = pre * gate
                act[r] = jnp.where(valid(f // 2, r), value, 0.0)
                if slope is not None and f < 2:
                    slope[f, r] = jnp.where(valid(0, r), gate + value * (1.0 - gate), 0.0)
                for c in range(3):
                    piece = act[r, c : c + TW, :].astype(BF16)
                    for a in range(3):
                        if 0 <= r - a < TH:
                            at, t = f * PIX + TW * (r - a), 3 * a + c
                            cols[at : at + TW, C * t : C * (t + 1)] = piece

    def base(f):
        tile, s = tiles[f // 2], f % 2
        noise = tile[s, TH + 2 : 2 * TH + 2].astype(F32)
        return (tile[s, 1 : TH + 1].astype(F32) - noise).reshape(PIX, C)

    def residual(fields, kernel):
        conv = jnp.dot(
            cols[0 : PIX * len(fields)],
            kernel[...].reshape(TAPS * C, C),
            preferred_element_type=F32,
        )
        return [base(f) + conv[PIX * f : PIX * (f + 1)] for f in fields]

    def signed_squares(resid):
        return jnp.sum(resid[0] * resid[0] - resid[1] * resid[1], axis=0, keepdims=True)

    time_row = bias[0:1]
    for copy in copies[0:4]:
        copy.wait()
    columns_of((0, 1), ref_gain[...].reshape(1, C), ref_shift[...].reshape(1, C) + time_row)
    copies[4].wait()
    resid = residual((0, 1), ref_weight)
    margin = -signed_squares(resid)
    g, b = gain[...].reshape(1, C), shift[...].reshape(1, C) + time_row
    columns_of((0, 1, 2, 3), g, b, slope)
    copies[5].wait()
    resid = residual((0, 1, 2, 3), weight)
    margin = margin + signed_squares(resid)
    for f in range(4):
        cot_out[PIX * f : PIX * (f + 1)] = (resid[f] if f % 2 == 0 else -resid[f]).astype(BF16)

    cot = cot_out[0 : 2 * PIX]
    back[...] = jnp.zeros_like(back)
    terms = lax.dot_general(
        cot, weight[...].reshape(TAPS * C, C), (((1,), (1,)), ((), ())), preferred_element_type=F32
    )
    for c in range(3):
        for a in range(3):
            term = terms[:, C * (3 * a + c) : C * (3 * a + c + 1)]
            for s in range(2):
                part = term[s * PIX : (s + 1) * PIX].reshape(TH, TW, C)
                if a == 0:
                    shifted[s, 0:TH] = part
                    shifted[s, TH:] = jnp.zeros((2, TW, C), F32)
                else:
                    shifted[s, a : a + TH] += part
        back[:, :, c : c + TW, :] += shifted[...]
    gains = jnp.zeros((24, C), F32)
    shifts = jnp.zeros((24, C), F32)
    for s in range(2):
        for r in range(TH + 2):
            dpre = back[s, r] * slope[s, r]
            gains = gains + dpre * field[s, r]
            shifts = shifts + dpre
    gains = jnp.sum(gains, axis=0, keepdims=True)
    shifts = jnp.sum(shifts, axis=0, keepdims=True)
    margin = jnp.broadcast_to(jnp.sum(margin, axis=1, keepdims=True), (1, WIDE))
    small[...] = jnp.concatenate(
        [side_by_side(gains, shifts), margin, jnp.zeros((6, WIDE), F32)], axis=0
    )


def kernel_gradient(cols, cot, out, grad):
    grad[0 : TAPS * C, :] = lax.dot_general(
        cols[...], cot[...], (((0,), (0,)), ((), ())), preferred_element_type=F32
    )
    row = lax.broadcasted_iota(jnp.int32, (48, C), 0)
    for core in range(2):

        @pl.when(lax.axis_index("core") == core)
        def _():
            for q in range(32):
                start = BLK * (2 * q + core)
                out[q] = jnp.where(row < BLK, grad[start : start + 48, :], 0.0)


def pack_blocks(blocks, small, other, out, extra):
    write_extras(extra, small[...] + other[...])

    for dest in range(8):
        for pair in range(2):
            q = 4 * dest + 2 * pair
            packed = packed_pair(side_by_side(blocks[q], blocks[q + 1]), extra[pair])
            for k, tile in enumerate(tiles_of(pair)):
                out[dest, tile] = packed[:, 128 * k : 128 * k + 128]


def chip_sum(blocks, out):
    def pair_of(source, pair, rows):
        parts = [blocks[source, tile].astype(jnp.int32)[rows] for tile in tiles_of(pair)]
        return jnp.concatenate(parts, axis=1)

    tail_rows = slice(40, 48)
    small = jnp.zeros((8, WIDE), F32)
    for source in range(8):
        small = small + read_extras([pair_of(source, k, tail_rows) for k in range(2)])
    high, low, exps = split_small(small[:, 0:128])
    lane = lax.broadcasted_iota(jnp.int32, (1, 128), 1)
    tail = jnp.zeros((1, 128), F32)
    vectors = []
    for k, vector in enumerate(apart(small[0:1])):
        e = exponent(jnp.max(jnp.abs(vector), axis=1, keepdims=True))
        q = rounded(vector, e)
        q = jnp.concatenate([q, jnp.zeros((1, 64), F32)], axis=1)
        vectors += [q[:, 0:128], q[:, 128:256], q[:, 256:384]]
        tail = jnp.where(lane == k, e.astype(F32), tail)
    for k, part in enumerate((high, low, exps)):
        tail = jnp.where(lane == 2 + k, part[1:2], tail)

    for pair in range(2):
        both = jnp.zeros((48, WIDE), F32)
        for source in range(8):
            both = both + unpacked_pair(pair_of(source, pair, slice(0, 48)))
        e = exponent(jnp.max(jnp.abs(both), axis=0, keepdims=True))
        values = apart(rounded(both, e))
        levels = apart(e.astype(F32))
        for k in range(2):
            for y in range(8):
                part = values[k][:, 40 * y : 40 * y + 40]
                tile = jnp.concatenate(
                    [part[0:16], part[16:32], part[32:48], jnp.zeros((16, 8), F32)], axis=1
                )
                ey = levels[k][:, 40 * y : 40 * y + 40]
                ey = jnp.concatenate([ey, ey, ey, jnp.zeros((1, 8), F32)], axis=1)
                full = jnp.concatenate([tile] + vectors + [ey, tail], axis=0)
                out[y, 2 * pair + k] = full.astype(jnp.int32).astype(I16)


def final_sum(blocks, loss, grad, gain, shift):
    y_at = lax.axis_index("y")
    weights = jnp.zeros((16, 128), F32)
    vectors = jnp.zeros((8, 128), F32)
    mine = jnp.zeros((1, 1), F32)
    row = lax.broadcasted_iota(jnp.int32, (8, 128), 0)
    for pair in range(8):
        part = jnp.zeros((16, 128), F32)
        vector = jnp.zeros((8, 128), F32)
        margin = jnp.zeros((1, 1), F32)
        for z in range(4):
            q = blocks[pair, z].astype(jnp.int32)
            v = q.astype(F32)
            tail = q[16:24]
            part = part + v[0:16] * pow2(tail[6:7] - 15)
            factor = pow2(tail[7:8] - 15)
            vector = vector + v[16:24] * jnp.where(row < 3, factor[:, 0:1], factor[:, 1:2])
            margin = margin + (v[23:24, 2:3] + v[23:24, 3:4] * (1.0 / 32768.0)) * factor[:, 4:5]
        margin = BETA * (margin / float(PIXELS * C))
        scale = BETA * jax.nn.sigmoid(margin) * (2.0 / (8 * C))
        weights = weights + scale * part
        vectors = vectors + scale * vector
        mine = jnp.where(y_at == pair, margin, mine)
    near = jnp.exp(-jnp.abs(mine))
    one = 1.0 + near
    log1p = jnp.where(one == 1.0, near, jnp.log(one) * near / jnp.where(one == 1.0, 1.0, one - 1.0))
    loss[...] = jnp.maximum(mine, 0.0) + log1p
    tall = jnp.concatenate([weights, jnp.roll(weights, -40, 1), jnp.roll(weights, -80, 1)], axis=0)
    tall = jnp.concatenate([tall, jnp.zeros((80, 128), F32)], axis=0)
    grad[...] = tall.T[0:40, 0:BLK]
    for out, k in ((gain, 0), (shift, 3)):
        pieces = [vectors[k : k + 1], vectors[k + 1 : k + 2], vectors[k + 2 : k + 3, 0:64]]
        out[...] = jnp.concatenate(pieces, axis=1).reshape(C)


def local(
    timesteps, features_win, features_lose, noise_win, noise_lose, conv_weight, ref_weight,
    norm_gain, norm_shift, ref_gain, ref_shift, time_weight,
):
    fw, fl = features_win[0], features_lose[0]
    strip = (2, TW, C)
    rows, columns = ("x", "zl"), ("zh", "core")
    up = [((i + 1) % 8, i) for i in range(8)]
    down = [(i, (i + 1) % 8) for i in range(8)]
    outward = [(i, (i + 1) % 8 if i % 2 else (i + 7) % 8) for i in range(8)]
    swap = [(0, 1), (1, 0)]

    first, last = call(
        edge_rows,
        [(strip, BF16), (strip, BF16)],
        [pltpu.SemaphoreType.DMA((4,))],
        far=(0, 1),
        grant=57,
    )(fw, fl)
    top = lax.ppermute(last, rows, down)
    bottom = lax.ppermute(first, rows, up)
    stats, edge, here = call(
        statistics,
        [((32, 128), F32), (strip, BF16), ((2, 2 * TH, TW, C), BF16)],
        [pltpu.SemaphoreType.DMA((4,))],
        flops=10**7,
        nbytes=10**6,
        far=range(4),
        grant=57,
    )(fw, fl, noise_win[0], noise_lose[0])
    stats = lax.all_to_all(stats, ("x", "zl", "zh"), 0, 0, tiled=True)
    (bias,) = call(
        time_bias,
        [((8, C), F32)],
        [pltpu.SMEM((1,), jnp.int32), pltpu.VMEM((C, C), F32), pltpu.SemaphoreType.DMA((2,))],
        flops=10**10,
        nbytes=10**6,
        far=(0, 1),
    )(timesteps, time_weight)
    (side,) = call(outer_column, [(strip, BF16)], flops=10**10, nbytes=10**6)(
        top, bottom, edge
    )
    side = lax.ppermute(side, columns, outward)
    totals, mine = call(
        sums_and_tile,
        [((8, 128), F32), ((2, 2 * TH + 3, TW, C), BF16)],
        flops=2 * 10**10,
        nbytes=10**6,
    )(stats, top, bottom, side, here)
    theirs = lax.ppermute(mine, "core", swap)

    cols, cot, small = call(
        forward,
        [((4 * PIX, TAPS * C), BF16), ((4 * PIX, C), BF16), ((8, WIDE), F32)],
        [
            pltpu.VMEM((4, TH + 2, 24, C), F32),
            pltpu.VMEM((TH + 2, 24, C), F32),
            pltpu.VMEM((2, TH + 2, 24, C), F32),
            pltpu.VMEM((2, TH + 2, 24, C), F32),
            pltpu.VMEM((2, TH + 2, TW, C), F32),
            pltpu.VMEM((TAPS, C, C), BF16),
            pltpu.VMEM((TAPS, C, C), BF16),
        ]
        + [pltpu.VMEM((C,), F32)] * 4
        + [pltpu.SemaphoreType.DMA((6,))],
        flops=2 * 10**9,
        nbytes=10**7,
        far=range(4, 10),
    )(
        totals, bias, mine, theirs, norm_gain, norm_shift, ref_gain, ref_shift,
        conv_weight, ref_weight,
    )
    other = lax.ppermute(small, "core", swap)
    block = (32, 48, C)
    (blocks,) = call(
        kernel_gradient,
        [(block, F32)],
        [pltpu.VMEM((TAPS * C + 8, C), F32)],
        flops=10**9,
        nbytes=10**7,
    )(cols, cot)
    (blocks,) = call(
        pack_blocks, [((8, 10, 48, 128), I16)], [pltpu.VMEM((2, 8, WIDE), F32)]
    )(blocks, small, other)
    blocks = lax.all_to_all(blocks, ("x", "zl"), 0, 0, tiled=True)
    (sums,) = call(chip_sum, [((8, 4, 24, 128), I16)])(blocks)
    sums = lax.all_to_all(sums.reshape(32, 24, 128), ("y", "zh"), 0, 0, tiled=True)
    loss, grad, gain, shift = call(
        final_sum, [((1, 1), F32), ((40, BLK), F32), ((C,), F32), ((C,), F32)]
    )(sums.reshape(8, 4, 24, 128))
    return loss.reshape(1), grad, gain, shift


def solution(mesh):
    fine = Mesh(mesh.devices.reshape(8, 4, 2, 4, 2), ("y", "x", "zl", "zh", "core"))
    image = P("y", ("x", "zl"), ("zh", "core"), None)
    return jax.shard_map(
        local,
        mesh=fine,
        in_specs=(P("y"), image, image, image, image) + (P(),) * 7,
        out_specs=(P("y"), P("y", ("x", "zl", "zh", "core")), P(), P()),
        check_vma=False,
    )
```
